256 devices in a mesh: doc: 16 (over x_hi, z), hidden: 16 (over y, x_lo, core).
Axes of the slice: x: 4 (x_hi: 2, x_lo: 2; x = x_hi * 2 + x_lo), y: 4, z: 8, core: 2. Of those that a mesh axis runs over, the one named last changes fastest.
Arguments:
- train_acts: bfloat16 [12288, 28672], P('doc', 'hidden'), may hold values from -0.4375 to 0.4375
- train_grads: bfloat16 [12288, 8192], P('doc', 'hidden'), may hold values from -0.625 to 0.625
- query_acts: bfloat16 [8192, 28672], P('doc', 'hidden'), may hold values from -0.4375 to 0.4375
- query_grads: bfloat16 [8192, 8192], P('doc', 'hidden'), may hold values from -0.625 to 0.625
- train_seg: int32 [16, 768], P('doc'), may hold values from 0 to 7, never falling along the last dimension, each value on 1 to 192 neighbouring positions
- query_seg: int32 [16, 512], replicated, may hold values from 0 to 7, never falling along the last dimension, each value on 1 to 128 neighbouring positions
Outputs:
- influence: float32 [128, 32], P('doc')
The draws below stay inside these ranges and needn't reach their ends.
All inputs are finite; a program needn't handle non-finite values.
Results may differ from the reference program's by a relative error of at most 0.0003.
Values may be sent and summed in bfloat16 or wider, within the bound.
A program may use at most 64 MiB of HBM per device.

```python
import math
import jax
import jax.numpy as jnp
import numpy as np
from jax import lax

DA = 28672
DG = 8192
TT = 768
TQ = 512
ST = 8
SQ = 8
CYCLE = 4
TRAIN_TOK = 12288
QUERY_TOK = 8192
N_DOC = 16


def level_of(stream_key, dims, split, least, high):
    level, own = 1.0, jax.random.fold_in(stream_key, 6)
    for position, blocks in split:
        heights = jnp.exp(jax.random.uniform(jax.random.fold_in(own, position), (blocks,), jnp.float32, least / len(split), high / len(split)))
        level = level * jnp.repeat(heights, dims[position] // blocks).reshape([-1 if axis == position else 1 for axis in range(len(dims))])
    return level


def length_profile(number_of, total, reach, skew):
    weights = [(1 << 20) // math.isqrt(grade ** skew) + 1 for grade in range(2, number_of + 1)]
    rest, holding = total - reach - (number_of - 1), [1] * (number_of - 1)
    while rest > 0:
        candidates = [i for i in range(number_of - 1) if holding[i] < reach]
        mass, left = sum([weights[i] for i in candidates]), rest
        for i in candidates:
            more = min(reach - holding[i], max(1, left * weights[i] // mass), rest)
            holding[i] = holding[i] + more
            rest = rest - more
    return np.array([reach] + holding)


def uneven(rng, number_of, total, most, slope):
    if number_of == 2:
        one = jax.random.randint(rng, (), max(1, total - most), min(most, total - 1) + 1)
        return jnp.stack([one, total - one])
    sizes = jnp.asarray(length_profile(number_of, total, most, slope), jnp.int32)
    couples = (number_of - 1) // 2
    donor, sink = sizes[1:1 + 2 * couples:2], sizes[2:2 + 2 * couples:2]
    slack = jnp.minimum(donor - 1, most - sink)
    moved = jax.random.randint(jax.random.fold_in(rng, 1), (couples,), 0, 1 << 20) % (slack + 1)
    sizes = sizes.at[1:1 + 2 * couples:2].set(donor - moved).at[2:2 + 2 * couples:2].set(sink + moved)
    return sizes[jax.random.permutation(jax.random.fold_in(rng, 2), number_of)]


def bell_draw(stream_key, extent, spread, most, shards=(), kind=jnp.bfloat16):
    entries = jax.random.normal(stream_key, extent, jnp.float32) * spread
    if len(shards) > 0:
        entries = level_of(stream_key, extent, shards, -0.22, 0.18) * entries
    return jnp.clip(entries, min=-most, max=most).astype(kind)


def setup_inputs(seed: int = 0) -> dict:
    splits = jax.random.split(jax.random.key(seed), 7)
    return {
        "train_acts": bell_draw(splits[0], (TRAIN_TOK, DA), (DA ** -0.25), 0.4375, ((0, 16), (1, 16))),
        "train_grads": bell_draw(splits[1], (TRAIN_TOK, DG), (DG ** -0.25), 0.625, ((0, 16), (1, 16))),
        "query_acts": bell_draw(splits[2], (QUERY_TOK, DA), (DA ** -0.25), 0.4375, ((0, 16), (1, 16))),
        "query_grads": bell_draw(splits[3], (QUERY_TOK, DG), (DG ** -0.25), 0.625, ((0, 16), (1, 16))),
        "train_seg": jax.vmap(lambda own: jnp.searchsorted(jnp.cumsum(uneven(own, ST, TT, 2 * TT // ST, 1)), jnp.arange(TT), side="right"))(jax.random.split(splits[4], N_DOC)).reshape((N_DOC, TT)).astype(jnp.int32),
        "query_seg": jax.vmap(lambda own: jnp.searchsorted(jnp.cumsum(uneven(own, SQ, TQ, 2 * TQ // SQ, 1)), jnp.arange(TQ), side="right"))(jax.random.split(splits[5], N_DOC)).reshape((N_DOC, TQ)).astype(jnp.int32),
    }


def reference(train_acts, train_grads, query_acts, query_grads, train_seg, query_seg):
    factor = math.sqrt(ST * SQ / (TT * TQ))
    train_ids = jnp.arange(ST).astype(jnp.int32)
    query_ids = jnp.arange(SQ).astype(jnp.int32)
    blocks = []
    for block in range(N_DOC):
        rows_a = train_acts[block * TT:(block + 1) * TT]
        rows_g = train_grads[block * TT:(block + 1) * TT]
        onehot_train = (train_ids[:, None] == train_seg[block][None, :]).astype(jnp.float32)
        columns = []
        for step in range(CYCLE):
            other = (block - step) % N_DOC
            cols_a = query_acts[other * TQ:(other + 1) * TQ]
            cols_g = query_grads[other * TQ:(other + 1) * TQ]
            act_gram = jnp.dot(rows_a, cols_a.T, preferred_element_type=jnp.float32)
            grad_gram = jnp.dot(rows_g, cols_g.T, preferred_element_type=jnp.float32)
            pair = act_gram * grad_gram
            onehot_query = (query_seg[other][:, None] == query_ids[None, :]).astype(jnp.float32)
            left = jnp.dot(onehot_train, pair, precision=lax.Precision.HIGHEST)
            columns.append(jnp.dot(left, onehot_query, precision=lax.Precision.HIGHEST) * factor)
        blocks.append(jnp.concatenate(columns, axis=1))
    return jnp.concatenate(blocks, axis=0)
```

```python
import functools
import math

import jax
import jax.numpy as jnp
from jax import lax
from jax.experimental import pallas as pl
from jax.experimental.pallas import tpu as pltpu
from jax.sharding import PartitionSpec as P

ST = 8
SQ = 8
CYCLE = 4
NY = 4
NX = 2
NCORE = 2
CHUNKS = 4
TPARTS = 4
LANES = 128
MESH = pl.DeviceIdType.MESH
CONTRACT = (((1,), (1,)), ((), ()))


def kernel(
    n_doc,
    ta_hbm,
    tg_hbm,
    qa_hbm,
    qg_hbm,
    tseg_ref,
    qseg_ref,
    out_ref,
    tbuf,
    qbuf,
    gram,
    yrecv,
    xsend,
    xrecv,
    pairs,
    segn,
    fin,
    local_sem,
    own_send,
    own_recv,
    z1_send,
    z1_recv,
    z2_send,
    z2_recv,
    tz_send,
    tz_recv,
    tf_send,
    tf_recv,
    y_send,
    y_recv,
    x_send,
    x_recv,
    f_send,
    f_recv,
):
    rows_t, wide_a = ta_hbm.shape
    rows_q, wide_g = qg_hbm.shape
    half = rows_q // NCORE
    chunk = half // CHUNKS
    part = rows_t // TPARTS
    ry = chunk // NY
    lx = rows_t // NX
    factor = math.sqrt(ST * SQ / (rows_t * rows_q))

    doc = lax.axis_index("doc")
    place = lax.axis_index("hidden")
    core = lax.rem(place, NCORE)
    other = 1 - core
    my_x = lax.rem(place // NCORE, NX)
    my_y = place // (NCORE * NX)
    plane = place - core
    up = lax.rem(doc + 1, n_doc)
    down = lax.rem(doc + n_doc - 1, n_doc)
    sibling = (doc, plane + other)
    x_peer = (doc, my_y * (NX * NCORE) + (1 - my_x) * NCORE + core)

    def y_of(d):
        return lax.rem(my_y + d, NY)

    def y_peer(d):
        return (doc, y_of(d) * (NX * NCORE) + my_x * NCORE + core)

    greet = [sibling, (up, place), (up, plane + other), (down, place), (down, plane + other), x_peer]
    greet += [y_peer(d) for d in range(1, NY)]
    barrier = pltpu.get_barrier_semaphore()
    for who in greet:
        pl.semaphore_signal(barrier, inc=1, device_id=who, device_id_type=MESH)
    pl.semaphore_wait(barrier, len(greet))

    def remote(src, dst, send, recv, who):
        return pltpu.make_async_remote_copy(
            src_ref=src, dst_ref=dst, send_sem=send, recv_sem=recv, device_id=who, device_id_type=MESH
        )

    acts = pl.ds(0, wide_a)
    grads = pl.ds(wide_a, wide_g)

    def q_rows(whose, m):
        return pl.ds(pl.multiple_of(whose * half + m * chunk, chunk), chunk)

    def m_rows(m):
        return pl.ds(m * chunk, chunk)

    def hop1(m, to_core, j):
        src, cols = ((qa_hbm, acts), (qg_hbm, grads))[j]
        to_core_id = core if to_core == 0 else other
        return remote(
            src.at[q_rows(to_core_id, m), :],
            qbuf.at[1, core, m_rows(m), cols],
            z1_send.at[m, to_core, j],
            z1_recv.at[m, to_core, j],
            (up, plane + to_core_id),
        )

    def hop1_arrival(m, from_core, j):
        src, cols = ((qa_hbm, acts), (qg_hbm, grads))[j]
        from_core_id = core if from_core == 0 else other
        return remote(
            src.at[q_rows(core, m), :],
            qbuf.at[1, from_core_id, m_rows(m), cols],
            z1_send.at[m, from_core, j],
            z1_recv.at[m, from_core, j],
            (up, plane + from_core_id),
        )

    def hop2(m):
        return remote(
            qbuf.at[1, :, m_rows(m), :],
            qbuf.at[2, :, m_rows(m), :],
            z2_send.at[m],
            z2_recv.at[m],
            (up, place),
        )

    def t_rows(p):
        return pl.ds(p * part, part)

    def t_down(p, j):
        src, cols = ((ta_hbm, acts), (tg_hbm, grads))[j]
        return remote(
            src.at[t_rows(p), :],
            tbuf.at[1, core, t_rows(p), cols],
            tz_send.at[p, j],
            tz_recv.at[p, j],
            (down, place),
        )

    def t_forward(p, whose):
        return remote(
            tbuf.at[1, whose, t_rows(p), :],
            tbuf.at[1, whose, t_rows(p), :],
            tf_send.at[p],
            tf_recv.at[p],
            sibling,
        )

    def swap(j, whose_q, whose):
        src, dst = (
            (qa_hbm.at[pl.ds(pl.multiple_of(whose_q * half, half), half), :], qbuf.at[0, whose, :, acts]),
            (qg_hbm.at[pl.ds(pl.multiple_of(whose_q * half, half), half), :], qbuf.at[0, whose, :, grads]),
            (ta_hbm, tbuf.at[0, whose, :, acts]),
            (tg_hbm, tbuf.at[0, whose, :, grads]),
        )[j]
        return src, dst

    def swap_out(j):
        src, dst = swap(j, other, core)
        return remote(src, dst, own_send.at[j], own_recv.at[j], sibling)

    def swap_in(j):
        src, dst = swap(j, core, other)
        return remote(src, dst, own_send.at[j], own_recv.at[j], sibling)

    def local(j):
        src, dst = swap(j, core, core)
        return pltpu.make_async_copy(src, dst, local_sem.at[j])

    seg_copy = remote(tseg_ref, segn, f_send.at[0], f_recv.at[0], (down, place))

    for j in range(4):
        local(j).start()
    for to_core in range(2):
        for j in range(2):
            hop1(0, to_core, j).start()
    for j in range(4):
        swap_out(j).start()
    for j in range(2):
        t_down(0, j).start()
    for m in range(1, CHUNKS):
        for to_core in range(2):
            for j in range(2):
                hop1(m, to_core, j).start()
    for p in range(1, TPARTS):
        for j in range(2):
            t_down(p, j).start()
    seg_copy.start()

    def compute(r, m):
        t_slot = 1 if r == 3 else 0
        q_slot = min(r, 2)
        tile = 256

        def body(n, carry):
            at = pl.ds(pl.multiple_of(n * tile, tile), tile)
            for which, cols in ((0, acts), (1, grads)):
                total = None
                for h in range(NCORE):
                    term = lax.dot_general(
                        qbuf[q_slot, h, m_rows(m), cols],
                        tbuf[t_slot, h, at, cols],
                        CONTRACT,
                        preferred_element_type=jnp.float32,
                    )
                    total = term if total is None else total + term
                gram[r, m, :, which, :, at] = total.reshape(NY, ry, tile)
            return carry

        lax.fori_loop(0, rows_t // tile, body, 0)

    def y_copy(r, m, d):
        return remote(
            gram.at[r, m, y_of(d)],
            yrecv.at[r, m, d - 1],
            y_send.at[r, m, d - 1],
            y_recv.at[r, m, d - 1],
            y_peer(d),
        )

    def x_copy(r, m):
        return remote(
            xsend.at[r, m, 1 - my_x], xrecv.at[r, m], x_send.at[r, m], x_recv.at[r, m], x_peer
        )

    def y_finish(r, m):
        for d in range(1, NY):
            y_copy(r, m, d).wait_recv()
        total = gram[r, m, my_y] + yrecv[r, m, 0] + yrecv[r, m, 1] + yrecv[r, m, 2]
        for x in range(NX):
            xsend[r, m, x] = total[:, :, x * lx : (x + 1) * lx]
        x_copy(r, m).start()

    def x_finish(r, m):
        x_copy(r, m).wait_recv()
        act = xsend[r, m, my_x, 0] + xrecv[r, m, 0]
        grad = xsend[r, m, my_x, 1] + xrecv[r, m, 1]
        pairs[r, pl.ds(m * ry, ry), :] = act * grad

    def segment_sum(r):
        seg_t = (segn if r == 3 else tseg_ref)[:, pl.ds(pl.multiple_of(my_x * lx, lx), lx)]
        onehot_t = (lax.broadcasted_iota(jnp.int32, (ST, lx), 0) == seg_t).astype(jnp.float32)
        q_slot = min(r, 2)
        owner = lax.rem(doc + n_doc - q_slot, n_doc)
        seg_q = qseg_ref[pl.ds(owner, 1), :]
        row = lax.broadcasted_iota(jnp.int32, (CHUNKS * ry, rows_q), 0)
        token = lax.broadcasted_iota(jnp.int32, (CHUNKS * ry, rows_q), 1)
        mine = core * half + (row // ry) * chunk + my_y * ry + row % ry
        ids = jnp.sum(jnp.where(token == mine, seg_q, 0), axis=1, keepdims=True)
        lane = lax.broadcasted_iota(jnp.int32, (CHUNKS * ry, LANES), 1)
        onehot_q = (lane == ids + r * SQ).astype(jnp.float32)
        left = lax.dot_general(
            onehot_t,
            pairs[r],
            CONTRACT,
            precision=lax.Precision.HIGHEST,
            preferred_element_type=jnp.float32,
        )
        return jnp.dot(
            left, onehot_q, precision=lax.Precision.HIGHEST, preferred_element_type=jnp.float32
        )

    todo_y, todo_x = [], []

    def finish(lag_y, lag_x):
        while len(todo_x) > lag_x:
            x_finish(*todo_x.pop(0))
        while len(todo_y) > lag_y:
            unit = todo_y.pop(0)
            y_finish(*unit)
            todo_x.append(unit)

    def unit(r, m):
        compute(r, m)
        for d in range(1, NY):
            y_copy(r, m, d).start()
        todo_y.append((r, m))

    def forward(p):
        for j in range(2):
            t_down(p, j).wait_recv()
        t_forward(p, core).start()

    for j in range(4):
        local(j).wait()
        swap_in(j).wait_recv()
    for m in range(CHUNKS):
        unit(0, m)
        finish(1, 1)
    for m in range(CHUNKS):
        for from_core in range(2):
            for j in range(2):
                hop1_arrival(m, from_core, j).wait_recv()
        hop2(m).start()
        unit(1, m)
        if m == 1:
            forward(0)
        if m == 3:
            forward(1)
        finish(1, 1)
    for m in range(2):
        hop2(m).wait_recv()
        unit(2, m)
        forward(2 + m)
        finish(1, 1)
    for p in range(TPARTS):
        t_forward(p, other).wait_recv()
    for m in range(2):
        unit(3, m)
        finish(1, 1)
    for m in range(2, CHUNKS):
        hop2(m).wait_recv()
        unit(3, m)
        finish(1, 1)
        unit(2, m)
        finish(1, 1)
    seg_copy.wait_recv()
    base = segment_sum(0) + segment_sum(1)
    finish(0, 1)
    finish(0, 1)

    fin[0] = segment_sum(3)
    third = remote(fin.at[0], fin.at[1], f_send.at[1], f_recv.at[1], (up, place))
    third.start()
    finish(0, 0)
    base = base + segment_sum(2)
    third.wait_recv()
    fin[2 + my_y] = base + fin[1]
    y_all = [
        remote(fin.at[2 + my_y], fin.at[2 + my_y], f_send.at[1 + d], f_recv.at[1 + d], y_peer(d))
        for d in range(1, NY)
    ]
    y_in = [
        remote(
            fin.at[2 + y_of(NY - d)],
            fin.at[2 + y_of(NY - d)],
            f_send.at[1 + d],
            f_recv.at[1 + d],
            y_peer(d),
        )
        for d in range(1, NY)
    ]
    for copy in y_all:
        copy.start()
    for copy in y_in:
        copy.wait_recv()
    fin[6] = (fin[2] + fin[3]) + (fin[4] + fin[5])
    x_all = remote(fin.at[6], fin.at[7], f_send.at[5], f_recv.at[5], x_peer)
    x_all.start()
    x_all.wait_recv()
    fin[8] = fin[6] + fin[7]
    core_all = remote(fin.at[8], fin.at[9], f_send.at[6], f_recv.at[6], sibling)
    core_all.start()
    core_all.wait_recv()
    out_ref[...] = ((fin[8] + fin[9]) * factor)[:, : CYCLE * SQ]

    seg_copy.wait_send()
    third.wait_send()
    for copy in y_all:
        copy.wait_send()
    x_all.wait_send()
    core_all.wait_send()
    for j in range(4):
        swap_out(j).wait_send()
    for m in range(CHUNKS):
        for to_core in range(2):
            for j in range(2):
                hop1(m, to_core, j).wait_send()
        hop2(m).wait_send()
    for p in range(TPARTS):
        for j in range(2):
            t_down(p, j).wait_send()
        t_forward(p, core).wait_send()
    for r in range(CYCLE):
        for m in range(CHUNKS):
            for d in range(1, NY):
                y_copy(r, m, d).wait_send()
            x_copy(r, m).wait_send()


def on_device(n_doc, train_acts, train_grads, query_acts, query_grads, train_seg, query_seg):
    rows_t, wide_a = train_acts.shape
    rows_q, wide_g = query_grads.shape
    half = rows_q // NCORE
    chunk = half // CHUNKS
    ry = chunk // NY
    lx = rows_t // NX
    wide = wide_a + wide_g
    dma = pltpu.SemaphoreType.DMA
    anywhere = pl.BlockSpec(memory_space=pl.ANY)
    vmem = pl.BlockSpec(memory_space=pltpu.VMEM)
    return pl.pallas_call(
        functools.partial(kernel, n_doc),
        out_shape=jax.ShapeDtypeStruct((ST, CYCLE * SQ), jnp.float32),
        in_specs=[anywhere] * 4 + [vmem] * 2,
        out_specs=vmem,
        scratch_shapes=[
            pltpu.VMEM((2, NCORE, rows_t, wide), jnp.bfloat16),
            pltpu.VMEM((3, NCORE, half, wide), jnp.bfloat16),
            pltpu.VMEM((CYCLE, CHUNKS, NY, 2, ry, rows_t), jnp.float32),
            pltpu.VMEM((CYCLE, CHUNKS, NY - 1, 2, ry, rows_t), jnp.float32),
            pltpu.VMEM((CYCLE, CHUNKS, NX, 2, ry, lx), jnp.float32),
            pltpu.VMEM((CYCLE, CHUNKS, 2, ry, lx), jnp.float32),
            pltpu.VMEM((CYCLE, CHUNKS * ry, lx), jnp.float32),
            pltpu.VMEM((1, rows_t), jnp.int32),
            pltpu.VMEM((10, ST, LANES), jnp.float32),
            dma((4,)),
            dma((4,)),
            dma((4,)),
            dma((CHUNKS, 2, 2)),
            dma((CHUNKS, 2, 2)),
            dma((CHUNKS,)),
            dma((CHUNKS,)),
            dma((TPARTS, 2)),
            dma((TPARTS, 2)),
            dma((TPARTS,)),
            dma((TPARTS,)),
            dma((CYCLE, CHUNKS, NY - 1)),
            dma((CYCLE, CHUNKS, NY - 1)),
            dma((CYCLE, CHUNKS)),
            dma((CYCLE, CHUNKS)),
            dma((7,)),
            dma((7,)),
        ],
        compiler_params=pltpu.CompilerParams(
            collective_id=0, has_side_effects=True, vmem_limit_bytes=56 * 1024 * 1024
        ),
        name="influence",
    )(train_acts, train_grads, query_acts, query_grads, train_seg, query_seg)


def solution(mesh):
    in_specs = (
        P("doc", "hidden"),
        P("doc", "hidden"),
        P("doc", "hidden"),
        P("doc", "hidden"),
        P("doc", None),
        P(),
    )
    return jax.shard_map(
        functools.partial(on_device, mesh.shape["doc"]),
        mesh=mesh,
        in_specs=in_specs,
        out_specs=P("doc", None),
        check_vma=False,
    )
```

```python
import functools
import math

import jax
import jax.numpy as jnp
from jax import lax
from jax.experimental import pallas as pl
from jax.experimental.pallas import tpu as pltpu
from jax.sharding import PartitionSpec as P

ST = 8
SQ = 8
CYCLE = 4
NY = 4
NX = 2
NCORE = 2
CHUNKS = 4
TPARTS = 3
LANES = 128
ACT = 0
GRAD = 1
MESH = pl.DeviceIdType.MESH
CONTRACT = (((1,), (1,)), ((), ()))
F32 = jnp.float32

UNITS = {
    "g0": (GRAD, 0, 0, 4, 0, 3),
    "a0": (ACT, 0, 0, 4, 0, 3),
    "g1": (GRAD, 1, 0, 4, 0, 3),
    "g2": (GRAD, 2, 0, 4, 0, 3),
    "g3": (GRAD, 3, 0, 4, 0, 3),
    "a1_01": (ACT, 1, 0, 2, 0, 3),
    "a1_23": (ACT, 1, 2, 2, 0, 3),
    "a2_0": (ACT, 2, 0, 1, 0, 3),
    "a2_1": (ACT, 2, 1, 1, 0, 3),
    "a2_2": (ACT, 2, 2, 1, 0, 3),
    "a2_3": (ACT, 2, 3, 1, 0, 3),
    "a3_01": (ACT, 3, 0, 2, 0, 2),
    "a3_2": (ACT, 3, 2, 1, 0, 2),
    "a3_3": (ACT, 3, 3, 1, 0, 2),
    "a3_all": (ACT, 3, 0, 4, 2, 1),
}
ORDER = list(UNITS)


def kernel(
    n_doc,
    ta_hbm,
    tg_hbm,
    qa_hbm,
    qg_hbm,
    tseg_ref,
    qseg_ref,
    out_ref,
    ta,
    tg,
    qa,
    qg,
    gram,
    yin,
    xin,
    done,
    gin,
    segn,
    small,
    fin_y,
    fin_x,
    local_sem,
    own_send,
    own_recv,
    qg_send,
    qg_recv,
    qa_send,
    qa_recv,
    hop_send,
    hop_recv,
    tg_send,
    tg_recv,
    ta_send,
    ta_recv,
    tgf_send,
    tgf_recv,
    taf_send,
    taf_recv,
    y_send,
    y_recv,
    x_send,
    x_recv,
    g_send,
    g_recv,
    s_send,
    s_recv,
    fy_send,
    fy_recv,
    fx_send,
    fx_recv,
):
    rows_t, wide_a = ta_hbm.shape
    rows_q, wide_g = qg_hbm.shape
    half = rows_q // NCORE
    chunk = half // CHUNKS
    part = rows_t // TPARTS
    ry = chunk // (NY * NX)
    factor = math.sqrt(ST * SQ / (rows_t * rows_q))

    doc = lax.axis_index("doc")
    place = lax.axis_index("hidden")
    core = lax.rem(place, NCORE)
    other = 1 - core
    my_x = lax.rem(place // NCORE, NX)
    my_y = place // (NCORE * NX)
    up = lax.rem(doc + 1, n_doc)
    down = lax.rem(doc + n_doc - 1, n_doc)

    def y_of(d):
        return lax.rem(my_y + d, NY)

    def spot(y, x, c):
        return y * (NX * NCORE) + x * NCORE + c

    sibling = (doc, spot(my_y, my_x, other))
    x_peer = (doc, spot(my_y, 1 - my_x, core))
    x_other = (doc, spot(my_y, 1 - my_x, other))

    def y_peer(d, of=doc):
        return (of, spot(y_of(d), my_x, core))

    greet = [sibling, x_peer, x_other]
    greet += [(up, spot(my_y, my_x, other)), (down, spot(my_y, my_x, other))]
    greet += [y_peer(d) for d in range(1, NY)]
    greet += [y_peer(d, up) for d in range(NY)]
    greet += [y_peer(d, down) for d in range(NY)]
    barrier = pltpu.get_barrier_semaphore()
    for who in greet:
        pl.semaphore_signal(barrier, inc=1, device_id=who, device_id_type=MESH)
    pl.semaphore_wait(barrier, len(greet))

    def remote(src, dst, send, recv, who):
        return pltpu.make_async_remote_copy(
            src_ref=src, dst_ref=dst, send_sem=send, recv_sem=recv, device_id=who, device_id_type=MESH
        )

    def cols(wide, whose):
        return pl.ds(pl.multiple_of(whose * wide, LANES), wide)

    def q_half(whose):
        return pl.ds(pl.multiple_of(whose * half, half), half)

    def swap(j, whose_q, whose):
        return (
            (qg_hbm.at[q_half(whose_q), :], qg.at[0, :, cols(wide_g, whose)]),
            (tg_hbm, tg.at[0, :, cols(wide_g, whose)]),
            (qa_hbm.at[q_half(whose_q), :], qa.at[0, :, cols(wide_a, whose)]),
            (ta_hbm, ta.at[0, :, cols(wide_a, whose)]),
        )[j]

    def swap_out(j):
        return remote(*swap(j, other, core), own_send.at[j], own_recv.at[j], sibling)

    def swap_in(j):
        return remote(*swap(j, core, other), own_send.at[j], own_recv.at[j], sibling)

    def local(j):
        return pltpu.make_async_copy(*swap(j, core, core), local_sem.at[j])

    def who_up(far):
        return core if far == 0 else other

    def qg_up(far):
        to = who_up(far)
        return remote(
            qg_hbm.at[q_half(to), :],
            qg.at[1, :, cols(wide_g, core)],
            qg_send.at[far],
            qg_recv.at[far],
            (up, spot(my_y, my_x, to)),
        )

    def qg_arrival(far):
        return remote(
            qg_hbm.at[q_half(core), :],
            qg.at[1, :, cols(wide_g, who_up(far))],
            qg_send.at[far],
            qg_recv.at[far],
            (up, spot(my_y, my_x, who_up(far))),
        )

    def q_chunk(m):
        return pl.ds(m * chunk, chunk)

    def qa_up(m, far):
        to = who_up(far)
        return remote(
            qa_hbm.at[pl.ds(pl.multiple_of(to * half + m * chunk, chunk), chunk), :],
            qa.at[1, q_chunk(m), cols(wide_a, core)],
            qa_send.at[m, far],
            qa_recv.at[m, far],
            (up, spot(my_y, my_x, to)),
        )

    def qa_arrival(m, far):
        return remote(
            qa_hbm.at[pl.ds(pl.multiple_of(core * half + m * chunk, chunk), chunk), :],
            qa.at[1, q_chunk(m), cols(wide_a, who_up(far))],
            qa_send.at[m, far],
            qa_recv.at[m, far],
            (up, spot(my_y, my_x, who_up(far))),
        )

    def qa_hop(m):
        return remote(
            qa.at[1, q_chunk(m), :], qa.at[2, q_chunk(m), :], hop_send.at[m], hop_recv.at[m], (up, place)
        )

    def tg_down(step):
        src = tg_hbm if step == 0 else tg.at[step, :, cols(wide_g, core)]
        return remote(
            src, tg.at[step + 1, :, cols(wide_g, core)], tg_send.at[step], tg_recv.at[step], (down, place)
        )

    def tg_across(step, whose):
        ref = tg.at[step + 1, :, cols(wide_g, whose)]
        return remote(ref, ref, tgf_send.at[step], tgf_recv.at[step], sibling)

    def t_part(p):
        return pl.ds(p * part, part)

    def ta_down(p):
        return remote(
            ta_hbm.at[t_part(p), :],
            ta.at[1, t_part(p), cols(wide_a, core)],
            ta_send.at[p],
            ta_recv.at[p],
            (down, place),
        )

    def ta_across(p, whose):
        ref = ta.at[1, t_part(p), cols(wide_a, whose)]
        return remote(ref, ref, taf_send.at[p], taf_recv.at[p], sibling)

    seg_copy = remote(tseg_ref, segn, s_send, s_recv, (down, place))

    def area(name):
        kind, r, m, n, p, k = UNITS[name]
        return kind, r, pl.ds(m * ry, n * ry), pl.ds(p * part, k * part)

    def compute(name):
        kind, r, m, n, p, k = UNITS[name]
        if kind == ACT:
            query, train = qa.at[min(r, 2)], ta.at[1 if r == 3 else 0]
        else:
            query, train = qg.at[min(r, 1)], tg.at[max(r - 1, 0)]
        left = query[m * chunk : (m + n) * chunk, :]
        right = train[p * part : (p + k) * part, :]
        if n == CHUNKS:
            total = lax.dot_general(left, right, CONTRACT, preferred_element_type=F32)
        else:
            total = lax.dot_general(right, left, CONTRACT, preferred_element_type=F32).T
        for i in range(n):
            gram[kind, r, :, :, (m + i) * ry : (m + i + 1) * ry, p * part : (p + k) * part] = total[
                i * chunk : (i + 1) * chunk
            ].reshape(NY, NX, ry, k * part)

    def y_copy(name, d):
        kind, r, rows, lanes = area(name)
        u = ORDER.index(name)
        return remote(
            gram.at[kind, r, y_of(d), :, rows, lanes],
            yin.at[kind, r, d - 1, :, rows, lanes],
            y_send.at[u, d - 1],
            y_recv.at[u, d - 1],
            y_peer(d),
        )

    def x_copy(name):
        kind, r, rows, lanes = area(name)
        u = ORDER.index(name)
        return remote(
            gram.at[kind, r, my_y, 1 - my_x, rows, lanes],
            xin.at[kind, r, rows, lanes],
            x_send.at[u],
            x_recv.at[u],
            x_peer,
        )

    def g_move(r):
        return remote(done.at[GRAD, r], gin.at[r - 2], g_send.at[r - 2], g_recv.at[r - 2], (up, place))

    def unit(name):
        compute(name)
        for d in range(1, NY):
            y_copy(name, d).start()

    def y_finish(name):
        kind, r, rows, lanes = area(name)
        for d in range(1, NY):
            y_copy(name, d).wait_recv()
        gram[kind, r, my_y, :, rows, lanes] = (
            gram[kind, r, my_y, :, rows, lanes] + yin[kind, r, 0, :, rows, lanes]
        ) + (yin[kind, r, 1, :, rows, lanes] + yin[kind, r, 2, :, rows, lanes])
        x_copy(name).start()

    def x_finish(name):
        kind, r, rows, lanes = area(name)
        x_copy(name).wait_recv()
        done[kind, r, rows, lanes] = gram[kind, r, my_y, my_x, rows, lanes] + xin[kind, r, rows, lanes]

    def onehots(r):
        seg_t = (segn if r == 3 else tseg_ref)[...]
        onehot_t = (lax.broadcasted_iota(jnp.int32, (ST, rows_t), 0) == seg_t).astype(F32)
        owner = lax.rem(doc + n_doc - min(r, 2), n_doc)
        seg_q = qseg_ref[pl.ds(owner, 1), :]
        row = lax.broadcasted_iota(jnp.int32, (CHUNKS * ry, rows_q), 0)
        token = lax.broadcasted_iota(jnp.int32, (CHUNKS * ry, rows_q), 1)
        mine = core * half + (row // ry) * chunk + my_y * (NX * ry) + my_x * ry + row % ry
        ids = jnp.sum(jnp.where(token == mine, seg_q, 0), axis=1, keepdims=True)
        lane = lax.broadcasted_iota(jnp.int32, (CHUNKS * ry, LANES), 1)
        return onehot_t, (lane == ids + r * SQ).astype(F32)

    def segment_sum(r, hots):
        onehot_t, onehot_q = hots
        grads = gin[r - 2] if r >= 2 else done[GRAD, r]
        left = lax.dot_general(
            onehot_t,
            done[ACT, r] * grads,
            CONTRACT,
            precision=lax.Precision.HIGHEST,
            preferred_element_type=F32,
        )
        return jnp.dot(left, onehot_q, precision=lax.Precision.HIGHEST, preferred_element_type=F32)

    def arrive_and_hop(m):
        for far in range(2):
            qa_arrival(m, far).wait_recv()
        qa_hop(m).start()

    for far in range(2):
        qg_up(far).start()
    tg_down(0).start()
    for j in range(4):
        swap_out(j).start()
        local(j).start()
    for far in range(2):
        qa_up(0, far).start()
    ta_down(0).start()
    for m in range(1, CHUNKS):
        for far in range(2):
            qa_up(m, far).start()
    seg_copy.start()

    for j in range(2):
        local(j).wait()
        swap_in(j).wait_recv()
    unit("g0")
    for j in range(2, 4):
        local(j).wait()
        swap_in(j).wait_recv()
    unit("a0")
    for far in range(2):
        qg_arrival(far).wait_recv()
    unit("g1")
    tg_down(0).wait_recv()
    tg_down(1).start()
    tg_across(0, core).start()
    for p in range(1, TPARTS):
        ta_down(p).start()
    tg_across(0, other).wait_recv()
    unit("g2")
    arrive_and_hop(0)
    y_finish("g0")
    y_finish("a0")
    arrive_and_hop(1)
    unit("a1_01")
    x_finish("g0")
    x_finish("a0")
    ta_down(0).wait_recv()
    ta_across(0, core).start()
    y_finish("g1")
    arrive_and_hop(2)
    y_finish("g2")
    x_finish("g1")
    arrive_and_hop(3)
    unit("a1_23")
    x_finish("g2")
    g_move(2).start()
    y_finish("a1_01")
    tg_down(1).wait_recv()
    tg_across(1, core).start()
    tg_across(1, other).wait_recv()
    unit("g3")
    x_finish("a1_01")
    qa_hop(0).wait_recv()
    unit("a2_0")
    y_finish("a1_23")
    y_finish("g3")
    qa_hop(1).wait_recv()
    unit("a2_1")
    x_finish("a1_23")
    x_finish("g3")
    g_move(3).start()
    y_finish("a2_0")
    ta_down(1).wait_recv()
    ta_across(1, core).start()
    base = segment_sum(0, onehots(0)) + segment_sum(1, onehots(1))
    seg_copy.wait_recv()
    hots_2, hots_3 = onehots(2), onehots(3)
    for p in range(2):
        ta_across(p, other).wait_recv()
    unit("a3_01")
    x_finish("a2_0")
    y_finish("a2_1")
    qa_hop(2).wait_recv()
    unit("a2_2")
    unit("a3_2")
    y_finish("a3_01")
    x_finish("a2_1")
    y_finish("a2_2")
    y_finish("a3_2")
    x_finish("a3_01")
    ta_down(2).wait_recv()
    ta_across(2, core).start()
    qa_hop(3).wait_recv()
    unit("a3_3")
    unit("a2_3")
    ta_across(2, other).wait_recv()
    unit("a3_all")
    x_finish("a2_2")
    x_finish("a3_2")
    y_finish("a3_3")
    y_finish("a2_3")
    y_finish("a3_all")
    for r in range(2, CYCLE):
        g_move(r).wait_recv()
    x_finish("a2_3")
    fin_y[0, my_y] = base + segment_sum(2, hots_2)
    fy = [
        remote(fin_y.at[0, my_y], fin_y.at[0, my_y], fy_send.at[0, d], fy_recv.at[0, my_y], y_peer(d))
        for d in range(1, NY)
    ]
    for copy in fy:
        copy.start()
    x_finish("a3_3")
    x_finish("a3_all")
    small[...] = segment_sum(3, hots_3)
    fu = [
        remote(small, fin_y.at[1, my_y], fy_send.at[1, d], fy_recv.at[1, my_y], y_peer(d, up))
        for d in range(NY)
    ]
    for copy in fu:
        copy.start()
    for d in range(1, NY):
        y = y_of(d)
        remote(fin_y.at[0, y], fin_y.at[0, y], fy_send.at[0, d], fy_recv.at[0, y], y_peer(d)).wait_recv()
    for d in range(NY):
        y = y_of(d)
        remote(small, fin_y.at[1, y], fy_send.at[1, d], fy_recv.at[1, y], y_peer(d, up)).wait_recv()
    total = fin_y[0, 0] + fin_y[1, 0]
    for y in range(1, NY):
        total = total + (fin_y[0, y] + fin_y[1, y])
    mine = lax.rem(place, NX * NCORE)
    fin_x[mine] = total
    fx = []
    for i, who in enumerate((sibling, x_peer, x_other)):
        fx.append(remote(fin_x.at[mine], fin_x.at[mine], fx_send.at[i], fx_recv.at[mine], who))
        fx[-1].start()
    for i, (x, c) in enumerate(((my_x, other), (1 - my_x, core), (1 - my_x, other))):
        at = x * NCORE + c
        remote(fin_x.at[at], fin_x.at[at], fx_send.at[i], fx_recv.at[at], sibling).wait_recv()
    out_ref[...] = (((fin_x[0] + fin_x[1]) + (fin_x[2] + fin_x[3])) * factor)[:, : CYCLE * SQ]

    seg_copy.wait_send()
    for copy in fy + fu + fx:
        copy.wait_send()
    for j in range(4):
        swap_out(j).wait_send()
    for far in range(2):
        qg_up(far).wait_send()
    for m in range(CHUNKS):
        for far in range(2):
            qa_up(m, far).wait_send()
        qa_hop(m).wait_send()
    for step in range(2):
        tg_down(step).wait_send()
        tg_across(step, core).wait_send()
    for p in range(TPARTS):
        ta_down(p).wait_send()
        ta_across(p, core).wait_send()
    for r in range(2, CYCLE):
        g_move(r).wait_send()
    for name in ORDER:
        for d in range(1, NY):
            y_copy(name, d).wait_send()
        x_copy(name).wait_send()


def on_device(n_doc, train_acts, train_grads, query_acts, query_grads, train_seg, query_seg):
    rows_t, wide_a = train_acts.shape
    rows_q, wide_g = query_grads.shape
    half = rows_q // NCORE
    rows = half // (NY * NX)
    units = len(ORDER)
    dma = pltpu.SemaphoreType.DMA
    anywhere = pl.BlockSpec(memory_space=pl.ANY)
    vmem = pl.BlockSpec(memory_space=pltpu.VMEM)
    bf16 = jnp.bfloat16

    def pair(*shape):
        return [dma(shape), dma(shape)]

    return pl.pallas_call(
        functools.partial(kernel, n_doc),
        out_shape=jax.ShapeDtypeStruct((ST, CYCLE * SQ), F32),
        in_specs=[anywhere] * 4 + [vmem] * 2,
        out_specs=vmem,
        scratch_shapes=[
            pltpu.VMEM((2, rows_t, NCORE * wide_a), bf16),
            pltpu.VMEM((3, rows_t, NCORE * wide_g), bf16),
            pltpu.VMEM((3, half, NCORE * wide_a), bf16),
            pltpu.VMEM((2, half, NCORE * wide_g), bf16),
            pltpu.VMEM((2, CYCLE, NY, NX, rows, rows_t), F32),
            pltpu.VMEM((2, CYCLE, NY - 1, NX, rows, rows_t), F32),
            pltpu.VMEM((2, CYCLE, rows, rows_t), F32),
            pltpu.VMEM((2, CYCLE, rows, rows_t), F32),
            pltpu.VMEM((2, rows, rows_t), F32),
            pltpu.VMEM((1, rows_t), jnp.int32),
            pltpu.VMEM((ST, LANES), F32),
            pltpu.VMEM((2, NY, ST, LANES), F32),
            pltpu.VMEM((NX * NCORE, ST, LANES), F32),
            dma((4,)),
            *pair(4),
            *pair(2),
            *pair(CHUNKS, 2),
            *pair(CHUNKS),
            *pair(2),
            *pair(TPARTS),
            *pair(2),
            *pair(TPARTS),
            *pair(units, NY - 1),
            *pair(units),
            *pair(2),
            dma,
            dma,
            *pair(2, NY),
            *pair(NX * NCORE),
        ],
        compiler_params=pltpu.CompilerParams(
            collective_id=0, has_side_effects=True, vmem_limit_bytes=56 * 1024 * 1024
        ),
        name="influence",
    )(train_acts, train_grads, query_acts, query_grads, train_seg, query_seg)


def solution(mesh):
    in_specs = (
        P("doc", "hidden"),
        P("doc", "hidden"),
        P("doc", "hidden"),
        P("doc", "hidden"),
        P("doc", None),
        P(),
    )
    return jax.shard_map(
        functools.partial(on_device, mesh.shape["doc"]),
        mesh=mesh,
        in_specs=in_specs,
        out_specs=P("doc", None),
        check_vma=False,
    )
```

```python
import functools
import math

import jax
import jax.numpy as jnp
from jax import lax
from jax.experimental import pallas as pl
from jax.experimental.pallas import tpu as pltpu
from jax.sharding import PartitionSpec as P

ST = 8
SQ = 8
CYCLE = 4
NY = 4
NX = 2
NCORE = 2
CHUNKS = 4
TPARTS = 3
LANES = 128
ACT = 0
GRAD = 1
MESH = pl.DeviceIdType.MESH
CONTRACT = (((1,), (1,)), ((), ()))
F32 = jnp.float32

UNITS = {
    "g0": (GRAD, 0, 0, 4, 0, 3),
    "a0": (ACT, 0, 0, 4, 0, 3),
    "g1": (GRAD, 1, 0, 4, 0, 3),
    "g2": (GRAD, 2, 0, 4, 0, 3),
    "g3": (GRAD, 3, 0, 4, 0, 3),
    "a1_01": (ACT, 1, 0, 2, 0, 3),
    "a1_23": (ACT, 1, 2, 2, 0, 3),
    "a2_0": (ACT, 2, 0, 1, 0, 3),
    "a2_1": (ACT, 2, 1, 1, 0, 3),
    "a2_2": (ACT, 2, 2, 1, 0, 3),
    "a2_3": (ACT, 2, 3, 1, 0, 3),
    "a3_01": (ACT, 3, 0, 2, 0, 2),
    "a3_2": (ACT, 3, 2, 1, 0, 2),
    "a3_3": (ACT, 3, 3, 1, 0, 2),
    "a3_all": (ACT, 3, 0, 4, 2, 1),
}
ORDER = list(UNITS)


def kernel(
    n_doc,
    ta_hbm,
    tg_hbm,
    qa_hbm,
    qg_hbm,
    tseg_ref,
    qseg_ref,
    out_ref,
    ta,
    tg,
    qa,
    qg,
    gram,
    yin,
    xin,
    done,
    gin,
    segn,
    small,
    fin_y,
    fin_x,
    local_sem,
    own_send,
    own_recv,
    qg_send,
    qg_recv,
    qa_send,
    qa_recv,
    hop_send,
    hop_recv,
    tg_send,
    tg_recv,
    ta_send,
    ta_recv,
    tgf_send,
    tgf_recv,
    taf_send,
    taf_recv,
    y_send,
    y_recv,
    x_send,
    x_recv,
    g_send,
    g_recv,
    s_send,
    s_recv,
    fy_send,
    fy_recv,
    fx_send,
    fx_recv,
):
    rows_t, wide_a = ta_hbm.shape
    rows_q, wide_g = qg_hbm.shape
    half = rows_q // NCORE
    chunk = half // CHUNKS
    part = rows_t // TPARTS
    ry = chunk // (NY * NX)
    factor = math.sqrt(ST * SQ / (rows_t * rows_q))

    doc = lax.axis_index("doc")
    place = lax.axis_index("hidden")
    core = lax.rem(place, NCORE)
    other = 1 - core
    my_x = lax.rem(place // NCORE, NX)
    my_y = place // (NCORE * NX)
    up = lax.rem(doc + 1, n_doc)
    down = lax.rem(doc + n_doc - 1, n_doc)

    def y_of(d):
        return lax.rem(my_y + d, NY)

    def spot(y, x, c):
        return y * (NX * NCORE) + x * NCORE + c

    sibling = (doc, spot(my_y, my_x, other))
    x_peer = (doc, spot(my_y, 1 - my_x, core))
    x_other = (doc, spot(my_y, 1 - my_x, other))

    def y_peer(d, of=doc):
        return (of, spot(y_of(d), my_x, core))

    greet = [sibling, x_peer, x_other]
    greet += [(up, spot(my_y, my_x, other)), (down, spot(my_y, my_x, other))]
    greet += [y_peer(d) for d in range(1, NY)]
    greet += [y_peer(d, up) for d in range(NY)]
    greet += [y_peer(d, down) for d in range(NY)]
    barrier = pltpu.get_barrier_semaphore()
    for who in greet:
        pl.semaphore_signal(barrier, inc=1, device_id=who, device_id_type=MESH)
    pl.semaphore_wait(barrier, len(greet))

    def remote(src, dst, send, recv, who):
        return pltpu.make_async_remote_copy(
            src_ref=src, dst_ref=dst, send_sem=send, recv_sem=recv, device_id=who, device_id_type=MESH
        )

    def cols(wide, whose):
        return pl.ds(pl.multiple_of(whose * wide, LANES), wide)

    def q_half(whose):
        return pl.ds(pl.multiple_of(whose * half, half), half)

    def swap(j, whose_q, whose):
        return (
            (qg_hbm.at[q_half(whose_q), :], qg.at[0, :, cols(wide_g, whose)]),
            (tg_hbm, tg.at[0, :, cols(wide_g, whose)]),
            (qa_hbm.at[q_half(whose_q), :], qa.at[0, :, cols(wide_a, whose)]),
            (ta_hbm, ta.at[0, :, cols(wide_a, whose)]),
        )[j]

    def swap_out(j):
        return remote(*swap(j, other, core), own_send.at[j], own_recv.at[j], sibling)

    def swap_in(j):
        return remote(*swap(j, core, other), own_send.at[j], own_recv.at[j], sibling)

    def local(j):
        return pltpu.make_async_copy(*swap(j, core, core), local_sem.at[j])

    def who_up(far):
        return core if far == 0 else other

    def qg_up(far):
        to = who_up(far)
        return remote(
            qg_hbm.at[q_half(to), :],
            qg.at[1, :, cols(wide_g, core)],
            qg_send.at[far],
            qg_recv.at[far],
            (up, spot(my_y, my_x, to)),
        )

    def qg_arrival(far):
        return remote(
            qg_hbm.at[q_half(core), :],
            qg.at[1, :, cols(wide_g, who_up(far))],
            qg_send.at[far],
            qg_recv.at[far],
            (up, spot(my_y, my_x, who_up(far))),
        )

    def q_chunk(m):
        return pl.ds(m * chunk, chunk)

    def qa_up(m, far):
        to = who_up(far)
        return remote(
            qa_hbm.at[pl.ds(pl.multiple_of(to * half + m * chunk, chunk), chunk), :],
            qa.at[1, q_chunk(m), cols(wide_a, core)],
            qa_send.at[m, far],
            qa_recv.at[m, far],
            (up, spot(my_y, my_x, to)),
        )

    def qa_arrival(m, far):
        return remote(
            qa_hbm.at[pl.ds(pl.multiple_of(core * half + m * chunk, chunk), chunk), :],
            qa.at[1, q_chunk(m), cols(wide_a, who_up(far))],
            qa_send.at[m, far],
            qa_recv.at[m, far],
            (up, spot(my_y, my_x, who_up(far))),
        )

    def qa_hop(m):
        return remote(
            qa.at[1, q_chunk(m), :], qa.at[2, q_chunk(m), :], hop_send.at[m], hop_recv.at[m], (up, place)
        )

    def tg_down(step):
        src = tg_hbm if step == 0 else tg.at[step, :, cols(wide_g, core)]
        return remote(
            src, tg.at[step + 1, :, cols(wide_g, core)], tg_send.at[step], tg_recv.at[step], (down, place)
        )

    def tg_across(step, whose):
        ref = tg.at[step + 1, :, cols(wide_g, whose)]
        return remote(ref, ref, tgf_send.at[step], tgf_recv.at[step], sibling)

    def t_part(p):
        return pl.ds(p * part, part)

    def ta_down(p):
        return remote(
            ta_hbm.at[t_part(p), :],
            ta.at[1, t_part(p), cols(wide_a, core)],
            ta_send.at[p],
            ta_recv.at[p],
            (down, place),
        )

    def ta_across(p, whose):
        ref = ta.at[1, t_part(p), cols(wide_a, whose)]
        return remote(ref, ref, taf_send.at[p], taf_recv.at[p], sibling)

    seg_copy = remote(tseg_ref, segn, s_send, s_recv, (down, place))

    def area(name):
        kind, r, m, n, p, k = UNITS[name]
        return kind, r, pl.ds(m * ry, n * ry), pl.ds(p * part, k * part)

    def compute(name):
        kind, r, m, n, p, k = UNITS[name]
        if kind == ACT:
            query, train = qa.at[min(r, 2)], ta.at[1 if r == 3 else 0]
        else:
            query, train = qg.at[min(r, 1)], tg.at[max(r - 1, 0)]
        left = query[m * chunk : (m + n) * chunk, :]
        right = train[p * part : (p + k) * part, :]
        if n == CHUNKS:
            total = lax.dot_general(left, right, CONTRACT, preferred_element_type=F32)
        else:
            total = lax.dot_general(right, left, CONTRACT, preferred_element_type=F32).T
        for i in range(n):
            gram[kind, r, :, :, (m + i) * ry : (m + i + 1) * ry, p * part : (p + k) * part] = total[
                i * chunk : (i + 1) * chunk
            ].reshape(NY, NX, ry, k * part)

    def y_copy(name, d):
        kind, r, rows, lanes = area(name)
        u = ORDER.index(name)
        return remote(
            gram.at[kind, r, y_of(d), :, rows, lanes],
            yin.at[kind, r, d - 1, :, rows, lanes],
            y_send.at[u, d - 1],
            y_recv.at[u, d - 1],
            y_peer(d),
        )

    def x_copy(name):
        kind, r, rows, lanes = area(name)
        u = ORDER.index(name)
        return remote(
            gram.at[kind, r, my_y, 1 - my_x, rows, lanes],
            xin.at[kind, r, rows, lanes],
            x_send.at[u],
            x_recv.at[u],
            x_peer,
        )

    def g_move(r):
        return remote(done.at[GRAD, r], gin.at[r - 2], g_send.at[r - 2], g_recv.at[r - 2], (up, place))

    def unit(name):
        compute(name)
        for d in range(1, NY):
            y_copy(name, d).start()

    def y_finish(name):
        kind, r, rows, lanes = area(name)
        for d in range(1, NY):
            y_copy(name, d).wait_recv()
        gram[kind, r, my_y, :, rows, lanes] = (
            gram[kind, r, my_y, :, rows, lanes] + yin[kind, r, 0, :, rows, lanes]
        ) + (yin[kind, r, 1, :, rows, lanes] + yin[kind, r, 2, :, rows, lanes])
        x_copy(name).start()

    def x_finish(name):
        kind, r, rows, lanes = area(name)
        x_copy(name).wait_recv()
        done[kind, r, rows, lanes] = gram[kind, r, my_y, my_x, rows, lanes] + xin[kind, r, rows, lanes]

    def onehots(r):
        seg_t = (segn if r == 3 else tseg_ref)[...]
        onehot_t = (lax.broadcasted_iota(jnp.int32, (ST, rows_t), 0) == seg_t).astype(F32)
        owner = lax.rem(doc + n_doc - min(r, 2), n_doc)
        seg_q = qseg_ref[pl.ds(owner, 1), :]
        row = lax.broadcasted_iota(jnp.int32, (CHUNKS * ry, rows_q), 0)
        token = lax.broadcasted_iota(jnp.int32, (CHUNKS * ry, rows_q), 1)
        mine = core * half + (row // ry) * chunk + my_y * (NX * ry) + my_x * ry + row % ry
        ids = jnp.sum(jnp.where(token == mine, seg_q, 0), axis=1, keepdims=True)
        lane = lax.broadcasted_iota(jnp.int32, (CHUNKS * ry, LANES), 1)
        return onehot_t, (lane == ids + r * SQ).astype(F32)

    def segment_sum(r, hots):
        onehot_t, onehot_q = hots
        grads = gin[r - 2] if r >= 2 else done[GRAD, r]
        left = lax.dot_general(
            onehot_t,
            done[ACT, r] * grads,
            CONTRACT,
            precision=lax.Precision.HIGHEST,
            preferred_element_type=F32,
        )
        return jnp.dot(left, onehot_q, precision=lax.Precision.HIGHEST, preferred_element_type=F32)

    def arrive_and_hop(m):
        for far in range(2):
            qa_arrival(m, far).wait_recv()
        qa_hop(m).start()

    for far in range(2):
        qg_up(far).start()
    tg_down(0).start()
    for j in range(4):
        swap_out(j).start()
        local(j).start()
    for far in range(2):
        qa_up(0, far).start()
    ta_down(0).start()
    for m in range(1, CHUNKS):
        for far in range(2):
            qa_up(m, far).start()
    seg_copy.start()

    for j in range(2):
        local(j).wait()
        swap_in(j).wait_recv()
    unit("g0")
    for j in range(2, 4):
        local(j).wait()
        swap_in(j).wait_recv()
    unit("a0")
    for far in range(2):
        qg_arrival(far).wait_recv()
    unit("g1")
    tg_down(0).wait_recv()
    tg_down(1).start()
    tg_across(0, core).start()
    for p in range(1, TPARTS):
        ta_down(p).start()
    tg_across(0, other).wait_recv()
    unit("g2")
    arrive_and_hop(0)
    y_finish("g0")
    y_finish("a0")
    arrive_and_hop(1)
    unit("a1_01")
    y_finish("g1")
    arrive_and_hop(2)
    ta_down(0).wait_recv()
    ta_across(0, core).start()
    y_finish("g2")
    arrive_and_hop(3)
    unit("a1_23")
    tg_down(1).wait_recv()
    tg_across(1, core).start()
    y_finish("a1_01")
    tg_across(1, other).wait_recv()
    unit("g3")
    qa_hop(0).wait_recv()
    unit("a2_0")
    y_finish("a1_23")
    qa_hop(1).wait_recv()
    unit("a2_1")
    y_finish("g3")
    for name in ("g0", "a0", "g1", "g2"):
        x_finish(name)
    g_move(2).start()
    y_finish("a2_0")
    ta_down(1).wait_recv()
    ta_across(1, core).start()
    for p in range(2):
        ta_across(p, other).wait_recv()
    unit("a3_01")
    y_finish("a2_1")
    for name in ("a1_01", "a1_23", "g3"):
        x_finish(name)
    g_move(3).start()
    base = segment_sum(0, onehots(0)) + segment_sum(1, onehots(1))
    seg_copy.wait_recv()
    hots_2, hots_3 = onehots(2), onehots(3)
    qa_hop(2).wait_recv()
    unit("a2_2")
    unit("a3_2")
    y_finish("a3_01")
    for name in ("a2_0", "a2_1"):
        x_finish(name)
    y_finish("a2_2")
    y_finish("a3_2")
    ta_down(2).wait_recv()
    ta_across(2, core).start()
    qa_hop(3).wait_recv()
    unit("a3_3")
    unit("a2_3")
    ta_across(2, other).wait_recv()
    unit("a3_all")
    for name in ("a3_01", "a2_2", "a3_2"):
        x_finish(name)
    y_finish("a3_3")
    y_finish("a2_3")
    y_finish("a3_all")
    for r in range(2, CYCLE):
        g_move(r).wait_recv()
    x_finish("a2_3")
    fin_y[0, my_y] = base + segment_sum(2, hots_2)
    fy = [
        remote(fin_y.at[0, my_y], fin_y.at[0, my_y], fy_send.at[0, d], fy_recv.at[0, my_y], y_peer(d))
        for d in range(1, NY)
    ]
    for copy in fy:
        copy.start()
    x_finish("a3_3")
    x_finish("a3_all")
    small[...] = segment_sum(3, hots_3)
    fu = [
        remote(small, fin_y.at[1, my_y], fy_send.at[1, d], fy_recv.at[1, my_y], y_peer(d, up))
        for d in range(NY)
    ]
    for copy in fu:
        copy.start()
    for d in range(1, NY):
        y = y_of(d)
        remote(fin_y.at[0, y], fin_y.at[0, y], fy_send.at[0, d], fy_recv.at[0, y], y_peer(d)).wait_recv()
    for d in range(NY):
        y = y_of(d)
        remote(small, fin_y.at[1, y], fy_send.at[1, d], fy_recv.at[1, y], y_peer(d, up)).wait_recv()
    total = fin_y[0, 0] + fin_y[1, 0]
    for y in range(1, NY):
        total = total + (fin_y[0, y] + fin_y[1, y])
    mine = lax.rem(place, NX * NCORE)
    fin_x[mine] = total
    fx = []
    for i, who in enumerate((sibling, x_peer, x_other)):
        fx.append(remote(fin_x.at[mine], fin_x.at[mine], fx_send.at[i], fx_recv.at[mine], who))
        fx[-1].start()
    for i, (x, c) in enumerate(((my_x, other), (1 - my_x, core), (1 - my_x, other))):
        at = x * NCORE + c
        remote(fin_x.at[at], fin_x.at[at], fx_send.at[i], fx_recv.at[at], sibling).wait_recv()
    out_ref[...] = (((fin_x[0] + fin_x[1]) + (fin_x[2] + fin_x[3])) * factor)[:, : CYCLE * SQ]

    seg_copy.wait_send()
    for copy in fy + fu + fx:
        copy.wait_send()
    for j in range(4):
        swap_out(j).wait_send()
    for far in range(2):
        qg_up(far).wait_send()
    for m in range(CHUNKS):
        for far in range(2):
            qa_up(m, far).wait_send()
        qa_hop(m).wait_send()
    for step in range(2):
        tg_down(step).wait_send()
        tg_across(step, core).wait_send()
    for p in range(TPARTS):
        ta_down(p).wait_send()
        ta_across(p, core).wait_send()
    for r in range(2, CYCLE):
        g_move(r).wait_send()
    for name in ORDER:
        for d in range(1, NY):
            y_copy(name, d).wait_send()
        x_copy(name).wait_send()


def on_device(n_doc, train_acts, train_grads, query_acts, query_grads, train_seg, query_seg):
    rows_t, wide_a = train_acts.shape
    rows_q, wide_g = query_grads.shape
    half = rows_q // NCORE
    rows = half // (NY * NX)
    units = len(ORDER)
    dma = pltpu.SemaphoreType.DMA
    anywhere = pl.BlockSpec(memory_space=pl.ANY)
    vmem = pl.BlockSpec(memory_space=pltpu.VMEM)
    bf16 = jnp.bfloat16

    def pair(*shape):
        return [dma(shape), dma(shape)]

    return pl.pallas_call(
        functools.partial(kernel, n_doc),
        out_shape=jax.ShapeDtypeStruct((ST, CYCLE * SQ), F32),
        in_specs=[anywhere] * 4 + [vmem] * 2,
        out_specs=vmem,
        scratch_shapes=[
            pltpu.VMEM((2, rows_t, NCORE * wide_a), bf16),
            pltpu.VMEM((3, rows_t, NCORE * wide_g), bf16),
            pltpu.VMEM((3, half, NCORE * wide_a), bf16),
            pltpu.VMEM((2, half, NCORE * wide_g), bf16),
            pltpu.VMEM((2, CYCLE, NY, NX, rows, rows_t), F32),
            pltpu.VMEM((2, CYCLE, NY - 1, NX, rows, rows_t), F32),
            pltpu.VMEM((2, CYCLE, rows, rows_t), F32),
            pltpu.VMEM((2, CYCLE, rows, rows_t), F32),
            pltpu.VMEM((2, rows, rows_t), F32),
            pltpu.VMEM((1, rows_t), jnp.int32),
            pltpu.VMEM((ST, LANES), F32),
            pltpu.VMEM((2, NY, ST, LANES), F32),
            pltpu.VMEM((NX * NCORE, ST, LANES), F32),
            dma((4,)),
            *pair(4),
            *pair(2),
            *pair(CHUNKS, 2),
            *pair(CHUNKS),
            *pair(2),
            *pair(TPARTS),
            *pair(2),
            *pair(TPARTS),
            *pair(units, NY - 1),
            *pair(units),
            *pair(2),
            dma,
            dma,
            *pair(2, NY),
            *pair(NX * NCORE),
        ],
        compiler_params=pltpu.CompilerParams(
            collective_id=0, has_side_effects=True, vmem_limit_bytes=56 * 1024 * 1024
        ),
        name="influence",
    )(train_acts, train_grads, query_acts, query_grads, train_seg, query_seg)


def solution(mesh):
    in_specs = (
        P("doc", "hidden"),
        P("doc", "hidden"),
        P("doc", "hidden"),
        P("doc", "hidden"),
        P("doc", None),
        P(),
    )
    return jax.shard_map(
        functools.partial(on_device, mesh.shape["doc"]),
        mesh=mesh,
        in_specs=in_specs,
        out_specs=P("doc", None),
        check_vma=False,
    )
```

```python
import functools
import math

import jax
import jax.numpy as jnp
from jax import lax
from jax.experimental import pallas as pl
from jax.experimental.pallas import tpu as pltpu
from jax.sharding import PartitionSpec as P

ST = 8
SQ = 8
CYCLE = 4
NY = 4
NX = 2
NCORE = 2
CHUNKS = 4
TPARTS = 3
LANES = 128
ACT = 0
GRAD = 1
MESH = pl.DeviceIdType.MESH
CONTRACT = (((1,), (1,)), ((), ()))
F32 = jnp.float32
I32 = jnp.int32
TOP = 32767.0
LEAST = 1e-34

UNITS = {
    "g0": (GRAD, 0, 0, 4, 0, 3),
    "a0": (ACT, 0, 0, 4, 0, 3),
    "g1": (GRAD, 1, 0, 4, 0, 3),
    "g2": (GRAD, 2, 0, 4, 0, 3),
    "g3": (GRAD, 3, 0, 4, 0, 3),
    "a1_01": (ACT, 1, 0, 2, 0, 3),
    "a1_23": (ACT, 1, 2, 2, 0, 3),
    "a2_0": (ACT, 2, 0, 1, 0, 3),
    "a2_1": (ACT, 2, 1, 1, 0, 3),
    "a2_2": (ACT, 2, 2, 1, 0, 3),
    "a2_3": (ACT, 2, 3, 1, 0, 3),
    "a3_01": (ACT, 3, 0, 2, 0, 2),
    "a3_2": (ACT, 3, 2, 1, 0, 2),
    "a3_3": (ACT, 3, 3, 1, 0, 2),
    "a3_all": (ACT, 3, 0, 4, 2, 1),
}
ORDER = list(UNITS)


def spread(tile, rows, lanes):
    wide = jnp.concatenate([tile] * (lanes // LANES), axis=1) if lanes > LANES else tile
    return jnp.concatenate([wide] * (rows // 8), axis=0) if rows > 8 else wide


def highest(value):
    rows, lanes = value.shape
    top = jnp.max(jnp.abs(value).reshape(rows // 8, 8, lanes), axis=0)
    return functools.reduce(
        jnp.maximum, [top[:, b * LANES : (b + 1) * LANES] for b in range(lanes // LANES)]
    )


def squeeze(high, low):
    scale = jnp.maximum(jnp.maximum(highest(high), highest(low)), LEAST)
    times = spread(TOP / scale, *high.shape)
    packed = jnp.round(high * times).astype(I32) * 65536 + jnp.round(low * times).astype(I32)
    return packed, scale * (1.0 / TOP)


def unsqueeze(packed, step):
    high = lax.shift_right_arithmetic(packed + 32768, jnp.full_like(packed, 16))
    low = packed - high * 65536
    step = spread(step, *packed.shape)
    return high.astype(F32) * step, low.astype(F32) * step


def kernel(
    n_doc,
    ta_hbm,
    tg_hbm,
    qa_hbm,
    qg_hbm,
    tseg_ref,
    qseg_ref,
    out_ref,
    ta,
    tg,
    qa,
    qg,
    gram,
    yout,
    yout_step,
    yin,
    yin_step,
    xout,
    xout_step,
    xin,
    xin_step,
    done,
    gin,
    segn,
    small,
    fin_y,
    fin_x,
    local_sem,
    own_send,
    own_recv,
    qg_send,
    qg_recv,
    qa_send,
    qa_recv,
    hop_send,
    hop_recv,
    tg_send,
    tg_recv,
    ta_send,
    ta_recv,
    tgf_send,
    tgf_recv,
    taf_send,
    taf_recv,
    y_send,
    y_recv,
    x_send,
    x_recv,
    g_send,
    g_recv,
    s_send,
    s_recv,
    fy_send,
    fy_recv,
    fx_send,
    fx_recv,
):
    rows_t, wide_a = ta_hbm.shape
    rows_q, wide_g = qg_hbm.shape
    half = rows_q // NCORE
    chunk = half // CHUNKS
    part = rows_t // TPARTS
    ry = chunk // (NY * NX)
    factor = math.sqrt(ST * SQ / (rows_t * rows_q))

    doc = lax.axis_index("doc")
    place = lax.axis_index("hidden")
    core = lax.rem(place, NCORE)
    other = 1 - core
    my_x = lax.rem(place // NCORE, NX)
    my_y = place // (NCORE * NX)
    up = lax.rem(doc + 1, n_doc)
    down = lax.rem(doc + n_doc - 1, n_doc)

    def y_of(d):
        return lax.rem(my_y + d, NY)

    def spot(y, x, c):
        return y * (NX * NCORE) + x * NCORE + c

    sibling = (doc, spot(my_y, my_x, other))
    x_peer = (doc, spot(my_y, 1 - my_x, core))
    x_other = (doc, spot(my_y, 1 - my_x, other))

    def y_peer(d, of=doc):
        return (of, spot(y_of(d), my_x, core))

    def remote(src, dst, send, recv, who):
        return pltpu.make_async_remote_copy(
            src_ref=src, dst_ref=dst, send_sem=send, recv_sem=recv, device_id=who, device_id_type=MESH
        )

    def cols(wide, whose):
        return pl.ds(pl.multiple_of(whose * wide, LANES), wide)

    def q_half(whose):
        return pl.ds(pl.multiple_of(whose * half, half), half)

    def swap(j, whose_q, whose):
        return (
            (qg_hbm.at[q_half(whose_q), :], qg.at[0, :, cols(wide_g, whose)]),
            (tg_hbm, tg.at[0, :, cols(wide_g, whose)]),
            (qa_hbm.at[q_half(whose_q), :], qa.at[0, :, cols(wide_a, whose)]),
            (ta_hbm, ta.at[0, :, cols(wide_a, whose)]),
        )[j]

    def swap_out(j):
        return remote(*swap(j, other, core), own_send.at[j], own_recv.at[j], sibling)

    def swap_in(j):
        return remote(*swap(j, core, other), own_send.at[j], own_recv.at[j], sibling)

    def local(j):
        return pltpu.make_async_copy(*swap(j, core, core), local_sem.at[j])

    def who_up(far):
        return core if far == 0 else other

    def qg_up(far):
        to = who_up(far)
        return remote(
            qg_hbm.at[q_half(to), :],
            qg.at[1, :, cols(wide_g, core)],
            qg_send.at[far],
            qg_recv.at[far],
            (up, spot(my_y, my_x, to)),
        )

    def qg_arrival(far):
        return remote(
            qg_hbm.at[q_half(core), :],
            qg.at[1, :, cols(wide_g, who_up(far))],
            qg_send.at[far],
            qg_recv.at[far],
            (up, spot(my_y, my_x, who_up(far))),
        )

    def q_chunk(m):
        return pl.ds(m * chunk, chunk)

    def qa_up(m, far):
        to = who_up(far)
        return remote(
            qa_hbm.at[pl.ds(pl.multiple_of(to * half + m * chunk, chunk), chunk), :],
            qa.at[1, q_chunk(m), cols(wide_a, core)],
            qa_send.at[m, far],
            qa_recv.at[m, far],
            (up, spot(my_y, my_x, to)),
        )

    def qa_arrival(m, far):
        return remote(
            qa_hbm.at[pl.ds(pl.multiple_of(core * half + m * chunk, chunk), chunk), :],
            qa.at[1, q_chunk(m), cols(wide_a, who_up(far))],
            qa_send.at[m, far],
            qa_recv.at[m, far],
            (up, spot(my_y, my_x, who_up(far))),
        )

    def qa_hop(m):
        return remote(
            qa.at[1, q_chunk(m), :], qa.at[2, q_chunk(m), :], hop_send.at[m], hop_recv.at[m], (up, place)
        )

    def tg_down(step):
        src = tg_hbm if step == 0 else tg.at[step, :, cols(wide_g, core)]
        return remote(
            src, tg.at[step + 1, :, cols(wide_g, core)], tg_send.at[step], tg_recv.at[step], (down, place)
        )

    def tg_across(step, whose):
        ref = tg.at[step + 1, :, cols(wide_g, whose)]
        return remote(ref, ref, tgf_send.at[step], tgf_recv.at[step], sibling)

    def t_part(p):
        return pl.ds(p * part, part)

    def ta_down(p):
        return remote(
            ta_hbm.at[t_part(p), :],
            ta.at[1, t_part(p), cols(wide_a, core)],
            ta_send.at[p],
            ta_recv.at[p],
            (down, place),
        )

    def ta_across(p, whose):
        ref = ta.at[1, t_part(p), cols(wide_a, whose)]
        return remote(ref, ref, taf_send.at[p], taf_recv.at[p], sibling)

    seg_copy = remote(tseg_ref, segn, s_send, s_recv, (down, place))

    def area(name):
        kind, r, m, n, p, k = UNITS[name]
        return kind, r, pl.ds(m * ry, n * ry), pl.ds(p * part, k * part)

    def compute(name):
        kind, r, m, n, p, k = UNITS[name]
        if kind == ACT:
            query, train = qa.at[min(r, 2)], ta.at[1 if r == 3 else 0]
        else:
            query, train = qg.at[min(r, 1)], tg.at[max(r - 1, 0)]
        left = query[m * chunk : (m + n) * chunk, :]
        right = train[p * part : (p + k) * part, :]
        if n == CHUNKS:
            total = lax.dot_general(left, right, CONTRACT, preferred_element_type=F32)
        else:
            total = lax.dot_general(right, left, CONTRACT, preferred_element_type=F32).T
        for i in range(n):
            gram[kind, r, :, :, (m + i) * ry : (m + i + 1) * ry, p * part : (p + k) * part] = total[
                i * chunk : (i + 1) * chunk
            ].reshape(NY, NX, ry, k * part)
        u = ORDER.index(name)
        _, _, rows, lanes = area(name)

        def code(y, carry):
            packed, step = squeeze(gram[kind, r, y, 0, rows, lanes], gram[kind, r, y, 1, rows, lanes])
            yout[kind, r, y, rows, lanes] = packed
            yout_step[u, y] = step
            return carry

        lax.fori_loop(0, NY, code, 0)

    def y_copy(name, d):
        kind, r, rows, lanes = area(name)
        u = ORDER.index(name)
        return (
            remote(
                yout.at[kind, r, y_of(d), rows, lanes],
                yin.at[kind, r, d - 1, rows, lanes],
                y_send.at[u, d - 1, 0],
                y_recv.at[u, d - 1, 0],
                y_peer(d),
            ),
            remote(
                yout_step.at[u, y_of(d)],
                yin_step.at[u, d - 1],
                y_send.at[u, d - 1, 1],
                y_recv.at[u, d - 1, 1],
                y_peer(d),
            ),
        )

    def x_copy(name):
        _, _, _, n, _, k = UNITS[name]
        u = ORDER.index(name)
        piece = (u, pl.ds(0, n * ry), pl.ds(0, k * part // 2))
        return (
            remote(xout.at[piece], xin.at[piece], x_send.at[u, 0], x_recv.at[u, 0], x_peer),
            remote(xout_step.at[u], xin_step.at[u], x_send.at[u, 1], x_recv.at[u, 1], x_peer),
        )

    def g_move(r):
        return remote(done.at[GRAD, r], gin.at[r - 2], g_send.at[r - 2], g_recv.at[r - 2], (up, place))

    def unit(name):
        compute(name)
        for d in range(1, NY):
            for copy in y_copy(name, d):
                copy.start()

    def y_finish(name):
        kind, r, m, n, p, k = UNITS[name]
        _, _, rows, lanes = area(name)
        u = ORDER.index(name)
        high, low = gram[kind, r, my_y, 0, rows, lanes], gram[kind, r, my_y, 1, rows, lanes]
        for d in range(1, NY):
            for copy in y_copy(name, d):
                copy.wait_recv()
            more = unsqueeze(yin[kind, r, d - 1, rows, lanes], yin_step[u, d - 1])
            high, low = high + more[0], low + more[1]
        gram[kind, r, my_y, 0, rows, lanes] = high
        gram[kind, r, my_y, 1, rows, lanes] = low
        go = gram[kind, r, my_y, 1 - my_x, rows, lanes]
        wide = k * part // 2
        packed, step = squeeze(go[:, :wide], go[:, wide:])
        xout[u, : n * ry, :wide] = packed
        xout_step[u] = step
        for copy in x_copy(name):
            copy.start()

    def x_finish(name):
        kind, r, m, n, p, k = UNITS[name]
        _, _, rows, _ = area(name)
        u = ORDER.index(name)
        for copy in x_copy(name):
            copy.wait_recv()
        wide = k * part // 2
        for i, more in enumerate(unsqueeze(xin[u, : n * ry, :wide], xin_step[u])):
            lanes = pl.ds(p * part + i * wide, wide)
            done[kind, r, rows, lanes] = gram[kind, r, my_y, my_x, rows, lanes] + more

    def onehots(r):
        seg_t = (segn if r == 3 else tseg_ref)[...]
        onehot_t = (lax.broadcasted_iota(jnp.int32, (ST, rows_t), 0) == seg_t).astype(F32)
        owner = lax.rem(doc + n_doc - min(r, 2), n_doc)
        seg_q = qseg_ref[pl.ds(owner, 1), :]
        row = lax.broadcasted_iota(jnp.int32, (CHUNKS * ry, rows_q), 0)
        token = lax.broadcasted_iota(jnp.int32, (CHUNKS * ry, rows_q), 1)
        mine = core * half + (row // ry) * chunk + my_y * (NX * ry) + my_x * ry + row % ry
        ids = jnp.sum(jnp.where(token == mine, seg_q, 0), axis=1, keepdims=True)
        lane = lax.broadcasted_iota(jnp.int32, (CHUNKS * ry, LANES), 1)
        return onehot_t, (lane == ids + r * SQ).astype(F32)

    def segment_sum(r, hots):
        onehot_t, onehot_q = hots
        grads = gin[r - 2] if r >= 2 else done[GRAD, r]
        left = lax.dot_general(
            onehot_t,
            done[ACT, r] * grads,
            CONTRACT,
            precision=lax.Precision.HIGHEST,
            preferred_element_type=F32,
        )
        return jnp.dot(left, onehot_q, precision=lax.Precision.HIGHEST, preferred_element_type=F32)

    def arrive_and_hop(m):
        for far in range(2):
            qa_arrival(m, far).wait_recv()
        qa_hop(m).start()

    for j in range(4):
        local(j).start()
    greet = [sibling, x_peer, x_other]
    greet += [(up, spot(my_y, my_x, other)), (down, spot(my_y, my_x, other))]
    greet += [y_peer(d) for d in range(1, NY)]
    greet += [y_peer(d, up) for d in range(NY)]
    greet += [y_peer(d, down) for d in range(NY)]
    barrier = pltpu.get_barrier_semaphore()
    for who in greet:
        pl.semaphore_signal(barrier, inc=1, device_id=who, device_id_type=MESH)
    pl.semaphore_wait(barrier, len(greet))

    for far in range(2):
        qg_up(far).start()
    tg_down(0).start()
    for j in range(4):
        swap_out(j).start()
    for far in range(2):
        qa_up(0, far).start()
    ta_down(0).start()
    for m in range(1, CHUNKS):
        for far in range(2):
            qa_up(m, far).start()
    seg_copy.start()

    for j in range(2):
        local(j).wait()
        swap_in(j).wait_recv()
    unit("g0")
    for j in range(2, 4):
        local(j).wait()
        swap_in(j).wait_recv()
    unit("a0")
    for far in range(2):
        qg_arrival(far).wait_recv()
    unit("g1")
    tg_down(0).wait_recv()
    tg_down(1).start()
    tg_across(0, core).start()
    for p in range(1, TPARTS):
        ta_down(p).start()
    tg_across(0, other).wait_recv()
    unit("g2")
    arrive_and_hop(0)
    y_finish("g0")
    y_finish("a0")
    arrive_and_hop(1)
    unit("a1_01")
    y_finish("g1")
    arrive_and_hop(2)
    ta_down(0).wait_recv()
    ta_across(0, core).start()
    y_finish("g2")
    arrive_and_hop(3)
    unit("a1_23")
    tg_down(1).wait_recv()
    tg_across(1, core).start()
    y_finish("a1_01")
    tg_across(1, other).wait_recv()
    unit("g3")
    qa_hop(0).wait_recv()
    unit("a2_0")
    y_finish("a1_23")
    qa_hop(1).wait_recv()
    unit("a2_1")
    y_finish("g3")
    for name in ("g0", "a0", "g1", "g2"):
        x_finish(name)
    g_move(2).start()
    y_finish("a2_0")
    ta_down(1).wait_recv()
    ta_across(1, core).start()
    for p in range(2):
        ta_across(p, other).wait_recv()
    unit("a3_01")
    y_finish("a2_1")
    for name in ("a1_01", "a1_23", "g3"):
        x_finish(name)
    g_move(3).start()
    base = segment_sum(0, onehots(0)) + segment_sum(1, onehots(1))
    seg_copy.wait_recv()
    hots_2, hots_3 = onehots(2), onehots(3)
    qa_hop(2).wait_recv()
    unit("a2_2")
    unit("a3_2")
    y_finish("a3_01")
    for name in ("a2_0", "a2_1"):
        x_finish(name)
    y_finish("a2_2")
    y_finish("a3_2")
    ta_down(2).wait_recv()
    ta_across(2, core).start()
    qa_hop(3).wait_recv()
    unit("a3_3")
    unit("a2_3")
    ta_across(2, other).wait_recv()
    unit("a3_all")
    for name in ("a3_01", "a2_2", "a3_2"):
        x_finish(name)
    y_finish("a3_3")
    y_finish("a2_3")
    y_finish("a3_all")
    for r in range(2, CYCLE):
        g_move(r).wait_recv()
    x_finish("a2_3")
    fin_y[0, my_y] = base + segment_sum(2, hots_2)
    fy = [
        remote(fin_y.at[0, my_y], fin_y.at[0, my_y], fy_send.at[0, d], fy_recv.at[0, my_y], y_peer(d))
        for d in range(1, NY)
    ]
    for copy in fy:
        copy.start()
    x_finish("a3_3")
    x_finish("a3_all")
    small[...] = segment_sum(3, hots_3)
    fu = [
        remote(small, fin_y.at[1, my_y], fy_send.at[1, d], fy_recv.at[1, my_y], y_peer(d, up))
        for d in range(NY)
    ]
    for copy in fu:
        copy.start()
    for d in range(1, NY):
        y = y_of(d)
        remote(fin_y.at[0, y], fin_y.at[0, y], fy_send.at[0, d], fy_recv.at[0, y], y_peer(d)).wait_recv()
    for d in range(NY):
        y = y_of(d)
        remote(small, fin_y.at[1, y], fy_send.at[1, d], fy_recv.at[1, y], y_peer(d, up)).wait_recv()
    total = fin_y[0, 0] + fin_y[1, 0]
    for y in range(1, NY):
        total = total + (fin_y[0, y] + fin_y[1, y])
    mine = lax.rem(place, NX * NCORE)
    fin_x[mine] = total
    fx = []
    for i, who in enumerate((sibling, x_peer, x_other)):
        fx.append(remote(fin_x.at[mine], fin_x.at[mine], fx_send.at[i], fx_recv.at[mine], who))
        fx[-1].start()
    for i, (x, c) in enumerate(((my_x, other), (1 - my_x, core), (1 - my_x, other))):
        at = x * NCORE + c
        remote(fin_x.at[at], fin_x.at[at], fx_send.at[i], fx_recv.at[at], sibling).wait_recv()
    out_ref[...] = (((fin_x[0] + fin_x[1]) + (fin_x[2] + fin_x[3])) * factor)[:, : CYCLE * SQ]

    seg_copy.wait_send()
    for copy in fy + fu + fx:
        copy.wait_send()
    for j in range(4):
        swap_out(j).wait_send()
    for far in range(2):
        qg_up(far).wait_send()
    for m in range(CHUNKS):
        for far in range(2):
            qa_up(m, far).wait_send()
        qa_hop(m).wait_send()
    for step in range(2):
        tg_down(step).wait_send()
        tg_across(step, core).wait_send()
    for p in range(TPARTS):
        ta_down(p).wait_send()
        ta_across(p, core).wait_send()
    for r in range(2, CYCLE):
        g_move(r).wait_send()
    for name in ORDER:
        for d in range(1, NY):
            for copy in y_copy(name, d):
                copy.wait_send()
        for copy in x_copy(name):
            copy.wait_send()


def on_device(n_doc, train_acts, train_grads, query_acts, query_grads, train_seg, query_seg):
    rows_t, wide_a = train_acts.shape
    rows_q, wide_g = query_grads.shape
    half = rows_q // NCORE
    rows = half // (NY * NX)
    units = len(ORDER)
    dma = pltpu.SemaphoreType.DMA
    anywhere = pl.BlockSpec(memory_space=pl.ANY)
    vmem = pl.BlockSpec(memory_space=pltpu.VMEM)
    bf16 = jnp.bfloat16

    def pair(*shape):
        return [dma(shape), dma(shape)]

    return pl.pallas_call(
        functools.partial(kernel, n_doc),
        out_shape=jax.ShapeDtypeStruct((ST, CYCLE * SQ), F32),
        in_specs=[anywhere] * 4 + [vmem] * 2,
        out_specs=vmem,
        scratch_shapes=[
            pltpu.VMEM((2, rows_t, NCORE * wide_a), bf16),
            pltpu.VMEM((3, rows_t, NCORE * wide_g), bf16),
            pltpu.VMEM((3, half, NCORE * wide_a), bf16),
            pltpu.VMEM((2, half, NCORE * wide_g), bf16),
            pltpu.VMEM((2, CYCLE, NY, NX, rows, rows_t), F32),
            pltpu.VMEM((2, CYCLE, NY, rows, rows_t), I32),
            pltpu.VMEM((units, NY, 8, LANES), F32),
            pltpu.VMEM((2, CYCLE, NY - 1, rows, rows_t), I32),
            pltpu.VMEM((units, NY - 1, 8, LANES), F32),
            pltpu.VMEM((units, rows, rows_t // 2), I32),
            pltpu.VMEM((units, 8, LANES), F32),
            pltpu.VMEM((units, rows, rows_t // 2), I32),
            pltpu.VMEM((units, 8, LANES), F32),
            pltpu.VMEM((2, CYCLE, rows, rows_t), F32),
            pltpu.VMEM((2, rows, rows_t), F32),
            pltpu.VMEM((1, rows_t), jnp.int32),
            pltpu.VMEM((ST, LANES), F32),
            pltpu.VMEM((2, NY, ST, LANES), F32),
            pltpu.VMEM((NX * NCORE, ST, LANES), F32),
            dma((4,)),
            *pair(4),
            *pair(2),
            *pair(CHUNKS, 2),
            *pair(CHUNKS),
            *pair(2),
            *pair(TPARTS),
            *pair(2),
            *pair(TPARTS),
            *pair(units, NY - 1, 2),
            *pair(units, 2),
            *pair(2),
            dma,
            dma,
            *pair(2, NY),
            *pair(NX * NCORE),
        ],
        compiler_params=pltpu.CompilerParams(
            collective_id=0, has_side_effects=True, vmem_limit_bytes=56 * 1024 * 1024
        ),
        name="influence",
    )(train_acts, train_grads, query_acts, query_grads, train_seg, query_seg)


def solution(mesh):
    in_specs = (
        P("doc", "hidden"),
        P("doc", "hidden"),
        P("doc", "hidden"),
        P("doc", "hidden"),
        P("doc", None),
        P(),
    )
    return jax.shard_map(
        functools.partial(on_device, mesh.shape["doc"]),
        mesh=mesh,
        in_specs=in_specs,
        out_specs=P("doc", None),
        check_vma=False,
    )
```

```python
import functools
import math

import jax
import jax.numpy as jnp
from jax import lax
from jax.experimental import pallas as pl
from jax.experimental.pallas import tpu as pltpu
from jax.sharding import PartitionSpec as P

ST = 8
SQ = 8
CYCLE = 4
NY = 4
NX = 2
NCORE = 2
X_HI = 2
CHUNKS = 4
TPARTS = 3
LANES = 128
ACT = 0
GRAD = 1
MESH = pl.DeviceIdType.MESH
CONTRACT = (((1,), (1,)), ((), ()))
F32 = jnp.float32
I32 = jnp.int32
TOP = 32767.0
LEAST = 1e-34

UNITS = {
    "g0": (GRAD, 0, 0, 4, 0, 3),
    "a0": (ACT, 0, 0, 4, 0, 3),
    "g1": (GRAD, 1, 0, 4, 0, 3),
    "g2": (GRAD, 2, 0, 4, 0, 3),
    "g3": (GRAD, 3, 0, 4, 0, 3),
    "a1_01": (ACT, 1, 0, 2, 0, 3),
    "a1_23": (ACT, 1, 2, 2, 0, 3),
    "a2_0": (ACT, 2, 0, 1, 0, 3),
    "a2_1": (ACT, 2, 1, 1, 0, 3),
    "a2_2": (ACT, 2, 2, 1, 0, 3),
    "a2_3": (ACT, 2, 3, 1, 0, 3),
    "a3_01": (ACT, 3, 0, 2, 0, 2),
    "a3_2": (ACT, 3, 2, 1, 0, 2),
    "a3_3": (ACT, 3, 3, 1, 0, 3),
    "a3_last": (ACT, 3, 0, 3, 2, 1),
}
ORDER = list(UNITS)


def spread(tile, rows, lanes):
    wide = jnp.concatenate([tile] * (lanes // LANES), axis=1) if lanes > LANES else tile
    return jnp.concatenate([wide] * (rows // 8), axis=0) if rows > 8 else wide


def highest(value):
    rows, lanes = value.shape
    top = jnp.max(jnp.abs(value).reshape(rows // 8, 8, lanes), axis=0)
    return functools.reduce(
        jnp.maximum, [top[:, b * LANES : (b + 1) * LANES] for b in range(lanes // LANES)]
    )


def squeeze(high, low):
    scale = jnp.maximum(jnp.maximum(highest(high), highest(low)), LEAST)
    times = spread(TOP / scale, *high.shape)
    packed = jnp.round(high * times).astype(I32) * 65536 + jnp.round(low * times).astype(I32)
    return packed, scale * (1.0 / TOP)


def unsqueeze(packed, step):
    high = lax.shift_right_arithmetic(packed + 32768, jnp.full_like(packed, 16))
    low = packed - high * 65536
    step = spread(step, *packed.shape)
    return high.astype(F32) * step, low.astype(F32) * step


def kernel(
    n_doc,
    ta_hbm,
    tg_hbm,
    qa_hbm,
    qg_hbm,
    tseg_ref,
    qseg_ref,
    out_ref,
    ta,
    tg,
    qa,
    qg,
    gram,
    yout,
    yout_step,
    yin,
    yin_step,
    xout,
    xout_step,
    xin,
    xin_step,
    done,
    gout,
    gout_step,
    gin,
    gin_step,
    grads_up,
    segn,
    small,
    fin_y,
    fin_x,
    local_sem,
    own_send,
    own_recv,
    qg_send,
    qg_recv,
    qa_send,
    qa_recv,
    hop_send,
    hop_recv,
    tg_send,
    tg_recv,
    ta_send,
    ta_recv,
    tgf_send,
    tgf_recv,
    taf_send,
    taf_recv,
    y_send,
    y_recv,
    x_send,
    x_recv,
    g_send,
    g_recv,
    s_send,
    s_recv,
    fy_send,
    fy_recv,
    fx_send,
    fx_recv,
):
    rows_t, wide_a = ta_hbm.shape
    rows_q, wide_g = qg_hbm.shape
    half = rows_q // NCORE
    chunk = half // CHUNKS
    part = rows_t // TPARTS
    ry = chunk // (NY * NX)
    factor = math.sqrt(ST * SQ / (rows_t * rows_q))

    doc = lax.axis_index("doc")
    place = lax.axis_index("hidden")
    core = lax.rem(place, NCORE)
    other = 1 - core
    my_x = lax.rem(place // NCORE, NX)
    my_y = place // (NCORE * NX)
    up = lax.rem(doc + 1, n_doc)
    down = lax.rem(doc + n_doc - 1, n_doc)

    def y_of(d):
        return lax.rem(my_y + d, NY)

    def spot(y, x, c):
        return y * (NX * NCORE) + x * NCORE + c

    sibling = (doc, spot(my_y, my_x, other))
    deep = n_doc // X_HI
    wrap = lax.rem(doc, deep) // (deep - 1)
    keep_far = my_x + wrap * (1 - 2 * my_x)

    def keep(kind, r):
        return keep_far if kind == GRAD and r >= 2 else my_x

    x_peer = (doc, spot(my_y, 1 - my_x, core))
    x_other = (doc, spot(my_y, 1 - my_x, other))

    def y_peer(d, of=doc):
        return (of, spot(y_of(d), my_x, core))

    def remote(src, dst, send, recv, who):
        return pltpu.make_async_remote_copy(
            src_ref=src, dst_ref=dst, send_sem=send, recv_sem=recv, device_id=who, device_id_type=MESH
        )

    def cols(wide, whose):
        return pl.ds(pl.multiple_of(whose * wide, LANES), wide)

    def q_half(whose):
        return pl.ds(pl.multiple_of(whose * half, half), half)

    def swap(j, whose_q, whose):
        return (
            (qg_hbm.at[q_half(whose_q), :], qg.at[0, :, cols(wide_g, whose)]),
            (tg_hbm, tg.at[0, :, cols(wide_g, whose)]),
            (qa_hbm.at[q_half(whose_q), :], qa.at[0, :, cols(wide_a, whose)]),
            (ta_hbm, ta.at[0, :, cols(wide_a, whose)]),
        )[j]

    def swap_out(j):
        return remote(*swap(j, other, core), own_send.at[j], own_recv.at[j], sibling)

    def swap_in(j):
        return remote(*swap(j, core, other), own_send.at[j], own_recv.at[j], sibling)

    def local(j):
        return pltpu.make_async_copy(*swap(j, core, core), local_sem.at[j])

    def who_up(far):
        return core if far == 0 else other

    def qg_up(far):
        to = who_up(far)
        return remote(
            qg_hbm.at[q_half(to), :],
            qg.at[1, :, cols(wide_g, core)],
            qg_send.at[far],
            qg_recv.at[far],
            (up, spot(my_y, my_x, to)),
        )

    def qg_arrival(far):
        return remote(
            qg_hbm.at[q_half(core), :],
            qg.at[1, :, cols(wide_g, who_up(far))],
            qg_send.at[far],
            qg_recv.at[far],
            (up, spot(my_y, my_x, who_up(far))),
        )

    def q_chunk(m):
        return pl.ds(m * chunk, chunk)

    def qa_up(m, far):
        to = who_up(far)
        return remote(
            qa_hbm.at[pl.ds(pl.multiple_of(to * half + m * chunk, chunk), chunk), :],
            qa.at[1, q_chunk(m), cols(wide_a, core)],
            qa_send.at[m, far],
            qa_recv.at[m, far],
            (up, spot(my_y, my_x, to)),
        )

    def qa_arrival(m, far):
        return remote(
            qa_hbm.at[pl.ds(pl.multiple_of(core * half + m * chunk, chunk), chunk), :],
            qa.at[1, q_chunk(m), cols(wide_a, who_up(far))],
            qa_send.at[m, far],
            qa_recv.at[m, far],
            (up, spot(my_y, my_x, who_up(far))),
        )

    def qa_hop(m):
        return remote(
            qa.at[1, q_chunk(m), :], qa.at[2, q_chunk(m), :], hop_send.at[m], hop_recv.at[m], (up, place)
        )

    def tg_down(step):
        src = tg_hbm if step == 0 else tg.at[step, :, cols(wide_g, core)]
        return remote(
            src, tg.at[step + 1, :, cols(wide_g, core)], tg_send.at[step], tg_recv.at[step], (down, place)
        )

    def tg_across(step, whose):
        ref = tg.at[step + 1, :, cols(wide_g, whose)]
        return remote(ref, ref, tgf_send.at[step], tgf_recv.at[step], sibling)

    def t_part(p):
        return pl.ds(p * part, part)

    def ta_down(p):
        return remote(
            ta_hbm.at[t_part(p), :],
            ta.at[1, t_part(p), cols(wide_a, core)],
            ta_send.at[p],
            ta_recv.at[p],
            (down, place),
        )

    def ta_across(p, whose):
        ref = ta.at[1, t_part(p), cols(wide_a, whose)]
        return remote(ref, ref, taf_send.at[p], taf_recv.at[p], sibling)

    seg_copy = remote(tseg_ref, segn, s_send, s_recv, (down, place))

    def area(name):
        kind, r, m, n, p, k = UNITS[name]
        return kind, r, pl.ds(m * ry, n * ry), pl.ds(p * part, k * part)

    def compute(name):
        kind, r, m, n, p, k = UNITS[name]
        if kind == ACT:
            query, train = qa.at[min(r, 2)], ta.at[1 if r == 3 else 0]
        else:
            query, train = qg.at[min(r, 1)], tg.at[max(r - 1, 0)]
        left = query[m * chunk : (m + n) * chunk, :]
        right = train[p * part : (p + k) * part, :]
        if n == CHUNKS:
            total = lax.dot_general(left, right, CONTRACT, preferred_element_type=F32)
        else:
            total = lax.dot_general(right, left, CONTRACT, preferred_element_type=F32).T
        for i in range(n):
            gram[kind, r, :, :, (m + i) * ry : (m + i + 1) * ry, p * part : (p + k) * part] = total[
                i * chunk : (i + 1) * chunk
            ].reshape(NY, NX, ry, k * part)
        u = ORDER.index(name)
        _, _, rows, lanes = area(name)

        def code(y, carry):
            packed, step = squeeze(gram[kind, r, y, 0, rows, lanes], gram[kind, r, y, 1, rows, lanes])
            yout[kind, r, y, rows, lanes] = packed
            yout_step[u, y] = step
            return carry

        lax.fori_loop(0, NY, code, 0)

    def y_copy(name, d):
        kind, r, rows, lanes = area(name)
        u = ORDER.index(name)
        return (
            remote(
                yout.at[kind, r, y_of(d), rows, lanes],
                yin.at[kind, r, d - 1, rows, lanes],
                y_send.at[u, d - 1, 0],
                y_recv.at[u, d - 1, 0],
                y_peer(d),
            ),
            remote(
                yout_step.at[u, y_of(d)],
                yin_step.at[u, d - 1],
                y_send.at[u, d - 1, 1],
                y_recv.at[u, d - 1, 1],
                y_peer(d),
            ),
        )

    def x_copy(name):
        _, _, _, n, _, k = UNITS[name]
        u = ORDER.index(name)
        piece = (u, pl.ds(0, n * ry), pl.ds(0, k * part // 2))
        return (
            remote(xout.at[piece], xin.at[piece], x_send.at[u, 0], x_recv.at[u, 0], x_peer),
            remote(xout_step.at[u], xin_step.at[u], x_send.at[u, 1], x_recv.at[u, 1], x_peer),
        )

    def g_move():
        who = (up, spot(my_y, keep_far, core))
        return (
            remote(gout, gin, g_send.at[0], g_recv.at[0], who),
            remote(gout_step, gin_step, g_send.at[1], g_recv.at[1], who),
        )

    def unit(name):
        compute(name)
        for d in range(1, NY):
            for copy in y_copy(name, d):
                copy.start()

    def y_finish(name):
        kind, r, m, n, p, k = UNITS[name]
        _, _, rows, lanes = area(name)
        u = ORDER.index(name)
        high, low = gram[kind, r, my_y, 0, rows, lanes], gram[kind, r, my_y, 1, rows, lanes]
        for d in range(1, NY):
            for copy in y_copy(name, d):
                copy.wait_recv()
            more = unsqueeze(yin[kind, r, d - 1, rows, lanes], yin_step[u, d - 1])
            high, low = high + more[0], low + more[1]
        gram[kind, r, my_y, 0, rows, lanes] = high
        gram[kind, r, my_y, 1, rows, lanes] = low
        go = gram[kind, r, my_y, 1 - keep(kind, r), rows, lanes]
        wide = k * part // 2
        packed, step = squeeze(go[:, :wide], go[:, wide:])
        xout[u, : n * ry, :wide] = packed
        xout_step[u] = step
        for copy in x_copy(name):
            copy.start()

    def x_finish(name):
        kind, r, m, n, p, k = UNITS[name]
        _, _, rows, _ = area(name)
        u = ORDER.index(name)
        for copy in x_copy(name):
            copy.wait_recv()
        wide = k * part // 2
        for i, more in enumerate(unsqueeze(xin[u, : n * ry, :wide], xin_step[u])):
            lanes = pl.ds(p * part + i * wide, wide)
            done[kind, r, rows, lanes] = gram[kind, r, my_y, keep(kind, r), rows, lanes] + more

    def onehots(r):
        seg_t = (segn if r == 3 else tseg_ref)[...]
        onehot_t = (lax.broadcasted_iota(jnp.int32, (ST, rows_t), 0) == seg_t).astype(F32)
        owner = lax.rem(doc + n_doc - min(r, 2), n_doc)
        seg_q = qseg_ref[pl.ds(owner, 1), :]
        row = lax.broadcasted_iota(jnp.int32, (CHUNKS * ry, rows_q), 0)
        token = lax.broadcasted_iota(jnp.int32, (CHUNKS * ry, rows_q), 1)
        mine = core * half + (row // ry) * chunk + my_y * (NX * ry) + my_x * ry + row % ry
        ids = jnp.sum(jnp.where(token == mine, seg_q, 0), axis=1, keepdims=True)
        lane = lax.broadcasted_iota(jnp.int32, (CHUNKS * ry, LANES), 1)
        return onehot_t, (lane == ids + r * SQ).astype(F32)

    def segment_sum(r, hots):
        onehot_t, onehot_q = hots
        grads = grads_up[r - 2] if r >= 2 else done[GRAD, r]
        left = lax.dot_general(
            onehot_t,
            done[ACT, r] * grads,
            CONTRACT,
            precision=lax.Precision.HIGHEST,
            preferred_element_type=F32,
        )
        return jnp.dot(left, onehot_q, precision=lax.Precision.HIGHEST, preferred_element_type=F32)

    def arrive_and_hop(m):
        for far in range(2):
            qa_arrival(m, far).wait_recv()
        qa_hop(m).start()

    for j in range(4):
        local(j).start()
    greet = [sibling, x_peer, x_other]
    greet += [(up, spot(my_y, my_x, other)), (down, spot(my_y, my_x, other))]
    greet += [(up, spot(my_y, 1 - my_x, core)), (down, spot(my_y, 1 - my_x, core))]
    greet += [y_peer(d) for d in range(1, NY)]
    greet += [y_peer(d, up) for d in range(NY)]
    greet += [y_peer(d, down) for d in range(NY)]
    barrier = pltpu.get_barrier_semaphore()
    for who in greet:
        pl.semaphore_signal(barrier, inc=1, device_id=who, device_id_type=MESH)
    pl.semaphore_wait(barrier, len(greet))

    for far in range(2):
        qg_up(far).start()
    tg_down(0).start()
    for j in range(4):
        swap_out(j).start()
    for far in range(2):
        qa_up(0, far).start()
    ta_down(0).start()
    for m in range(1, CHUNKS):
        for far in range(2):
            qa_up(m, far).start()
    seg_copy.start()

    for j in range(2):
        local(j).wait()
        swap_in(j).wait_recv()
    unit("g0")
    for j in range(2, 4):
        local(j).wait()
        swap_in(j).wait_recv()
    unit("a0")
    for far in range(2):
        qg_arrival(far).wait_recv()
    unit("g1")
    tg_down(0).wait_recv()
    tg_down(1).start()
    tg_across(0, core).start()
    for p in range(1, TPARTS):
        ta_down(p).start()
    tg_across(0, other).wait_recv()
    unit("g2")
    arrive_and_hop(0)
    y_finish("g0")
    y_finish("a0")
    arrive_and_hop(1)
    unit("a1_01")
    y_finish("g1")
    arrive_and_hop(2)
    ta_down(0).wait_recv()
    ta_across(0, core).start()
    y_finish("g2")
    arrive_and_hop(3)
    unit("a1_23")
    tg_down(1).wait_recv()
    tg_across(1, core).start()
    y_finish("a1_01")
    tg_across(1, other).wait_recv()
    unit("g3")
    qa_hop(0).wait_recv()
    unit("a2_0")
    y_finish("a1_23")
    qa_hop(1).wait_recv()
    unit("a2_1")
    y_finish("g3")
    y_finish("a2_0")
    ta_down(1).wait_recv()
    ta_across(1, core).start()
    for p in range(2):
        ta_across(p, other).wait_recv()
    unit("a3_01")
    y_finish("a2_1")
    seg_copy.wait_recv()
    hots_2, hots_3 = onehots(2), onehots(3)
    qa_hop(2).wait_recv()
    unit("a2_2")
    unit("a3_2")
    y_finish("a3_01")
    y_finish("a2_2")
    y_finish("a3_2")
    ta_down(2).wait_recv()
    ta_across(2, core).start()
    for name in ("g2", "g3"):
        x_finish(name)
    gout[...], gout_step[...] = squeeze(done[GRAD, 2], done[GRAD, 3])
    for copy in g_move():
        copy.start()
    ta_across(2, other).wait_recv()
    unit("a3_last")
    qa_hop(3).wait_recv()
    unit("a3_3")
    unit("a2_3")
    for name in ("g0", "a0", "g1", "a1_01", "a1_23"):
        x_finish(name)
    base = segment_sum(0, onehots(0)) + segment_sum(1, onehots(1))
    for name in ("a2_0", "a2_1", "a3_01", "a2_2", "a3_2"):
        x_finish(name)
    y_finish("a3_last")
    y_finish("a3_3")
    y_finish("a2_3")
    for copy in g_move():
        copy.wait_recv()
    grads_up[0], grads_up[1] = unsqueeze(gin[...], gin_step[...])
    x_finish("a3_last")
    x_finish("a3_3")
    small[...] = segment_sum(3, hots_3)
    fu = [
        remote(small, fin_y.at[1, my_y], fy_send.at[1, d], fy_recv.at[1, my_y], y_peer(d, up))
        for d in range(NY)
    ]
    for copy in fu:
        copy.start()
    x_finish("a2_3")
    fin_y[0, my_y] = base + segment_sum(2, hots_2)
    fy = [
        remote(fin_y.at[0, my_y], fin_y.at[0, my_y], fy_send.at[0, d], fy_recv.at[0, my_y], y_peer(d))
        for d in range(1, NY)
    ]
    for copy in fy:
        copy.start()
    for d in range(1, NY):
        y = y_of(d)
        remote(fin_y.at[0, y], fin_y.at[0, y], fy_send.at[0, d], fy_recv.at[0, y], y_peer(d)).wait_recv()
    for d in range(NY):
        y = y_of(d)
        remote(small, fin_y.at[1, y], fy_send.at[1, d], fy_recv.at[1, y], y_peer(d, up)).wait_recv()
    total = fin_y[0, 0] + fin_y[1, 0]
    for y in range(1, NY):
        total = total + (fin_y[0, y] + fin_y[1, y])
    mine = lax.rem(place, NX * NCORE)
    fin_x[mine] = total
    fx = []
    for i, who in enumerate((sibling, x_peer, x_other)):
        fx.append(remote(fin_x.at[mine], fin_x.at[mine], fx_send.at[i], fx_recv.at[mine], who))
        fx[-1].start()
    for i, (x, c) in enumerate(((my_x, other), (1 - my_x, core), (1 - my_x, other))):
        at = x * NCORE + c
        remote(fin_x.at[at], fin_x.at[at], fx_send.at[i], fx_recv.at[at], sibling).wait_recv()
    out_ref[...] = (((fin_x[0] + fin_x[1]) + (fin_x[2] + fin_x[3])) * factor)[:, : CYCLE * SQ]

    seg_copy.wait_send()
    for copy in fy + fu + fx:
        copy.wait_send()
    for j in range(4):
        swap_out(j).wait_send()
    for far in range(2):
        qg_up(far).wait_send()
    for m in range(CHUNKS):
        for far in range(2):
            qa_up(m, far).wait_send()
        qa_hop(m).wait_send()
    for step in range(2):
        tg_down(step).wait_send()
        tg_across(step, core).wait_send()
    for p in range(TPARTS):
        ta_down(p).wait_send()
        ta_across(p, core).wait_send()
    for copy in g_move():
        copy.wait_send()
    for name in ORDER:
        for d in range(1, NY):
            for copy in y_copy(name, d):
                copy.wait_send()
        for copy in x_copy(name):
            copy.wait_send()


def on_device(n_doc, train_acts, train_grads, query_acts, query_grads, train_seg, query_seg):
    rows_t, wide_a = train_acts.shape
    rows_q, wide_g = query_grads.shape
    half = rows_q // NCORE
    rows = half // (NY * NX)
    units = len(ORDER)
    dma = pltpu.SemaphoreType.DMA
    anywhere = pl.BlockSpec(memory_space=pl.ANY)
    vmem = pl.BlockSpec(memory_space=pltpu.VMEM)
    bf16 = jnp.bfloat16

    def pair(*shape):
        return [dma(shape), dma(shape)]

    return pl.pallas_call(
        functools.partial(kernel, n_doc),
        out_shape=jax.ShapeDtypeStruct((ST, CYCLE * SQ), F32),
        in_specs=[anywhere] * 4 + [vmem] * 2,
        out_specs=vmem,
        scratch_shapes=[
            pltpu.VMEM((2, rows_t, NCORE * wide_a), bf16),
            pltpu.VMEM((3, rows_t, NCORE * wide_g), bf16),
            pltpu.VMEM((3, half, NCORE * wide_a), bf16),
            pltpu.VMEM((2, half, NCORE * wide_g), bf16),
            pltpu.VMEM((2, CYCLE, NY, NX, rows, rows_t), F32),
            pltpu.VMEM((2, CYCLE, NY, rows, rows_t), I32),
            pltpu.VMEM((units, NY, 8, LANES), F32),
            pltpu.VMEM((2, CYCLE, NY - 1, rows, rows_t), I32),
            pltpu.VMEM((units, NY - 1, 8, LANES), F32),
            pltpu.VMEM((units, rows, rows_t // 2), I32),
            pltpu.VMEM((units, 8, LANES), F32),
            pltpu.VMEM((units, rows, rows_t // 2), I32),
            pltpu.VMEM((units, 8, LANES), F32),
            pltpu.VMEM((2, CYCLE, rows, rows_t), F32),
            pltpu.VMEM((rows, rows_t), I32),
            pltpu.VMEM((8, LANES), F32),
            pltpu.VMEM((rows, rows_t), I32),
            pltpu.VMEM((8, LANES), F32),
            pltpu.VMEM((2, rows, rows_t), F32),
            pltpu.VMEM((1, rows_t), I32),
            pltpu.VMEM((ST, LANES), F32),
            pltpu.VMEM((2, NY, ST, LANES), F32),
            pltpu.VMEM((NX * NCORE, ST, LANES), F32),
            dma((4,)),
            *pair(4),
            *pair(2),
            *pair(CHUNKS, 2),
            *pair(CHUNKS),
            *pair(2),
            *pair(TPARTS),
            *pair(2),
            *pair(TPARTS),
            *pair(units, NY - 1, 2),
            *pair(units, 2),
            *pair(2),
            dma,
            dma,
            *pair(2, NY),
            *pair(NX * NCORE),
        ],
        compiler_params=pltpu.CompilerParams(
            collective_id=0, has_side_effects=True, vmem_limit_bytes=56 * 1024 * 1024
        ),
        name="influence",
    )(train_acts, train_grads, query_acts, query_grads, train_seg, query_seg)


def solution(mesh):
    in_specs = (
        P("doc", "hidden"),
        P("doc", "hidden"),
        P("doc", "hidden"),
        P("doc", "hidden"),
        P("doc", None),
        P(),
    )
    return jax.shard_map(
        functools.partial(on_device, mesh.shape["doc"]),
        mesh=mesh,
        in_specs=in_specs,
        out_specs=P("doc", None),
        check_vma=False,
    )
```

```python
import functools
import math

import jax
import jax.numpy as jnp
from jax import lax
from jax.experimental import pallas as pl
from jax.experimental.pallas import tpu as pltpu
from jax.sharding import PartitionSpec as P

ST = 8
SQ = 8
CYCLE = 4
NY = 4
NX = 2
NCORE = 2
X_HI = 2
CHUNKS = 4
TPARTS = 3
LANES = 128
ACT = 0
GRAD = 1
MESH = pl.DeviceIdType.MESH
CONTRACT = (((1,), (1,)), ((), ()))
F32 = jnp.float32
I32 = jnp.int32
TOP = 32767.0
LEAST = 1e-34

UNITS = {
    "g0": (GRAD, 0, 0, 4, 0, 3),
    "a0": (ACT, 0, 0, 4, 0, 3),
    "g1": (GRAD, 1, 0, 4, 0, 3),
    "g2": (GRAD, 2, 0, 4, 0, 3),
    "g3": (GRAD, 3, 0, 4, 0, 3),
    "a1_01": (ACT, 1, 0, 2, 0, 3),
    "a1_23": (ACT, 1, 2, 2, 0, 3),
    "a2_0": (ACT, 2, 0, 1, 0, 3),
    "a2_1": (ACT, 2, 1, 1, 0, 3),
    "a2_2": (ACT, 2, 2, 1, 0, 3),
    "a2_3": (ACT, 2, 3, 1, 0, 3),
    "a3_01": (ACT, 3, 0, 2, 0, 2),
    "a3_2": (ACT, 3, 2, 1, 0, 2),
    "a3_3": (ACT, 3, 3, 1, 0, 3),
    "a3_last": (ACT, 3, 0, 3, 2, 1),
}
ORDER = list(UNITS)
HELD = ("g0", "a0", "g1", "a1_01", "a1_23")


def spread(tile, rows, lanes):
    wide = jnp.concatenate([tile] * (lanes // LANES), axis=1) if lanes > LANES else tile
    return jnp.concatenate([wide] * (rows // 8), axis=0) if rows > 8 else wide


def highest(value):
    rows, lanes = value.shape
    top = jnp.max(jnp.abs(value).reshape(rows // 8, 8, lanes), axis=0)
    return functools.reduce(
        jnp.maximum, [top[:, b * LANES : (b + 1) * LANES] for b in range(lanes // LANES)]
    )


def squeeze(high, low):
    scale = jnp.maximum(jnp.maximum(highest(high), highest(low)), LEAST)
    times = spread(TOP / scale, *high.shape)
    packed = jnp.round(high * times).astype(I32) * 65536 + jnp.round(low * times).astype(I32)
    return packed, scale * (1.0 / TOP)


def unsqueeze(packed, step):
    high = lax.shift_right_arithmetic(packed + 32768, jnp.full_like(packed, 16))
    low = packed - high * 65536
    step = spread(step, *packed.shape)
    return high.astype(F32) * step, low.astype(F32) * step


def thirds(value, axis):
    parts = []
    for _ in range(3):
        parts.append(value.astype(jnp.bfloat16))
        value = value - parts[-1].astype(F32)
    return jnp.concatenate(parts, axis=axis)


def kernel(
    n_doc,
    ta_hbm,
    tg_hbm,
    qa_hbm,
    qg_hbm,
    tseg_ref,
    qseg_ref,
    out_ref,
    ta,
    tg,
    qa,
    qg,
    gram,
    yout,
    yout_step,
    yin,
    yin_step,
    xout,
    xout_step,
    xin,
    xin_step,
    done,
    gout,
    gout_step,
    gin,
    gin_step,
    grads_up,
    segn,
    small,
    fin_y,
    fin_x,
    early_sum,
    local_sem,
    own_send,
    own_recv,
    qg_send,
    qg_recv,
    qa_send,
    qa_recv,
    hop_send,
    hop_recv,
    tg_send,
    tg_recv,
    ta_send,
    ta_recv,
    tgf_send,
    tgf_recv,
    taf_send,
    taf_recv,
    y_send,
    y_recv,
    x_send,
    x_recv,
    g_send,
    g_recv,
    s_send,
    s_recv,
    fy_send,
    fy_recv,
    fx_send,
    fx_recv,
):
    rows_t, wide_a = ta_hbm.shape
    rows_q, wide_g = qg_hbm.shape
    half = rows_q // NCORE
    chunk = half // CHUNKS
    part = rows_t // TPARTS
    ry = chunk // (NY * NX)
    factor = math.sqrt(ST * SQ / (rows_t * rows_q))

    doc = lax.axis_index("doc")
    place = lax.axis_index("hidden")
    core = lax.rem(place, NCORE)
    other = 1 - core
    my_x = lax.rem(place // NCORE, NX)
    my_y = place // (NCORE * NX)
    up = lax.rem(doc + 1, n_doc)
    down = lax.rem(doc + n_doc - 1, n_doc)

    def y_of(d):
        return lax.rem(my_y + d, NY)

    def spot(y, x, c):
        return y * (NX * NCORE) + x * NCORE + c

    sibling = (doc, spot(my_y, my_x, other))
    deep = n_doc // X_HI
    wrap = lax.rem(doc, deep) // (deep - 1)
    keep_far = my_x + wrap * (1 - 2 * my_x)

    def keep(kind, r):
        return keep_far if kind == GRAD and r >= 2 else my_x

    x_peer = (doc, spot(my_y, 1 - my_x, core))
    x_other = (doc, spot(my_y, 1 - my_x, other))

    def y_peer(d, of=doc):
        return (of, spot(y_of(d), my_x, core))

    def remote(src, dst, send, recv, who):
        return pltpu.make_async_remote_copy(
            src_ref=src, dst_ref=dst, send_sem=send, recv_sem=recv, device_id=who, device_id_type=MESH
        )

    def cols(wide, whose):
        return pl.ds(pl.multiple_of(whose * wide, LANES), wide)

    def q_half(whose):
        return pl.ds(pl.multiple_of(whose * half, half), half)

    def swap(j, whose_q, whose):
        return (
            (qg_hbm.at[q_half(whose_q), :], qg.at[0, :, cols(wide_g, whose)]),
            (tg_hbm, tg.at[0, :, cols(wide_g, whose)]),
            (qa_hbm.at[q_half(whose_q), :], qa.at[0, :, cols(wide_a, whose)]),
            (ta_hbm, ta.at[0, :, cols(wide_a, whose)]),
        )[j]

    def swap_out(j):
        return remote(*swap(j, other, core), own_send.at[j], own_recv.at[j], sibling)

    def swap_in(j):
        return remote(*swap(j, core, other), own_send.at[j], own_recv.at[j], sibling)

    def local(j):
        return pltpu.make_async_copy(*swap(j, core, core), local_sem.at[j])

    def who_up(far):
        return core if far == 0 else other

    def qg_up(far):
        to = who_up(far)
        return remote(
            qg_hbm.at[q_half(to), :],
            qg.at[1, :, cols(wide_g, core)],
            qg_send.at[far],
            qg_recv.at[far],
            (up, spot(my_y, my_x, to)),
        )

    def qg_arrival(far):
        return remote(
            qg_hbm.at[q_half(core), :],
            qg.at[1, :, cols(wide_g, who_up(far))],
            qg_send.at[far],
            qg_recv.at[far],
            (up, spot(my_y, my_x, who_up(far))),
        )

    def q_chunk(m):
        return pl.ds(m * chunk, chunk)

    def qa_up(m, far):
        to = who_up(far)
        return remote(
            qa_hbm.at[pl.ds(pl.multiple_of(to * half + m * chunk, chunk), chunk), :],
            qa.at[1, q_chunk(m), cols(wide_a, core)],
            qa_send.at[m, far],
            qa_recv.at[m, far],
            (up, spot(my_y, my_x, to)),
        )

    def qa_arrival(m, far):
        return remote(
            qa_hbm.at[pl.ds(pl.multiple_of(core * half + m * chunk, chunk), chunk), :],
            qa.at[1, q_chunk(m), cols(wide_a, who_up(far))],
            qa_send.at[m, far],
            qa_recv.at[m, far],
            (up, spot(my_y, my_x, who_up(far))),
        )

    def qa_hop(m, far):
        at = cols(wide_a, who_up(far))
        return remote(
            qa.at[1, q_chunk(m), at],
            qa.at[2, q_chunk(m), at],
            hop_send.at[m, far],
            hop_recv.at[m, far],
            (up, place),
        )

    def hop_arrival(m):
        for far in range(2):
            qa_hop(m, far).wait_recv()

    def tg_down(step):
        src = tg_hbm if step == 0 else tg.at[step, :, cols(wide_g, core)]
        return remote(
            src, tg.at[step + 1, :, cols(wide_g, core)], tg_send.at[step], tg_recv.at[step], (down, place)
        )

    def tg_across(step, whose):
        ref = tg.at[step + 1, :, cols(wide_g, whose)]
        return remote(ref, ref, tgf_send.at[step], tgf_recv.at[step], sibling)

    def t_part(p):
        return pl.ds(p * part, part)

    def ta_down(p):
        return remote(
            ta_hbm.at[t_part(p), :],
            ta.at[1, t_part(p), cols(wide_a, core)],
            ta_send.at[p],
            ta_recv.at[p],
            (down, place),
        )

    def ta_across(p, whose):
        ref = ta.at[1, t_part(p), cols(wide_a, whose)]
        return remote(ref, ref, taf_send.at[p], taf_recv.at[p], sibling)

    seg_copy = remote(tseg_ref, segn, s_send, s_recv, (down, place))

    def area(name):
        kind, r, m, n, p, k = UNITS[name]
        return kind, r, pl.ds(m * ry, n * ry), pl.ds(p * part, k * part)

    early = []

    def half_compute(name):
        _, r, m, n, _, _ = UNITS[name]
        at = cols(wide_a, core)
        early_sum[len(early)] = lax.dot_general(
            ta[1 if r == 3 else 0, :, at],
            qa[2, m * chunk : (m + n) * chunk, at],
            CONTRACT,
            preferred_element_type=F32,
        )
        early.append(name)

    def compute(name):
        kind, r, m, n, p, k = UNITS[name]
        if kind == ACT:
            query, train = qa.at[min(r, 2)], ta.at[1 if r == 3 else 0]
        else:
            query, train = qg.at[min(r, 1)], tg.at[max(r - 1, 0)]
        left = query[m * chunk : (m + n) * chunk, :]
        right = train[p * part : (p + k) * part, :]
        if name in early:
            at = cols(wide_a, other)
            late = lax.dot_general(
                ta[1 if r == 3 else 0, :, at],
                qa[2, m * chunk : (m + n) * chunk, at],
                CONTRACT,
                preferred_element_type=F32,
            )
            total = (early_sum[early.index(name)] + late).T
        elif n == CHUNKS:
            total = lax.dot_general(left, right, CONTRACT, preferred_element_type=F32)
        else:
            total = lax.dot_general(right, left, CONTRACT, preferred_element_type=F32).T
        for i in range(n):
            gram[kind, r, :, :, (m + i) * ry : (m + i + 1) * ry, p * part : (p + k) * part] = total[
                i * chunk : (i + 1) * chunk
            ].reshape(NY, NX, ry, k * part)
        u = ORDER.index(name)
        _, _, rows, lanes = area(name)

        def code(y, carry):
            packed, step = squeeze(gram[kind, r, y, 0, rows, lanes], gram[kind, r, y, 1, rows, lanes])
            yout[kind, r, y, rows, lanes] = packed
            yout_step[u, y] = step
            return carry

        lax.fori_loop(0, NY, code, 0)

    def y_copy(name, d):
        kind, r, rows, lanes = area(name)
        u = ORDER.index(name)
        return (
            remote(
                yout.at[kind, r, y_of(d), rows, lanes],
                yin.at[kind, r, d - 1, rows, lanes],
                y_send.at[u, d - 1, 0],
                y_recv.at[u, d - 1, 0],
                y_peer(d),
            ),
            remote(
                yout_step.at[u, y_of(d)],
                yin_step.at[u, d - 1],
                y_send.at[u, d - 1, 1],
                y_recv.at[u, d - 1, 1],
                y_peer(d),
            ),
        )

    def x_copy(name):
        _, _, _, n, _, k = UNITS[name]
        u = ORDER.index(name)
        piece = (u, pl.ds(0, n * ry), pl.ds(0, k * part // 2))
        return (
            remote(xout.at[piece], xin.at[piece], x_send.at[u, 0], x_recv.at[u, 0], x_peer),
            remote(xout_step.at[u], xin_step.at[u], x_send.at[u, 1], x_recv.at[u, 1], x_peer),
        )

    def g_move():
        who = (up, spot(my_y, keep_far, core))
        return (
            remote(gout, gin, g_send.at[0], g_recv.at[0], who),
            remote(gout_step, gin_step, g_send.at[1], g_recv.at[1], who),
        )

    def unit(name):
        compute(name)
        for d in range(1, NY):
            for copy in y_copy(name, d):
                copy.start()

    def x_start(name):
        for copy in x_copy(name):
            copy.start()

    def y_finish(name):
        kind, r, m, n, p, k = UNITS[name]
        _, _, rows, lanes = area(name)
        u = ORDER.index(name)
        high, low = gram[kind, r, my_y, 0, rows, lanes], gram[kind, r, my_y, 1, rows, lanes]
        for d in range(1, NY):
            for copy in y_copy(name, d):
                copy.wait_recv()
            more = unsqueeze(yin[kind, r, d - 1, rows, lanes], yin_step[u, d - 1])
            high, low = high + more[0], low + more[1]
        gram[kind, r, my_y, 0, rows, lanes] = high
        gram[kind, r, my_y, 1, rows, lanes] = low
        go = gram[kind, r, my_y, 1 - keep(kind, r), rows, lanes]
        wide = k * part // 2
        packed, step = squeeze(go[:, :wide], go[:, wide:])
        xout[u, : n * ry, :wide] = packed
        xout_step[u] = step
        if name not in HELD:
            x_start(name)

    def x_finish(name):
        kind, r, m, n, p, k = UNITS[name]
        _, _, rows, _ = area(name)
        u = ORDER.index(name)
        for copy in x_copy(name):
            copy.wait_recv()
        wide = k * part // 2
        for i, more in enumerate(unsqueeze(xin[u, : n * ry, :wide], xin_step[u])):
            lanes = pl.ds(p * part + i * wide, wide)
            done[kind, r, rows, lanes] = gram[kind, r, my_y, keep(kind, r), rows, lanes] + more

    def onehots(r):
        seg_t = (segn if r == 3 else tseg_ref)[...]
        onehot_t = (lax.broadcasted_iota(jnp.int32, (ST, rows_t), 0) == seg_t).astype(jnp.bfloat16)
        owner = lax.rem(doc + n_doc - min(r, 2), n_doc)
        seg_q = qseg_ref[pl.ds(owner, 1), :]
        row = lax.broadcasted_iota(jnp.int32, (CHUNKS * ry, rows_q), 0)
        token = lax.broadcasted_iota(jnp.int32, (CHUNKS * ry, rows_q), 1)
        mine = core * half + (row // ry) * chunk + my_y * (NX * ry) + my_x * ry + row % ry
        ids = jnp.sum(jnp.where(token == mine, seg_q, 0), axis=1, keepdims=True)
        lane = lax.broadcasted_iota(jnp.int32, (CHUNKS * ry, LANES), 1)
        onehot_q = (lane == ids + r * SQ).astype(jnp.bfloat16)
        return onehot_t, jnp.concatenate([onehot_q] * 3, axis=0)

    def segment_sum(r, hots):
        onehot_t, onehot_q = hots
        grads = grads_up[r - 2] if r >= 2 else done[GRAD, r]
        parts = thirds(done[ACT, r] * grads, 0)
        left = lax.dot_general(onehot_t, parts, CONTRACT, preferred_element_type=F32)
        total = jnp.dot(thirds(left, 0), onehot_q, preferred_element_type=F32)
        return (total[:ST] + total[ST : 2 * ST]) + total[2 * ST :]

    def arrive_and_hop(m):
        for far in range(2):
            qa_arrival(m, far).wait_recv()
            qa_hop(m, far).start()

    for j in range(4):
        local(j).start()
    greet = [sibling, x_peer, x_other]
    greet += [(up, spot(my_y, my_x, other)), (down, spot(my_y, my_x, other))]
    greet += [(up, spot(my_y, 1 - my_x, core)), (down, spot(my_y, 1 - my_x, core))]
    greet += [y_peer(d) for d in range(1, NY)]
    greet += [y_peer(d, up) for d in range(NY)]
    greet += [y_peer(d, down) for d in range(NY)]
    barrier = pltpu.get_barrier_semaphore()
    for who in greet:
        pl.semaphore_signal(barrier, inc=1, device_id=who, device_id_type=MESH)
    pl.semaphore_wait(barrier, len(greet))

    for far in range(2):
        qg_up(far).start()
    tg_down(0).start()
    for j in range(4):
        swap_out(j).start()
    for far in range(2):
        qa_up(0, far).start()
    ta_down(0).start()
    for m in range(1, CHUNKS):
        for far in range(2):
            qa_up(m, far).start()
    seg_copy.start()

    for j in range(2):
        local(j).wait()
        swap_in(j).wait_recv()
    unit("g0")
    for j in range(2, 4):
        local(j).wait()
        swap_in(j).wait_recv()
    unit("a0")
    for far in range(2):
        qg_arrival(far).wait_recv()
    unit("g1")
    tg_down(0).wait_recv()
    tg_down(1).start()
    tg_across(0, core).start()
    for p in range(1, TPARTS):
        ta_down(p).start()
    tg_across(0, other).wait_recv()
    unit("g2")
    arrive_and_hop(0)
    y_finish("g0")
    y_finish("a0")
    arrive_and_hop(1)
    unit("a1_01")
    y_finish("g1")
    arrive_and_hop(2)
    ta_down(0).wait_recv()
    ta_across(0, core).start()
    y_finish("g2")
    arrive_and_hop(3)
    unit("a1_23")
    tg_down(1).wait_recv()
    tg_across(1, core).start()
    y_finish("a1_01")
    tg_across(1, other).wait_recv()
    unit("g3")
    hop_arrival(0)
    unit("a2_0")
    y_finish("a1_23")
    hop_arrival(1)
    unit("a2_1")
    y_finish("g3")
    y_finish("a2_0")
    ta_down(1).wait_recv()
    ta_across(1, core).start()
    for p in range(2):
        ta_across(p, other).wait_recv()
    unit("a3_01")
    y_finish("a2_1")
    seg_copy.wait_recv()
    hots_0, hots_1, hots_2, hots_3 = onehots(0), onehots(1), onehots(2), onehots(3)
    hop_arrival(2)
    unit("a2_2")
    unit("a3_2")
    y_finish("a3_01")
    y_finish("a2_2")
    y_finish("a3_2")
    ta_down(2).wait_recv()
    ta_across(2, core).start()
    for name in ("g2", "g3"):
        x_finish(name)
    gout[...], gout_step[...] = squeeze(done[GRAD, 2], done[GRAD, 3])
    for copy in g_move():
        copy.start()
    ta_across(2, other).wait_recv()
    unit("a3_last")
    qa_hop(3, 0).wait_recv()
    for name in ("a3_3", "a2_3"):
        half_compute(name)
    qa_hop(3, 1).wait_recv()
    for name in HELD:
        x_start(name)
    unit("a3_3")
    unit("a2_3")
    for name in ("a2_0", "a2_1", "a3_01", "a2_2", "a3_2"):
        x_finish(name)
    y_finish("a3_last")
    y_finish("a3_3")
    y_finish("a2_3")
    for name in HELD:
        x_finish(name)
    base = segment_sum(0, hots_0) + segment_sum(1, hots_1)
    for copy in g_move():
        copy.wait_recv()
    grads_up[0], grads_up[1] = unsqueeze(gin[...], gin_step[...])
    x_finish("a3_last")
    x_finish("a3_3")
    small[...] = segment_sum(3, hots_3)
    fu = [
        remote(small, fin_y.at[1, my_y], fy_send.at[1, d], fy_recv.at[1, my_y], y_peer(d, up))
        for d in range(NY)
    ]
    for copy in fu:
        copy.start()
    x_finish("a2_3")
    fin_y[0, my_y] = base + segment_sum(2, hots_2)
    fy = [
        remote(fin_y.at[0, my_y], fin_y.at[0, my_y], fy_send.at[0, d], fy_recv.at[0, my_y], y_peer(d))
        for d in range(1, NY)
    ]
    for copy in fy:
        copy.start()
    for d in range(1, NY):
        y = y_of(d)
        remote(fin_y.at[0, y], fin_y.at[0, y], fy_send.at[0, d], fy_recv.at[0, y], y_peer(d)).wait_recv()
    for d in range(NY):
        y = y_of(d)
        remote(small, fin_y.at[1, y], fy_send.at[1, d], fy_recv.at[1, y], y_peer(d, up)).wait_recv()
    total = fin_y[0, 0] + fin_y[1, 0]
    for y in range(1, NY):
        total = total + (fin_y[0, y] + fin_y[1, y])
    mine = lax.rem(place, NX * NCORE)
    fin_x[mine] = total
    fx = []
    for i, who in enumerate((sibling, x_peer, x_other)):
        fx.append(remote(fin_x.at[mine], fin_x.at[mine], fx_send.at[i], fx_recv.at[mine], who))
        fx[-1].start()
    for i, (x, c) in enumerate(((my_x, other), (1 - my_x, core), (1 - my_x, other))):
        at = x * NCORE + c
        remote(fin_x.at[at], fin_x.at[at], fx_send.at[i], fx_recv.at[at], sibling).wait_recv()
    out_ref[...] = (((fin_x[0] + fin_x[1]) + (fin_x[2] + fin_x[3])) * factor)[:, : CYCLE * SQ]

    seg_copy.wait_send()
    for copy in fy + fu + fx:
        copy.wait_send()
    for j in range(4):
        swap_out(j).wait_send()
    for far in range(2):
        qg_up(far).wait_send()
    for m in range(CHUNKS):
        for far in range(2):
            qa_up(m, far).wait_send()
            qa_hop(m, far).wait_send()
    for step in range(2):
        tg_down(step).wait_send()
        tg_across(step, core).wait_send()
    for p in range(TPARTS):
        ta_down(p).wait_send()
        ta_across(p, core).wait_send()
    for copy in g_move():
        copy.wait_send()
    for name in ORDER:
        for d in range(1, NY):
            for copy in y_copy(name, d):
                copy.wait_send()
        for copy in x_copy(name):
            copy.wait_send()


def on_device(n_doc, train_acts, train_grads, query_acts, query_grads, train_seg, query_seg):
    rows_t, wide_a = train_acts.shape
    rows_q, wide_g = query_grads.shape
    half = rows_q // NCORE
    rows = half // (NY * NX)
    units = len(ORDER)
    dma = pltpu.SemaphoreType.DMA
    anywhere = pl.BlockSpec(memory_space=pl.ANY)
    vmem = pl.BlockSpec(memory_space=pltpu.VMEM)
    bf16 = jnp.bfloat16

    def pair(*shape):
        return [dma(shape), dma(shape)]

    return pl.pallas_call(
        functools.partial(kernel, n_doc),
        out_shape=jax.ShapeDtypeStruct((ST, CYCLE * SQ), F32),
        in_specs=[anywhere] * 4 + [vmem] * 2,
        out_specs=vmem,
        scratch_shapes=[
            pltpu.VMEM((2, rows_t, NCORE * wide_a), bf16),
            pltpu.VMEM((3, rows_t, NCORE * wide_g), bf16),
            pltpu.VMEM((3, half, NCORE * wide_a), bf16),
            pltpu.VMEM((2, half, NCORE * wide_g), bf16),
            pltpu.VMEM((2, CYCLE, NY, NX, rows, rows_t), F32),
            pltpu.VMEM((2, CYCLE, NY, rows, rows_t), I32),
            pltpu.VMEM((units, NY, 8, LANES), F32),
            pltpu.VMEM((2, CYCLE, NY - 1, rows, rows_t), I32),
            pltpu.VMEM((units, NY - 1, 8, LANES), F32),
            pltpu.VMEM((units, rows, rows_t // 2), I32),
            pltpu.VMEM((units, 8, LANES), F32),
            pltpu.VMEM((units, rows, rows_t // 2), I32),
            pltpu.VMEM((units, 8, LANES), F32),
            pltpu.VMEM((2, CYCLE, rows, rows_t), F32),
            pltpu.VMEM((rows, rows_t), I32),
            pltpu.VMEM((8, LANES), F32),
            pltpu.VMEM((rows, rows_t), I32),
            pltpu.VMEM((8, LANES), F32),
            pltpu.VMEM((2, rows, rows_t), F32),
            pltpu.VMEM((1, rows_t), I32),
            pltpu.VMEM((ST, LANES), F32),
            pltpu.VMEM((2, NY, ST, LANES), F32),
            pltpu.VMEM((NX * NCORE, ST, LANES), F32),
            pltpu.VMEM((2, rows_t, half // CHUNKS), F32),
            dma((4,)),
            *pair(4),
            *pair(2),
            *pair(CHUNKS, 2),
            *pair(CHUNKS, 2),
            *pair(2),
            *pair(TPARTS),
            *pair(2),
            *pair(TPARTS),
            *pair(units, NY - 1, 2),
            *pair(units, 2),
            *pair(2),
            dma,
            dma,
            *pair(2, NY),
            *pair(NX * NCORE),
        ],
        compiler_params=pltpu.CompilerParams(
            collective_id=0, has_side_effects=True, vmem_limit_bytes=56 * 1024 * 1024
        ),
        name="influence",
    )(train_acts, train_grads, query_acts, query_grads, train_seg, query_seg)


def solution(mesh):
    in_specs = (
        P("doc", "hidden"),
        P("doc", "hidden"),
        P("doc", "hidden"),
        P("doc", "hidden"),
        P("doc", None),
        P(),
    )
    return jax.shard_map(
        functools.partial(on_device, mesh.shape["doc"]),
        mesh=mesh,
        in_specs=in_specs,
        out_specs=P("doc", None),
        check_vma=False,
    )
```

```python
import functools
import math

import jax
import jax.numpy as jnp
from jax import lax
from jax.experimental import pallas as pl
from jax.experimental.pallas import tpu as pltpu
from jax.sharding import PartitionSpec as P

ST = 8
SQ = 8
CYCLE = 4
NY = 4
NX = 2
NCORE = 2
X_HI = 2
CHUNKS = 4
TPARTS = 3
LANES = 128
ACT = 0
GRAD = 1
MESH = pl.DeviceIdType.MESH
CONTRACT = (((1,), (1,)), ((), ()))
F32 = jnp.float32
I32 = jnp.int32
TOP = 32767.0
LEAST = 1e-34

UNITS = {
    "g0": (GRAD, 0, 0, 4, 0, 3),
    "a0": (ACT, 0, 0, 4, 0, 3),
    "g1": (GRAD, 1, 0, 4, 0, 3),
    "g2": (GRAD, 2, 0, 4, 0, 3),
    "g3": (GRAD, 3, 0, 4, 0, 3),
    "a1_01": (ACT, 1, 0, 2, 0, 3),
    "a1_23": (ACT, 1, 2, 2, 0, 3),
    "a2_0": (ACT, 2, 0, 1, 0, 3),
    "a2_1": (ACT, 2, 1, 1, 0, 3),
    "a2_2": (ACT, 2, 2, 1, 0, 3),
    "a2_3": (ACT, 2, 3, 1, 0, 3),
    "a3_01": (ACT, 3, 0, 2, 0, 2),
    "a3_2": (ACT, 3, 2, 1, 0, 2),
    "a3_3": (ACT, 3, 3, 1, 0, 3),
    "a3_last": (ACT, 3, 0, 3, 2, 1),
}
ORDER = list(UNITS)
HELD = ("g0", "a0", "g1", "a1_01", "a1_23")


def spread(tile, rows, lanes):
    wide = jnp.concatenate([tile] * (lanes // LANES), axis=1) if lanes > LANES else tile
    return jnp.concatenate([wide] * (rows // 8), axis=0) if rows > 8 else wide


def highest(value):
    rows, lanes = value.shape
    top = jnp.max(jnp.abs(value).reshape(rows // 8, 8, lanes), axis=0)
    return functools.reduce(
        jnp.maximum, [top[:, b * LANES : (b + 1) * LANES] for b in range(lanes // LANES)]
    )


def squeeze(high, low):
    scale = jnp.maximum(jnp.maximum(highest(high), highest(low)), LEAST)
    times = spread(TOP / scale, *high.shape)
    packed = jnp.round(high * times).astype(I32) * 65536 + jnp.round(low * times).astype(I32)
    return packed, scale * (1.0 / TOP)


def unsqueeze(packed, step):
    high = lax.shift_right_arithmetic(packed + 32768, jnp.full_like(packed, 16))
    low = packed - high * 65536
    step = spread(step, *packed.shape)
    return high.astype(F32) * step, low.astype(F32) * step


def thirds(value, axis):
    parts = []
    for _ in range(3):
        parts.append(value.astype(jnp.bfloat16))
        value = value - parts[-1].astype(F32)
    return jnp.concatenate(parts, axis=axis)


def kernel(
    n_doc,
    ta_hbm,
    tg_hbm,
    qa_hbm,
    qg_hbm,
    tseg_ref,
    qseg_ref,
    out_ref,
    ta,
    tg,
    qa,
    qg,
    gram,
    yout,
    yout_step,
    yin,
    yin_step,
    xout,
    xout_step,
    xin,
    xin_step,
    done,
    gout,
    gout_step,
    gin,
    gin_step,
    grads_up,
    segn,
    small,
    fin_y,
    fin_x,
    early_sum,
    local_sem,
    own_send,
    own_recv,
    qg_send,
    qg_recv,
    qa_send,
    qa_recv,
    hop_send,
    hop_recv,
    tg_send,
    tg_recv,
    ta_send,
    ta_recv,
    tgf_send,
    tgf_recv,
    taf_send,
    taf_recv,
    y_send,
    y_recv,
    x_send,
    x_recv,
    g_send,
    g_recv,
    s_send,
    s_recv,
    fy_send,
    fy_recv,
    fx_send,
    fx_recv,
):
    rows_t, wide_a = ta_hbm.shape
    rows_q, wide_g = qg_hbm.shape
    half = rows_q // NCORE
    chunk = half // CHUNKS
    part = rows_t // TPARTS
    ry = chunk // (NY * NX)
    factor = math.sqrt(ST * SQ / (rows_t * rows_q))

    doc = lax.axis_index("doc")
    place = lax.axis_index("hidden")
    core = lax.rem(place, NCORE)
    other = 1 - core
    my_x = lax.rem(place // NCORE, NX)
    my_y = place // (NCORE * NX)
    up = lax.rem(doc + 1, n_doc)
    down = lax.rem(doc + n_doc - 1, n_doc)

    def y_of(d):
        return lax.rem(my_y + d, NY)

    def spot(y, x, c):
        return y * (NX * NCORE) + x * NCORE + c

    sibling = (doc, spot(my_y, my_x, other))
    deep = n_doc // X_HI
    wrap = lax.rem(doc, deep) // (deep - 1)
    keep_far = my_x + wrap * (1 - 2 * my_x)

    def keep(kind, r):
        return keep_far if kind == GRAD and r >= 2 else my_x

    x_peer = (doc, spot(my_y, 1 - my_x, core))
    x_other = (doc, spot(my_y, 1 - my_x, other))

    def y_peer(d, of=doc):
        return (of, spot(y_of(d), my_x, core))

    def remote(src, dst, send, recv, who):
        return pltpu.make_async_remote_copy(
            src_ref=src, dst_ref=dst, send_sem=send, recv_sem=recv, device_id=who, device_id_type=MESH
        )

    def cols(wide, whose):
        return pl.ds(pl.multiple_of(whose * wide, LANES), wide)

    def q_half(whose):
        return pl.ds(pl.multiple_of(whose * half, half), half)

    def swap(j, whose_q, whose):
        return (
            (qg_hbm.at[q_half(whose_q), :], qg.at[0, :, cols(wide_g, whose)]),
            (tg_hbm, tg.at[0, :, cols(wide_g, whose)]),
            (qa_hbm.at[q_half(whose_q), :], qa.at[0, :, cols(wide_a, whose)]),
            (ta_hbm, ta.at[0, :, cols(wide_a, whose)]),
        )[j]

    def swap_out(j):
        return remote(*swap(j, other, core), own_send.at[j], own_recv.at[j], sibling)

    def swap_in(j):
        return remote(*swap(j, core, other), own_send.at[j], own_recv.at[j], sibling)

    def local(j):
        return pltpu.make_async_copy(*swap(j, core, core), local_sem.at[j])

    def who_up(far):
        return core if far == 0 else other

    def qg_up(far):
        to = who_up(far)
        return remote(
            qg_hbm.at[q_half(to), :],
            qg.at[1, :, cols(wide_g, core)],
            qg_send.at[far],
            qg_recv.at[far],
            (up, spot(my_y, my_x, to)),
        )

    def qg_arrival(far):
        return remote(
            qg_hbm.at[q_half(core), :],
            qg.at[1, :, cols(wide_g, who_up(far))],
            qg_send.at[far],
            qg_recv.at[far],
            (up, spot(my_y, my_x, who_up(far))),
        )

    def q_chunk(m):
        return pl.ds(m * chunk, chunk)

    def qa_up(m, far):
        to = who_up(far)
        return remote(
            qa_hbm.at[pl.ds(pl.multiple_of(to * half + m * chunk, chunk), chunk), :],
            qa.at[1, q_chunk(m), cols(wide_a, core)],
            qa_send.at[m, far],
            qa_recv.at[m, far],
            (up, spot(my_y, my_x, to)),
        )

    def qa_arrival(m, far):
        return remote(
            qa_hbm.at[pl.ds(pl.multiple_of(core * half + m * chunk, chunk), chunk), :],
            qa.at[1, q_chunk(m), cols(wide_a, who_up(far))],
            qa_send.at[m, far],
            qa_recv.at[m, far],
            (up, spot(my_y, my_x, who_up(far))),
        )

    def qa_hop(m, far):
        at = cols(wide_a, who_up(far))
        return remote(
            qa.at[1, q_chunk(m), at],
            qa.at[2, q_chunk(m), at],
            hop_send.at[m, far],
            hop_recv.at[m, far],
            (up, place),
        )

    def hop_arrival(m):
        for far in range(2):
            qa_hop(m, far).wait_recv()

    def tg_down(step):
        src = tg_hbm if step == 0 else tg.at[step, :, cols(wide_g, core)]
        return remote(
            src, tg.at[step + 1, :, cols(wide_g, core)], tg_send.at[step], tg_recv.at[step], (down, place)
        )

    def tg_across(step, whose):
        ref = tg.at[step + 1, :, cols(wide_g, whose)]
        return remote(ref, ref, tgf_send.at[step], tgf_recv.at[step], sibling)

    def t_part(p):
        return pl.ds(p * part, part)

    def ta_down(p):
        return remote(
            ta_hbm.at[t_part(p), :],
            ta.at[1, t_part(p), cols(wide_a, core)],
            ta_send.at[p],
            ta_recv.at[p],
            (down, place),
        )

    def ta_across(p, whose):
        ref = ta.at[1, t_part(p), cols(wide_a, whose)]
        return remote(ref, ref, taf_send.at[p], taf_recv.at[p], sibling)

    seg_copy = remote(tseg_ref, segn, s_send, s_recv, (down, place))

    def area(name):
        kind, r, m, n, p, k = UNITS[name]
        return kind, r, pl.ds(m * ry, n * ry), pl.ds(p * part, k * part)

    early = []

    def half_compute(name):
        _, r, m, n, _, _ = UNITS[name]
        at = cols(wide_a, core)
        early_sum[len(early)] = lax.dot_general(
            ta[1 if r == 3 else 0, :, at],
            qa[2, m * chunk : (m + n) * chunk, at],
            CONTRACT,
            preferred_element_type=F32,
        )
        early.append(name)

    def compute(name):
        kind, r, m, n, p, k = UNITS[name]
        if kind == ACT:
            query, train = qa.at[min(r, 2)], ta.at[1 if r == 3 else 0]
        else:
            query, train = qg.at[min(r, 1)], tg.at[max(r - 1, 0)]
        left = query[m * chunk : (m + n) * chunk, :]
        right = train[p * part : (p + k) * part, :]
        if name in early:
            at = cols(wide_a, other)
            late = lax.dot_general(
                ta[1 if r == 3 else 0, :, at],
                qa[2, m * chunk : (m + n) * chunk, at],
                CONTRACT,
                preferred_element_type=F32,
            )
            total = (early_sum[early.index(name)] + late).T
        elif n == CHUNKS:
            total = lax.dot_general(left, right, CONTRACT, preferred_element_type=F32)
        else:
            total = lax.dot_general(right, left, CONTRACT, preferred_element_type=F32).T
        for i in range(n):
            gram[kind, r, :, :, (m + i) * ry : (m + i + 1) * ry, p * part : (p + k) * part] = total[
                i * chunk : (i + 1) * chunk
            ].reshape(NY, NX, ry, k * part)

    def y_copy(name, d):
        kind, r, rows, lanes = area(name)
        u = ORDER.index(name)
        return (
            remote(
                yout.at[kind, r, y_of(d), rows, lanes],
                yin.at[kind, r, d - 1, rows, lanes],
                y_send.at[u, d - 1, 0],
                y_recv.at[u, d - 1, 0],
                y_peer(d),
            ),
            remote(
                yout_step.at[u, y_of(d)],
                yin_step.at[u, d - 1],
                y_send.at[u, d - 1, 1],
                y_recv.at[u, d - 1, 1],
                y_peer(d),
            ),
        )

    def x_copy(name):
        _, _, _, n, _, k = UNITS[name]
        u = ORDER.index(name)
        piece = (u, pl.ds(0, n * ry), pl.ds(0, k * part // 2))
        return (
            remote(xout.at[piece], xin.at[piece], x_send.at[u, 0], x_recv.at[u, 0], x_peer),
            remote(xout_step.at[u], xin_step.at[u], x_send.at[u, 1], x_recv.at[u, 1], x_peer),
        )

    def g_move():
        who = (up, spot(my_y, keep_far, core))
        return (
            remote(gout, gin, g_send.at[0], g_recv.at[0], who),
            remote(gout_step, gin_step, g_send.at[1], g_recv.at[1], who),
        )

    def unit(name):
        compute(name)
        kind, r, rows, lanes = area(name)
        for d in range(1, NY):
            y = y_of(d)
            packed, step = squeeze(gram[kind, r, y, 0, rows, lanes], gram[kind, r, y, 1, rows, lanes])
            yout[kind, r, y, rows, lanes] = packed
            yout_step[ORDER.index(name), y] = step
            for copy in y_copy(name, d):
                copy.start()

    def x_start(name):
        for copy in x_copy(name):
            copy.start()

    def y_finish(name):
        kind, r, m, n, p, k = UNITS[name]
        _, _, rows, lanes = area(name)
        u = ORDER.index(name)
        high, low = gram[kind, r, my_y, 0, rows, lanes], gram[kind, r, my_y, 1, rows, lanes]
        for d in range(1, NY):
            for copy in y_copy(name, d):
                copy.wait_recv()
            more = unsqueeze(yin[kind, r, d - 1, rows, lanes], yin_step[u, d - 1])
            high, low = high + more[0], low + more[1]
        gram[kind, r, my_y, 0, rows, lanes] = high
        gram[kind, r, my_y, 1, rows, lanes] = low
        go = gram[kind, r, my_y, 1 - keep(kind, r), rows, lanes]
        wide = k * part // 2
        packed, step = squeeze(go[:, :wide], go[:, wide:])
        xout[u, : n * ry, :wide] = packed
        xout_step[u] = step
        if name not in HELD:
            x_start(name)

    def x_finish(name):
        kind, r, m, n, p, k = UNITS[name]
        _, _, rows, _ = area(name)
        u = ORDER.index(name)
        for copy in x_copy(name):
            copy.wait_recv()
        wide = k * part // 2
        for i, more in enumerate(unsqueeze(xin[u, : n * ry, :wide], xin_step[u])):
            lanes = pl.ds(p * part + i * wide, wide)
            done[kind, r, rows, lanes] = gram[kind, r, my_y, keep(kind, r), rows, lanes] + more

    def onehots(r):
        seg_t = (segn if r == 3 else tseg_ref)[...]
        onehot_t = (lax.broadcasted_iota(jnp.int32, (ST, rows_t), 0) == seg_t).astype(jnp.bfloat16)
        owner = lax.rem(doc + n_doc - min(r, 2), n_doc)
        seg_q = qseg_ref[pl.ds(owner, 1), :]
        row = lax.broadcasted_iota(jnp.int32, (CHUNKS * ry, rows_q), 0)
        token = lax.broadcasted_iota(jnp.int32, (CHUNKS * ry, rows_q), 1)
        mine = core * half + (row // ry) * chunk + my_y * (NX * ry) + my_x * ry + row % ry
        ids = jnp.sum(jnp.where(token == mine, seg_q, 0), axis=1, keepdims=True)
        lane = lax.broadcasted_iota(jnp.int32, (CHUNKS * ry, LANES), 1)
        onehot_q = (lane == ids + r * SQ).astype(jnp.bfloat16)
        return onehot_t, jnp.concatenate([onehot_q] * 3, axis=0)

    def segment_sum(r, hots):
        onehot_t, onehot_q = hots
        grads = grads_up[r - 2] if r >= 2 else done[GRAD, r]
        parts = thirds(done[ACT, r] * grads, 0)
        left = lax.dot_general(onehot_t, parts, CONTRACT, preferred_element_type=F32)
        total = jnp.dot(thirds(left, 0), onehot_q, preferred_element_type=F32)
        return (total[:ST] + total[ST : 2 * ST]) + total[2 * ST :]

    def arrive_and_hop(m):
        for far in range(2):
            qa_arrival(m, far).wait_recv()
            qa_hop(m, far).start()

    for j in range(4):
        local(j).start()
    greet = [sibling, x_peer, x_other]
    greet += [(up, spot(my_y, my_x, other)), (down, spot(my_y, my_x, other))]
    greet += [(up, spot(my_y, 1 - my_x, core)), (down, spot(my_y, 1 - my_x, core))]
    greet += [y_peer(d) for d in range(1, NY)]
    greet += [y_peer(d, up) for d in range(NY)]
    greet += [y_peer(d, down) for d in range(NY)]
    barrier = pltpu.get_barrier_semaphore()
    for who in greet:
        pl.semaphore_signal(barrier, inc=1, device_id=who, device_id_type=MESH)
    pl.semaphore_wait(barrier, len(greet))

    for far in range(2):
        qg_up(far).start()
    tg_down(0).start()
    for j in range(4):
        swap_out(j).start()
    for far in range(2):
        qa_up(0, far).start()
    ta_down(0).start()
    for m in range(1, CHUNKS):
        for far in range(2):
            qa_up(m, far).start()
    seg_copy.start()

    for j in range(2):
        local(j).wait()
        swap_in(j).wait_recv()
    unit("g0")
    for j in range(2, 4):
        local(j).wait()
        swap_in(j).wait_recv()
    unit("a0")
    for far in range(2):
        qg_arrival(far).wait_recv()
    unit("g1")
    tg_down(0).wait_recv()
    tg_down(1).start()
    tg_across(0, core).start()
    for p in range(1, TPARTS):
        ta_down(p).start()
    tg_across(0, other).wait_recv()
    unit("g2")
    arrive_and_hop(0)
    y_finish("g0")
    y_finish("a0")
    arrive_and_hop(1)
    unit("a1_01")
    y_finish("g1")
    arrive_and_hop(2)
    ta_down(0).wait_recv()
    ta_across(0, core).start()
    y_finish("g2")
    arrive_and_hop(3)
    unit("a1_23")
    tg_down(1).wait_recv()
    tg_across(1, core).start()
    y_finish("a1_01")
    tg_across(1, other).wait_recv()
    unit("g3")
    hop_arrival(0)
    unit("a2_0")
    y_finish("a1_23")
    hop_arrival(1)
    unit("a2_1")
    y_finish("g3")
    y_finish("a2_0")
    ta_down(1).wait_recv()
    ta_across(1, core).start()
    for p in range(2):
        ta_across(p, other).wait_recv()
    unit("a3_01")
    y_finish("a2_1")
    seg_copy.wait_recv()
    hots_0, hots_1, hots_2, hots_3 = onehots(0), onehots(1), onehots(2), onehots(3)
    hop_arrival(2)
    unit("a2_2")
    unit("a3_2")
    y_finish("a3_01")
    y_finish("a2_2")
    y_finish("a3_2")
    ta_down(2).wait_recv()
    ta_across(2, core).start()
    ta_across(2, other).wait_recv()
    unit("a3_last")
    qa_hop(3, 0).wait_recv()
    for name in ("a3_3", "a2_3"):
        half_compute(name)
    qa_hop(3, 1).wait_recv()
    for name in HELD:
        x_start(name)
    unit("a3_3")
    unit("a2_3")
    for name in ("g2", "g3"):
        x_finish(name)
    gout[...], gout_step[...] = squeeze(done[GRAD, 2], done[GRAD, 3])
    for copy in g_move():
        copy.start()
    for name in ("a2_0", "a2_1", "a3_01", "a2_2", "a3_2"):
        x_finish(name)
    y_finish("a3_last")
    y_finish("a3_3")
    y_finish("a2_3")
    for name in HELD:
        x_finish(name)
    base = segment_sum(0, hots_0) + segment_sum(1, hots_1)
    for copy in g_move():
        copy.wait_recv()
    grads_up[0], grads_up[1] = unsqueeze(gin[...], gin_step[...])
    x_finish("a3_last")
    x_finish("a3_3")
    small[...] = segment_sum(3, hots_3)
    fu = [
        remote(small, fin_y.at[1, my_y], fy_send.at[1, d], fy_recv.at[1, my_y], y_peer(d, up))
        for d in range(NY)
    ]
    for copy in fu:
        copy.start()
    x_finish("a2_3")
    fin_y[0, my_y] = base + segment_sum(2, hots_2)
    fy = [
        remote(fin_y.at[0, my_y], fin_y.at[0, my_y], fy_send.at[0, d], fy_recv.at[0, my_y], y_peer(d))
        for d in range(1, NY)
    ]
    for copy in fy:
        copy.start()
    for d in range(1, NY):
        y = y_of(d)
        remote(fin_y.at[0, y], fin_y.at[0, y], fy_send.at[0, d], fy_recv.at[0, y], y_peer(d)).wait_recv()
    for d in range(NY):
        y = y_of(d)
        remote(small, fin_y.at[1, y], fy_send.at[1, d], fy_recv.at[1, y], y_peer(d, up)).wait_recv()
    total = fin_y[0, 0] + fin_y[1, 0]
    for y in range(1, NY):
        total = total + (fin_y[0, y] + fin_y[1, y])
    mine = lax.rem(place, NX * NCORE)
    fin_x[mine] = total
    fx = []
    for i, who in enumerate((sibling, x_peer, x_other)):
        fx.append(remote(fin_x.at[mine], fin_x.at[mine], fx_send.at[i], fx_recv.at[mine], who))
        fx[-1].start()
    for i, (x, c) in enumerate(((my_x, other), (1 - my_x, core), (1 - my_x, other))):
        at = x * NCORE + c
        remote(fin_x.at[at], fin_x.at[at], fx_send.at[i], fx_recv.at[at], sibling).wait_recv()
    out_ref[...] = (((fin_x[0] + fin_x[1]) + (fin_x[2] + fin_x[3])) * factor)[:, : CYCLE * SQ]

    seg_copy.wait_send()
    for copy in fy + fu + fx:
        copy.wait_send()
    for j in range(4):
        swap_out(j).wait_send()
    for far in range(2):
        qg_up(far).wait_send()
    for m in range(CHUNKS):
        for far in range(2):
            qa_up(m, far).wait_send()
            qa_hop(m, far).wait_send()
    for step in range(2):
        tg_down(step).wait_send()
        tg_across(step, core).wait_send()
    for p in range(TPARTS):
        ta_down(p).wait_send()
        ta_across(p, core).wait_send()
    for copy in g_move():
        copy.wait_send()
    for name in ORDER:
        for d in range(1, NY):
            for copy in y_copy(name, d):
                copy.wait_send()
        for copy in x_copy(name):
            copy.wait_send()


def on_device(n_doc, train_acts, train_grads, query_acts, query_grads, train_seg, query_seg):
    rows_t, wide_a = train_acts.shape
    rows_q, wide_g = query_grads.shape
    half = rows_q // NCORE
    rows = half // (NY * NX)
    units = len(ORDER)
    dma = pltpu.SemaphoreType.DMA
    anywhere = pl.BlockSpec(memory_space=pl.ANY)
    vmem = pl.BlockSpec(memory_space=pltpu.VMEM)
    bf16 = jnp.bfloat16

    def pair(*shape):
        return [dma(shape), dma(shape)]

    return pl.pallas_call(
        functools.partial(kernel, n_doc),
        out_shape=jax.ShapeDtypeStruct((ST, CYCLE * SQ), F32),
        in_specs=[anywhere] * 4 + [vmem] * 2,
        out_specs=vmem,
        scratch_shapes=[
            pltpu.VMEM((2, rows_t, NCORE * wide_a), bf16),
            pltpu.VMEM((3, rows_t, NCORE * wide_g), bf16),
            pltpu.VMEM((3, half, NCORE * wide_a), bf16),
            pltpu.VMEM((2, half, NCORE * wide_g), bf16),
            pltpu.VMEM((2, CYCLE, NY, NX, rows, rows_t), F32),
            pltpu.VMEM((2, CYCLE, NY, rows, rows_t), I32),
            pltpu.VMEM((units, NY, 8, LANES), F32),
            pltpu.VMEM((2, CYCLE, NY - 1, rows, rows_t), I32),
            pltpu.VMEM((units, NY - 1, 8, LANES), F32),
            pltpu.VMEM((units, rows, rows_t // 2), I32),
            pltpu.VMEM((units, 8, LANES), F32),
            pltpu.VMEM((units, rows, rows_t // 2), I32),
            pltpu.VMEM((units, 8, LANES), F32),
            pltpu.VMEM((2, CYCLE, rows, rows_t), F32),
            pltpu.VMEM((rows, rows_t), I32),
            pltpu.VMEM((8, LANES), F32),
            pltpu.VMEM((rows, rows_t), I32),
            pltpu.VMEM((8, LANES), F32),
            pltpu.VMEM((2, rows, rows_t), F32),
            pltpu.VMEM((1, rows_t), I32),
            pltpu.VMEM((ST, LANES), F32),
            pltpu.VMEM((2, NY, ST, LANES), F32),
            pltpu.VMEM((NX * NCORE, ST, LANES), F32),
            pltpu.VMEM((2, rows_t, half // CHUNKS), F32),
            dma((4,)),
            *pair(4),
            *pair(2),
            *pair(CHUNKS, 2),
            *pair(CHUNKS, 2),
            *pair(2),
            *pair(TPARTS),
            *pair(2),
            *pair(TPARTS),
            *pair(units, NY - 1, 2),
            *pair(units, 2),
            *pair(2),
            dma,
            dma,
            *pair(2, NY),
            *pair(NX * NCORE),
        ],
        compiler_params=pltpu.CompilerParams(
            collective_id=0, has_side_effects=True, vmem_limit_bytes=56 * 1024 * 1024
        ),
        name="influence",
    )(train_acts, train_grads, query_acts, query_grads, train_seg, query_seg)


def solution(mesh):
    in_specs = (
        P("doc", "hidden"),
        P("doc", "hidden"),
        P("doc", "hidden"),
        P("doc", "hidden"),
        P("doc", None),
        P(),
    )
    return jax.shard_map(
        functools.partial(on_device, mesh.shape["doc"]),
        mesh=mesh,
        in_specs=in_specs,
        out_specs=P("doc", None),
        check_vma=False,
    )
```

```python
import functools
import math

import jax
import jax.numpy as jnp
from jax import lax
from jax.experimental import pallas as pl
from jax.experimental.pallas import tpu as pltpu
from jax.sharding import PartitionSpec as P

ST = 8
SQ = 8
CYCLE = 4
NY = 4
NX = 2
NCORE = 2
X_HI = 2
CHUNKS = 4
TPARTS = 3
LANES = 128
ACT = 0
GRAD = 1
MESH = pl.DeviceIdType.MESH
CONTRACT = (((1,), (1,)), ((), ()))
F32 = jnp.float32
I32 = jnp.int32
TOP = 32767.0
LEAST = 1e-34

UNITS = {
    "g0": (GRAD, 0, 0, 4, 0, 3),
    "a0": (ACT, 0, 0, 4, 0, 3),
    "g1": (GRAD, 1, 0, 4, 0, 3),
    "g2": (GRAD, 2, 0, 4, 0, 3),
    "g3": (GRAD, 3, 0, 4, 0, 3),
    "a1_01": (ACT, 1, 0, 2, 0, 3),
    "a1_23": (ACT, 1, 2, 2, 0, 3),
    "a2_0": (ACT, 2, 0, 1, 0, 3),
    "a2_1": (ACT, 2, 1, 1, 0, 3),
    "a2_2": (ACT, 2, 2, 1, 0, 3),
    "a2_3": (ACT, 2, 3, 1, 0, 3),
    "a3_01": (ACT, 3, 0, 2, 0, 2),
    "a3_2": (ACT, 3, 2, 1, 0, 2),
    "a3_3": (ACT, 3, 3, 1, 0, 3),
    "a3_last": (ACT, 3, 0, 3, 2, 1),
}
ORDER = list(UNITS)
HELD = ("g0", "a0", "g1", "a1_01", "a1_23")


def spread(tile, rows, lanes):
    wide = jnp.concatenate([tile] * (lanes // LANES), axis=1) if lanes > LANES else tile
    return jnp.concatenate([wide] * (rows // 8), axis=0) if rows > 8 else wide


def highest(value):
    rows, lanes = value.shape
    top = jnp.max(jnp.abs(value).reshape(rows // 8, 8, lanes), axis=0)
    return functools.reduce(
        jnp.maximum, [top[:, b * LANES : (b + 1) * LANES] for b in range(lanes // LANES)]
    )


def squeeze(high, low):
    scale = jnp.maximum(jnp.maximum(highest(high), highest(low)), LEAST)
    times = spread(TOP / scale, *high.shape)
    packed = jnp.round(high * times).astype(I32) * 65536 + jnp.round(low * times).astype(I32)
    return packed, scale * (1.0 / TOP)


def unsqueeze(packed, step):
    high = lax.shift_right_arithmetic(packed + 32768, jnp.full_like(packed, 16))
    low = packed - high * 65536
    step = spread(step, *packed.shape)
    return high.astype(F32) * step, low.astype(F32) * step


def thirds(value, axis):
    parts = []
    for _ in range(3):
        parts.append(value.astype(jnp.bfloat16))
        value = value - parts[-1].astype(F32)
    return jnp.concatenate(parts, axis=axis)


def kernel(
    n_doc,
    ta_hbm,
    tg_hbm,
    qa_hbm,
    qg_hbm,
    tseg_ref,
    qseg_ref,
    out_ref,
    ta,
    tg,
    qa,
    qg,
    gram,
    yout,
    yout_step,
    yin,
    yin_step,
    xout,
    xout_step,
    xin,
    xin_step,
    done,
    gout,
    gout_step,
    gin,
    gin_step,
    grads_up,
    segn,
    small,
    fin_y,
    fin_x,
    early_sum,
    local_sem,
    own_send,
    own_recv,
    qg_send,
    qg_recv,
    qa_send,
    qa_recv,
    hop_send,
    hop_recv,
    tg_send,
    tg_recv,
    ta_send,
    ta_recv,
    tgf_send,
    tgf_recv,
    taf_send,
    taf_recv,
    y_send,
    y_recv,
    x_send,
    x_recv,
    g_send,
    g_recv,
    s_send,
    s_recv,
    fy_send,
    fy_recv,
    fx_send,
    fx_recv,
):
    rows_t, wide_a = ta_hbm.shape
    rows_q, wide_g = qg_hbm.shape
    half = rows_q // NCORE
    chunk = half // CHUNKS
    part = rows_t // TPARTS
    ry = chunk // (NY * NX)
    factor = math.sqrt(ST * SQ / (rows_t * rows_q))

    doc = lax.axis_index("doc")
    place = lax.axis_index("hidden")
    core = lax.rem(place, NCORE)
    other = 1 - core
    my_x = lax.rem(place // NCORE, NX)
    my_y = place // (NCORE * NX)
    up = lax.rem(doc + 1, n_doc)
    down = lax.rem(doc + n_doc - 1, n_doc)

    def y_of(d):
        return lax.rem(my_y + d, NY)

    def spot(y, x, c):
        return y * (NX * NCORE) + x * NCORE + c

    sibling = (doc, spot(my_y, my_x, other))
    deep = n_doc // X_HI
    wrap = lax.rem(doc, deep) // (deep - 1)
    keep_far = my_x + wrap * (1 - 2 * my_x)

    def keep(kind, r):
        return keep_far if kind == GRAD and r >= 2 else my_x

    x_peer = (doc, spot(my_y, 1 - my_x, core))
    x_other = (doc, spot(my_y, 1 - my_x, other))

    def y_peer(d, of=doc):
        return (of, spot(y_of(d), my_x, core))

    def remote(src, dst, send, recv, who):
        return pltpu.make_async_remote_copy(
            src_ref=src, dst_ref=dst, send_sem=send, recv_sem=recv, device_id=who, device_id_type=MESH
        )

    def cols(wide, whose):
        return pl.ds(pl.multiple_of(whose * wide, LANES), wide)

    def q_half(whose):
        return pl.ds(pl.multiple_of(whose * half, half), half)

    def swap(j, whose_q, whose):
        return (
            (qg_hbm.at[q_half(whose_q), :], qg.at[0, :, cols(wide_g, whose)]),
            (tg_hbm, tg.at[0, :, cols(wide_g, whose)]),
            (qa_hbm.at[q_half(whose_q), :], qa.at[0, :, cols(wide_a, whose)]),
            (ta_hbm, ta.at[0, :, cols(wide_a, whose)]),
        )[j]

    def swap_out(j):
        return remote(*swap(j, other, core), own_send.at[j], own_recv.at[j], sibling)

    def swap_in(j):
        return remote(*swap(j, core, other), own_send.at[j], own_recv.at[j], sibling)

    def local(j):
        return pltpu.make_async_copy(*swap(j, core, core), local_sem.at[j])

    def who_up(far):
        return core if far == 0 else other

    def qg_up(far):
        to = who_up(far)
        return remote(
            qg_hbm.at[q_half(to), :],
            qg.at[1, :, cols(wide_g, core)],
            qg_send.at[far],
            qg_recv.at[far],
            (up, spot(my_y, my_x, to)),
        )

    def qg_arrival(far):
        return remote(
            qg_hbm.at[q_half(core), :],
            qg.at[1, :, cols(wide_g, who_up(far))],
            qg_send.at[far],
            qg_recv.at[far],
            (up, spot(my_y, my_x, who_up(far))),
        )

    def q_chunk(m):
        return pl.ds(m * chunk, chunk)

    def qa_up(m, far):
        to = who_up(far)
        return remote(
            qa_hbm.at[pl.ds(pl.multiple_of(to * half + m * chunk, chunk), chunk), :],
            qa.at[1, q_chunk(m), cols(wide_a, core)],
            qa_send.at[m, far],
            qa_recv.at[m, far],
            (up, spot(my_y, my_x, to)),
        )

    def qa_arrival(m, far):
        return remote(
            qa_hbm.at[pl.ds(pl.multiple_of(core * half + m * chunk, chunk), chunk), :],
            qa.at[1, q_chunk(m), cols(wide_a, who_up(far))],
            qa_send.at[m, far],
            qa_recv.at[m, far],
            (up, spot(my_y, my_x, who_up(far))),
        )

    def qa_hop(m, far):
        at = cols(wide_a, who_up(far))
        return remote(
            qa.at[1, q_chunk(m), at],
            qa.at[2, q_chunk(m), at],
            hop_send.at[m, far],
            hop_recv.at[m, far],
            (up, place),
        )

    def hop_arrival(m):
        for far in range(2):
            qa_hop(m, far).wait_recv()

    def tg_down(step):
        src = tg_hbm if step == 0 else tg.at[step, :, cols(wide_g, core)]
        return remote(
            src, tg.at[step + 1, :, cols(wide_g, core)], tg_send.at[step], tg_recv.at[step], (down, place)
        )

    def tg_across(step, whose):
        ref = tg.at[step + 1, :, cols(wide_g, whose)]
        return remote(ref, ref, tgf_send.at[step], tgf_recv.at[step], sibling)

    def t_part(p):
        return pl.ds(p * part, part)

    def ta_down(p):
        return remote(
            ta_hbm.at[t_part(p), :],
            ta.at[1, t_part(p), cols(wide_a, core)],
            ta_send.at[p],
            ta_recv.at[p],
            (down, place),
        )

    def ta_across(p, whose):
        ref = ta.at[1, t_part(p), cols(wide_a, whose)]
        return remote(ref, ref, taf_send.at[p], taf_recv.at[p], sibling)

    seg_copy = remote(tseg_ref, segn, s_send, s_recv, (down, place))

    def area(name):
        kind, r, m, n, p, k = UNITS[name]
        return kind, r, pl.ds(m * ry, n * ry), pl.ds(p * part, k * part)

    early = []

    def half_compute(name):
        _, r, m, n, _, _ = UNITS[name]
        at = cols(wide_a, core)
        early_sum[len(early)] = lax.dot_general(
            ta[1 if r == 3 else 0, :, at],
            qa[2, m * chunk : (m + n) * chunk, at],
            CONTRACT,
            preferred_element_type=F32,
        )
        early.append(name)

    def compute(name):
        kind, r, m, n, p, k = UNITS[name]
        if kind == ACT:
            query, train = qa.at[min(r, 2)], ta.at[1 if r == 3 else 0]
        else:
            query, train = qg.at[min(r, 1)], tg.at[max(r - 1, 0)]
        left = query[m * chunk : (m + n) * chunk, :]
        right = train[p * part : (p + k) * part, :]
        if name in early:
            at = cols(wide_a, other)
            late = lax.dot_general(
                ta[1 if r == 3 else 0, :, at],
                qa[2, m * chunk : (m + n) * chunk, at],
                CONTRACT,
                preferred_element_type=F32,
            )
            total = (early_sum[early.index(name)] + late).T
        elif n == CHUNKS:
            total = lax.dot_general(left, right, CONTRACT, preferred_element_type=F32)
        else:
            total = lax.dot_general(right, left, CONTRACT, preferred_element_type=F32).T
        for i in range(n):
            gram[kind, r, :, :, (m + i) * ry : (m + i + 1) * ry, p * part : (p + k) * part] = total[
                i * chunk : (i + 1) * chunk
            ].reshape(NY, NX, ry, k * part)

    def y_copy(name, d):
        kind, r, rows, lanes = area(name)
        u = ORDER.index(name)
        return (
            remote(
                yout.at[kind, r, y_of(d), rows, lanes],
                yin.at[kind, r, d - 1, rows, lanes],
                y_send.at[u, d - 1, 0],
                y_recv.at[u, d - 1, 0],
                y_peer(d),
            ),
            remote(
                yout_step.at[u, y_of(d)],
                yin_step.at[u, d - 1],
                y_send.at[u, d - 1, 1],
                y_recv.at[u, d - 1, 1],
                y_peer(d),
            ),
        )

    def x_copy(name):
        _, _, _, n, _, k = UNITS[name]
        u = ORDER.index(name)
        piece = (u, pl.ds(0, n * ry), pl.ds(0, k * part // 2))
        return (
            remote(xout.at[piece], xin.at[piece], x_send.at[u, 0], x_recv.at[u, 0], x_peer),
            remote(xout_step.at[u], xin_step.at[u], x_send.at[u, 1], x_recv.at[u, 1], x_peer),
        )

    def g_move():
        who = (up, spot(my_y, keep_far, core))
        return (
            remote(gout, gin, g_send.at[0], g_recv.at[0], who),
            remote(gout_step, gin_step, g_send.at[1], g_recv.at[1], who),
        )

    def unit(name):
        compute(name)
        kind, r, rows, lanes = area(name)
        for d in range(1, NY):
            y = y_of(d)
            packed, step = squeeze(gram[kind, r, y, 0, rows, lanes], gram[kind, r, y, 1, rows, lanes])
            yout[kind, r, y, rows, lanes] = packed
            yout_step[ORDER.index(name), y] = step
            for copy in y_copy(name, d):
                copy.start()

    def x_start(name):
        for copy in x_copy(name):
            copy.start()

    def y_finish(name):
        kind, r, m, n, p, k = UNITS[name]
        _, _, rows, lanes = area(name)
        u = ORDER.index(name)
        high, low = gram[kind, r, my_y, 0, rows, lanes], gram[kind, r, my_y, 1, rows, lanes]
        for d in range(1, NY):
            for copy in y_copy(name, d):
                copy.wait_recv()
            more = unsqueeze(yin[kind, r, d - 1, rows, lanes], yin_step[u, d - 1])
            high, low = high + more[0], low + more[1]
        gram[kind, r, my_y, 0, rows, lanes] = high
        gram[kind, r, my_y, 1, rows, lanes] = low
        go = gram[kind, r, my_y, 1 - keep(kind, r), rows, lanes]
        wide = k * part // 2
        packed, step = squeeze(go[:, :wide], go[:, wide:])
        xout[u, : n * ry, :wide] = packed
        xout_step[u] = step
        if name not in HELD:
            x_start(name)

    def x_finish(name):
        kind, r, m, n, p, k = UNITS[name]
        _, _, rows, _ = area(name)
        u = ORDER.index(name)
        for copy in x_copy(name):
            copy.wait_recv()
        wide = k * part // 2
        for i, more in enumerate(unsqueeze(xin[u, : n * ry, :wide], xin_step[u])):
            lanes = pl.ds(p * part + i * wide, wide)
            done[kind, r, rows, lanes] = gram[kind, r, my_y, keep(kind, r), rows, lanes] + more

    def onehots(r):
        seg_t = (segn if r == 3 else tseg_ref)[...]
        onehot_t = (lax.broadcasted_iota(jnp.int32, (ST, rows_t), 0) == seg_t).astype(jnp.bfloat16)
        owner = lax.rem(doc + n_doc - min(r, 2), n_doc)
        seg_q = qseg_ref[pl.ds(owner, 1), :]
        row = lax.broadcasted_iota(jnp.int32, (CHUNKS * ry, rows_q), 0)
        token = lax.broadcasted_iota(jnp.int32, (CHUNKS * ry, rows_q), 1)
        mine = core * half + (row // ry) * chunk + my_y * (NX * ry) + my_x * ry + row % ry
        ids = jnp.sum(jnp.where(token == mine, seg_q, 0), axis=1, keepdims=True)
        lane = lax.broadcasted_iota(jnp.int32, (CHUNKS * ry, LANES), 1)
        onehot_q = (lane == ids + r * SQ).astype(jnp.bfloat16)
        return onehot_t, jnp.concatenate([onehot_q] * 3, axis=0)

    def segment_sum(r, hots):
        onehot_t, onehot_q = hots
        grads = grads_up[r - 2] if r >= 2 else done[GRAD, r]
        parts = thirds(done[ACT, r] * grads, 0)
        left = lax.dot_general(onehot_t, parts, CONTRACT, preferred_element_type=F32)
        total = jnp.dot(thirds(left, 0), onehot_q, preferred_element_type=F32)
        return (total[:ST] + total[ST : 2 * ST]) + total[2 * ST :]

    def arrive_and_hop(m):
        for far in range(2):
            qa_arrival(m, far).wait_recv()
            qa_hop(m, far).start()

    for j in range(4):
        local(j).start()
    greet = [sibling, x_peer, x_other]
    greet += [(up, spot(my_y, my_x, other)), (down, spot(my_y, my_x, other))]
    greet += [(up, spot(my_y, 1 - my_x, core)), (down, spot(my_y, 1 - my_x, core))]
    greet += [y_peer(d) for d in range(1, NY)]
    greet += [y_peer(d, up) for d in range(NY)]
    greet += [y_peer(d, down) for d in range(NY)]
    barrier = pltpu.get_barrier_semaphore()
    for who in greet:
        pl.semaphore_signal(barrier, inc=1, device_id=who, device_id_type=MESH)
    pl.semaphore_wait(barrier, len(greet))

    for far in range(2):
        qg_up(far).start()
    tg_down(0).start()
    for j in range(4):
        swap_out(j).start()
    for far in range(2):
        qa_up(0, far).start()
    ta_down(0).start()
    for m in range(1, CHUNKS):
        for far in range(2):
            qa_up(m, far).start()
    seg_copy.start()

    for j in range(2):
        local(j).wait()
        swap_in(j).wait_recv()
    unit("g0")
    for j in range(2, 4):
        local(j).wait()
        swap_in(j).wait_recv()
    unit("a0")
    for far in range(2):
        qg_arrival(far).wait_recv()
    unit("g1")
    tg_down(0).wait_recv()
    tg_down(1).start()
    tg_across(0, core).start()
    for p in range(1, TPARTS):
        ta_down(p).start()
    tg_across(0, other).wait_recv()
    unit("g2")
    arrive_and_hop(0)
    y_finish("g0")
    y_finish("a0")
    arrive_and_hop(1)
    unit("a1_01")
    y_finish("g1")
    arrive_and_hop(2)
    ta_down(0).wait_recv()
    ta_across(0, core).start()
    y_finish("g2")
    arrive_and_hop(3)
    unit("a1_23")
    tg_down(1).wait_recv()
    tg_across(1, core).start()
    y_finish("a1_01")
    tg_across(1, other).wait_recv()
    unit("g3")
    hop_arrival(0)
    unit("a2_0")
    y_finish("a1_23")
    hop_arrival(1)
    unit("a2_1")
    y_finish("g3")
    y_finish("a2_0")
    ta_down(1).wait_recv()
    ta_across(1, core).start()
    for p in range(2):
        ta_across(p, other).wait_recv()
    unit("a3_01")
    y_finish("a2_1")
    seg_copy.wait_recv()
    hots_0, hots_1, hots_2, hots_3 = onehots(0), onehots(1), onehots(2), onehots(3)
    hop_arrival(2)
    unit("a2_2")
    unit("a3_2")
    y_finish("a3_01")
    y_finish("a2_2")
    y_finish("a3_2")
    ta_down(2).wait_recv()
    ta_across(2, core).start()
    ta_across(2, other).wait_recv()
    unit("a3_last")
    qa_hop(3, 0).wait_recv()
    for name in ("a3_3", "a2_3"):
        half_compute(name)
    qa_hop(3, 1).wait_recv()
    for name in HELD:
        x_start(name)
    unit("a3_3")
    unit("a2_3")
    y_finish("a3_last")
    for name in ("g2", "g3"):
        x_finish(name)
    gout[...], gout_step[...] = squeeze(done[GRAD, 2], done[GRAD, 3])
    for copy in g_move():
        copy.start()
    for name in ("a2_0", "a2_1", "a3_01", "a2_2", "a3_2"):
        x_finish(name)
    y_finish("a3_3")
    y_finish("a2_3")
    for name in HELD:
        x_finish(name)
    base = segment_sum(0, hots_0) + segment_sum(1, hots_1)
    for copy in g_move():
        copy.wait_recv()
    grads_up[0], grads_up[1] = unsqueeze(gin[...], gin_step[...])
    x_finish("a3_last")
    x_finish("a3_3")
    small[...] = segment_sum(3, hots_3)
    fu = [
        remote(small, fin_y.at[1, my_y], fy_send.at[1, d], fy_recv.at[1, my_y], y_peer(d, up))
        for d in range(NY)
    ]
    for copy in fu:
        copy.start()
    x_finish("a2_3")
    fin_y[0, my_y] = base + segment_sum(2, hots_2)
    fy = [
        remote(fin_y.at[0, my_y], fin_y.at[0, my_y], fy_send.at[0, d], fy_recv.at[0, my_y], y_peer(d))
        for d in range(1, NY)
    ]
    for copy in fy:
        copy.start()
    for d in range(1, NY):
        y = y_of(d)
        remote(fin_y.at[0, y], fin_y.at[0, y], fy_send.at[0, d], fy_recv.at[0, y], y_peer(d)).wait_recv()
    for d in range(NY):
        y = y_of(d)
        remote(small, fin_y.at[1, y], fy_send.at[1, d], fy_recv.at[1, y], y_peer(d, up)).wait_recv()
    total = fin_y[0, 0] + fin_y[1, 0]
    for y in range(1, NY):
        total = total + (fin_y[0, y] + fin_y[1, y])
    mine = lax.rem(place, NX * NCORE)
    fin_x[mine] = total
    fx = []
    for i, who in enumerate((sibling, x_peer, x_other)):
        fx.append(remote(fin_x.at[mine], fin_x.at[mine], fx_send.at[i], fx_recv.at[mine], who))
        fx[-1].start()
    for i, (x, c) in enumerate(((my_x, other), (1 - my_x, core), (1 - my_x, other))):
        at = x * NCORE + c
        remote(fin_x.at[at], fin_x.at[at], fx_send.at[i], fx_recv.at[at], sibling).wait_recv()
    out_ref[...] = (((fin_x[0] + fin_x[1]) + (fin_x[2] + fin_x[3])) * factor)[:, : CYCLE * SQ]

    seg_copy.wait_send()
    for copy in fy + fu + fx:
        copy.wait_send()
    for j in range(4):
        swap_out(j).wait_send()
    for far in range(2):
        qg_up(far).wait_send()
    for m in range(CHUNKS):
        for far in range(2):
            qa_up(m, far).wait_send()
            qa_hop(m, far).wait_send()
    for step in range(2):
        tg_down(step).wait_send()
        tg_across(step, core).wait_send()
    for p in range(TPARTS):
        ta_down(p).wait_send()
        ta_across(p, core).wait_send()
    for copy in g_move():
        copy.wait_send()
    for name in ORDER:
        for d in range(1, NY):
            for copy in y_copy(name, d):
                copy.wait_send()
        for copy in x_copy(name):
            copy.wait_send()


def on_device(n_doc, train_acts, train_grads, query_acts, query_grads, train_seg, query_seg):
    rows_t, wide_a = train_acts.shape
    rows_q, wide_g = query_grads.shape
    half = rows_q // NCORE
    rows = half // (NY * NX)
    units = len(ORDER)
    dma = pltpu.SemaphoreType.DMA
    anywhere = pl.BlockSpec(memory_space=pl.ANY)
    vmem = pl.BlockSpec(memory_space=pltpu.VMEM)
    bf16 = jnp.bfloat16

    def pair(*shape):
        return [dma(shape), dma(shape)]

    return pl.pallas_call(
        functools.partial(kernel, n_doc),
        out_shape=jax.ShapeDtypeStruct((ST, CYCLE * SQ), F32),
        in_specs=[anywhere] * 4 + [vmem] * 2,
        out_specs=vmem,
        scratch_shapes=[
            pltpu.VMEM((2, rows_t, NCORE * wide_a), bf16),
            pltpu.VMEM((3, rows_t, NCORE * wide_g), bf16),
            pltpu.VMEM((3, half, NCORE * wide_a), bf16),
            pltpu.VMEM((2, half, NCORE * wide_g), bf16),
            pltpu.VMEM((2, CYCLE, NY, NX, rows, rows_t), F32),
            pltpu.VMEM((2, CYCLE, NY, rows, rows_t), I32),
            pltpu.VMEM((units, NY, 8, LANES), F32),
            pltpu.VMEM((2, CYCLE, NY - 1, rows, rows_t), I32),
            pltpu.VMEM((units, NY - 1, 8, LANES), F32),
            pltpu.VMEM((units, rows, rows_t // 2), I32),
            pltpu.VMEM((units, 8, LANES), F32),
            pltpu.VMEM((units, rows, rows_t // 2), I32),
            pltpu.VMEM((units, 8, LANES), F32),
            pltpu.VMEM((2, CYCLE, rows, rows_t), F32),
            pltpu.VMEM((rows, rows_t), I32),
            pltpu.VMEM((8, LANES), F32),
            pltpu.VMEM((rows, rows_t), I32),
            pltpu.VMEM((8, LANES), F32),
            pltpu.VMEM((2, rows, rows_t), F32),
            pltpu.VMEM((1, rows_t), I32),
            pltpu.VMEM((ST, LANES), F32),
            pltpu.VMEM((2, NY, ST, LANES), F32),
            pltpu.VMEM((NX * NCORE, ST, LANES), F32),
            pltpu.VMEM((2, rows_t, half // CHUNKS), F32),
            dma((4,)),
            *pair(4),
            *pair(2),
            *pair(CHUNKS, 2),
            *pair(CHUNKS, 2),
            *pair(2),
            *pair(TPARTS),
            *pair(2),
            *pair(TPARTS),
            *pair(units, NY - 1, 2),
            *pair(units, 2),
            *pair(2),
            dma,
            dma,
            *pair(2, NY),
            *pair(NX * NCORE),
        ],
        compiler_params=pltpu.CompilerParams(
            collective_id=0, has_side_effects=True, vmem_limit_bytes=56 * 1024 * 1024
        ),
        name="influence",
    )(train_acts, train_grads, query_acts, query_grads, train_seg, query_seg)


def solution(mesh):
    in_specs = (
        P("doc", "hidden"),
        P("doc", "hidden"),
        P("doc", "hidden"),
        P("doc", "hidden"),
        P("doc", None),
        P(),
    )
    return jax.shard_map(
        functools.partial(on_device, mesh.shape["doc"]),
        mesh=mesh,
        in_specs=in_specs,
        out_specs=P("doc", None),
        check_vma=False,
    )
```

```python
import functools
import math

import jax
import jax.numpy as jnp
from jax import lax
from jax.experimental import pallas as pl
from jax.experimental.pallas import tpu as pltpu
from jax.sharding import PartitionSpec as P

ST = 8
SQ = 8
CYCLE = 4
NY = 4
NX = 2
NCORE = 2
X_HI = 2
CHUNKS = 4
TPARTS = 3
LANES = 128
ACT = 0
GRAD = 1
MESH = pl.DeviceIdType.MESH
CONTRACT = (((1,), (1,)), ((), ()))
F32 = jnp.float32
I32 = jnp.int32
TOP = 32767.0
LEAST = 1e-34

UNITS = {
    "g0": (GRAD, 0, 0, 4, 0, 3),
    "a0": (ACT, 0, 0, 4, 0, 3),
    "g1": (GRAD, 1, 0, 4, 0, 3),
    "g2": (GRAD, 2, 0, 4, 0, 3),
    "g3": (GRAD, 3, 0, 4, 0, 3),
    "a1_01": (ACT, 1, 0, 2, 0, 3),
    "a1_23": (ACT, 1, 2, 2, 0, 3),
    "a2_0": (ACT, 2, 0, 1, 0, 3),
    "a2_1": (ACT, 2, 1, 1, 0, 3),
    "a2_2": (ACT, 2, 2, 1, 0, 3),
    "a2_3": (ACT, 2, 3, 1, 0, 3),
    "a3_01": (ACT, 3, 0, 2, 0, 2),
    "a3_2": (ACT, 3, 2, 1, 0, 2),
    "a3_3": (ACT, 3, 3, 1, 0, 3),
    "a3_last": (ACT, 3, 0, 3, 2, 1),
}
ORDER = list(UNITS)
HELD = ("g0", "a0", "g1", "a1_01", "a1_23")


def spread(tile, rows, lanes):
    wide = jnp.concatenate([tile] * (lanes // LANES), axis=1) if lanes > LANES else tile
    return jnp.concatenate([wide] * (rows // 8), axis=0) if rows > 8 else wide


def highest(value):
    rows, lanes = value.shape
    top = jnp.max(jnp.abs(value).reshape(rows // 8, 8, lanes), axis=0)
    return functools.reduce(
        jnp.maximum, [top[:, b * LANES : (b + 1) * LANES] for b in range(lanes // LANES)]
    )


def squeeze(high, low):
    scale = jnp.maximum(jnp.maximum(highest(high), highest(low)), LEAST)
    times = spread(TOP / scale, *high.shape)
    packed = jnp.round(high * times).astype(I32) * 65536 + jnp.round(low * times).astype(I32)
    return packed, scale * (1.0 / TOP)


def unsqueeze(packed, step):
    high = lax.shift_right_arithmetic(packed + 32768, jnp.full_like(packed, 16))
    low = packed - high * 65536
    step = spread(step, *packed.shape)
    return high.astype(F32) * step, low.astype(F32) * step


def thirds(value, axis):
    parts = []
    for _ in range(3):
        parts.append(value.astype(jnp.bfloat16))
        value = value - parts[-1].astype(F32)
    return jnp.concatenate(parts, axis=axis)


def kernel(
    n_doc,
    ta_hbm,
    tg_hbm,
    qa_hbm,
    qg_hbm,
    tseg_ref,
    qseg_ref,
    out_ref,
    ta,
    tg,
    qa,
    qg,
    gram,
    yout,
    yout_step,
    yin,
    yin_step,
    xout,
    xout_step,
    xin,
    xin_step,
    done,
    gout,
    gout_step,
    gin,
    gin_step,
    grads_up,
    segn,
    small,
    fin_y,
    fin_x,
    early_sum,
    local_sem,
    own_send,
    own_recv,
    qg_send,
    qg_recv,
    qa_send,
    qa_recv,
    hop_send,
    hop_recv,
    tg_send,
    tg_recv,
    ta_send,
    ta_recv,
    tgf_send,
    tgf_recv,
    taf_send,
    taf_recv,
    y_send,
    y_recv,
    x_send,
    x_recv,
    g_send,
    g_recv,
    s_send,
    s_recv,
    fy_send,
    fy_recv,
    fx_send,
    fx_recv,
):
    rows_t, wide_a = ta_hbm.shape
    rows_q, wide_g = qg_hbm.shape
    half = rows_q // NCORE
    chunk = half // CHUNKS
    part = rows_t // TPARTS
    ry = chunk // (NY * NX)
    factor = math.sqrt(ST * SQ / (rows_t * rows_q))

    doc = lax.axis_index("doc")
    place = lax.axis_index("hidden")
    core = lax.rem(place, NCORE)
    other = 1 - core
    my_x = lax.rem(place // NCORE, NX)
    my_y = place // (NCORE * NX)
    up = lax.rem(doc + 1, n_doc)
    down = lax.rem(doc + n_doc - 1, n_doc)

    def y_of(d):
        return lax.rem(my_y + d, NY)

    def spot(y, x, c):
        return y * (NX * NCORE) + x * NCORE + c

    sibling = (doc, spot(my_y, my_x, other))
    deep = n_doc // X_HI
    wrap = lax.rem(doc, deep) // (deep - 1)
    keep_far = my_x + wrap * (1 - 2 * my_x)

    def keep(kind, r):
        return keep_far if kind == GRAD and r >= 2 else my_x

    x_peer = (doc, spot(my_y, 1 - my_x, core))
    x_other = (doc, spot(my_y, 1 - my_x, other))

    def y_peer(d, of=doc):
        return (of, spot(y_of(d), my_x, core))

    def remote(src, dst, send, recv, who):
        return pltpu.make_async_remote_copy(
            src_ref=src, dst_ref=dst, send_sem=send, recv_sem=recv, device_id=who, device_id_type=MESH
        )

    def cols(wide, whose):
        return pl.ds(pl.multiple_of(whose * wide, LANES), wide)

    def q_half(whose):
        return pl.ds(pl.multiple_of(whose * half, half), half)

    def swap(j, whose_q, whose):
        return (
            (qg_hbm.at[q_half(whose_q), :], qg.at[0, :, cols(wide_g, whose)]),
            (tg_hbm, tg.at[0, :, cols(wide_g, whose)]),
            (qa_hbm.at[q_half(whose_q), :], qa.at[0, :, cols(wide_a, whose)]),
            (ta_hbm, ta.at[0, :, cols(wide_a, whose)]),
        )[j]

    def swap_out(j):
        return remote(*swap(j, other, core), own_send.at[j], own_recv.at[j], sibling)

    def swap_in(j):
        return remote(*swap(j, core, other), own_send.at[j], own_recv.at[j], sibling)

    def local(j):
        return pltpu.make_async_copy(*swap(j, core, core), local_sem.at[j])

    def who_up(far):
        return core if far == 0 else other

    def qg_up(far):
        to = who_up(far)
        return remote(
            qg_hbm.at[q_half(to), :],
            qg.at[1, :, cols(wide_g, core)],
            qg_send.at[far],
            qg_recv.at[far],
            (up, spot(my_y, my_x, to)),
        )

    def qg_arrival(far):
        return remote(
            qg_hbm.at[q_half(core), :],
            qg.at[1, :, cols(wide_g, who_up(far))],
            qg_send.at[far],
            qg_recv.at[far],
            (up, spot(my_y, my_x, who_up(far))),
        )

    def q_chunk(m):
        return pl.ds(m * chunk, chunk)

    def qa_up(m, far):
        to = who_up(far)
        return remote(
            qa_hbm.at[pl.ds(pl.multiple_of(to * half + m * chunk, chunk), chunk), :],
            qa.at[1, q_chunk(m), cols(wide_a, core)],
            qa_send.at[m, far],
            qa_recv.at[m, far],
            (up, spot(my_y, my_x, to)),
        )

    def qa_arrival(m, far):
        return remote(
            qa_hbm.at[pl.ds(pl.multiple_of(core * half + m * chunk, chunk), chunk), :],
            qa.at[1, q_chunk(m), cols(wide_a, who_up(far))],
            qa_send.at[m, far],
            qa_recv.at[m, far],
            (up, spot(my_y, my_x, who_up(far))),
        )

    def qa_hop(m, far):
        at = cols(wide_a, who_up(far))
        return remote(
            qa.at[1, q_chunk(m), at],
            qa.at[2, q_chunk(m), at],
            hop_send.at[m, far],
            hop_recv.at[m, far],
            (up, place),
        )

    def hop_arrival(m):
        for far in range(2):
            qa_hop(m, far).wait_recv()

    def tg_down(step):
        src = tg_hbm if step == 0 else tg.at[step, :, cols(wide_g, core)]
        return remote(
            src, tg.at[step + 1, :, cols(wide_g, core)], tg_send.at[step], tg_recv.at[step], (down, place)
        )

    def tg_across(step, whose):
        ref = tg.at[step + 1, :, cols(wide_g, whose)]
        return remote(ref, ref, tgf_send.at[step], tgf_recv.at[step], sibling)

    def t_part(p):
        return pl.ds(p * part, part)

    def ta_down(p):
        return remote(
            ta_hbm.at[t_part(p), :],
            ta.at[1, t_part(p), cols(wide_a, core)],
            ta_send.at[p],
            ta_recv.at[p],
            (down, place),
        )

    def ta_across(p, whose):
        ref = ta.at[1, t_part(p), cols(wide_a, whose)]
        return remote(ref, ref, taf_send.at[p], taf_recv.at[p], sibling)

    seg_copy = remote(tseg_ref, segn, s_send, s_recv, (down, place))

    def area(name):
        kind, r, m, n, p, k = UNITS[name]
        return kind, r, pl.ds(m * ry, n * ry), pl.ds(p * part, k * part)

    early = []

    def half_compute(name):
        _, r, m, n, _, _ = UNITS[name]
        at = cols(wide_a, core)
        early_sum[len(early)] = lax.dot_general(
            ta[1 if r == 3 else 0, :, at],
            qa[2, m * chunk : (m + n) * chunk, at],
            CONTRACT,
            preferred_element_type=F32,
        )
        early.append(name)

    def compute(name):
        kind, r, m, n, p, k = UNITS[name]
        if kind == ACT:
            query, train = qa.at[min(r, 2)], ta.at[1 if r == 3 else 0]
        else:
            query, train = qg.at[min(r, 1)], tg.at[max(r - 1, 0)]
        left = query[m * chunk : (m + n) * chunk, :]
        right = train[p * part : (p + k) * part, :]
        if name in early:
            at = cols(wide_a, other)
            late = lax.dot_general(
                ta[1 if r == 3 else 0, :, at],
                qa[2, m * chunk : (m + n) * chunk, at],
                CONTRACT,
                preferred_element_type=F32,
            )
            total = (early_sum[early.index(name)] + late).T
        elif n == CHUNKS:
            total = lax.dot_general(left, right, CONTRACT, preferred_element_type=F32)
        else:
            total = lax.dot_general(right, left, CONTRACT, preferred_element_type=F32).T
        for i in range(n):
            gram[kind, r, :, :, (m + i) * ry : (m + i + 1) * ry, p * part : (p + k) * part] = total[
                i * chunk : (i + 1) * chunk
            ].reshape(NY, NX, ry, k * part)

    def y_copy(name, d):
        kind, r, rows, lanes = area(name)
        u = ORDER.index(name)
        return (
            remote(
                yout.at[kind, r, y_of(d), rows, lanes],
                yin.at[kind, r, d - 1, rows, lanes],
                y_send.at[u, d - 1, 0],
                y_recv.at[u, d - 1, 0],
                y_peer(d),
            ),
            remote(
                yout_step.at[u, y_of(d)],
                yin_step.at[u, d - 1],
                y_send.at[u, d - 1, 1],
                y_recv.at[u, d - 1, 1],
                y_peer(d),
            ),
        )

    def x_copy(name):
        _, _, _, n, _, k = UNITS[name]
        u = ORDER.index(name)
        piece = (u, pl.ds(0, n * ry), pl.ds(0, k * part // 2))
        return (
            remote(xout.at[piece], xin.at[piece], x_send.at[u, 0], x_recv.at[u, 0], x_peer),
            remote(xout_step.at[u], xin_step.at[u], x_send.at[u, 1], x_recv.at[u, 1], x_peer),
        )

    def g_move():
        who = (up, spot(my_y, keep_far, core))
        return (
            remote(gout, gin, g_send.at[0], g_recv.at[0], who),
            remote(gout_step, gin_step, g_send.at[1], g_recv.at[1], who),
        )

    def unit(name):
        compute(name)
        kind, r, rows, lanes = area(name)
        for d in range(1, NY):
            y = y_of(d)
            packed, step = squeeze(gram[kind, r, y, 0, rows, lanes], gram[kind, r, y, 1, rows, lanes])
            yout[kind, r, y, rows, lanes] = packed
            yout_step[ORDER.index(name), y] = step
            for copy in y_copy(name, d):
                copy.start()

    def x_start(name):
        for copy in x_copy(name):
            copy.start()

    def y_finish(name):
        kind, r, m, n, p, k = UNITS[name]
        _, _, rows, lanes = area(name)
        u = ORDER.index(name)
        high, low = gram[kind, r, my_y, 0, rows, lanes], gram[kind, r, my_y, 1, rows, lanes]
        for d in range(1, NY):
            for copy in y_copy(name, d):
                copy.wait_recv()
            more = unsqueeze(yin[kind, r, d - 1, rows, lanes], yin_step[u, d - 1])
            high, low = high + more[0], low + more[1]
        gram[kind, r, my_y, 0, rows, lanes] = high
        gram[kind, r, my_y, 1, rows, lanes] = low
        go = gram[kind, r, my_y, 1 - keep(kind, r), rows, lanes]
        wide = k * part // 2
        packed, step = squeeze(go[:, :wide], go[:, wide:])
        xout[u, : n * ry, :wide] = packed
        xout_step[u] = step
        if name not in HELD:
            x_start(name)

    def x_finish(name):
        kind, r, m, n, p, k = UNITS[name]
        _, _, rows, _ = area(name)
        u = ORDER.index(name)
        for copy in x_copy(name):
            copy.wait_recv()
        wide = k * part // 2
        for i, more in enumerate(unsqueeze(xin[u, : n * ry, :wide], xin_step[u])):
            lanes = pl.ds(p * part + i * wide, wide)
            done[kind, r, rows, lanes] = gram[kind, r, my_y, keep(kind, r), rows, lanes] + more

    def onehots(r):
        seg_t = (segn if r == 3 else tseg_ref)[...]
        onehot_t = (lax.broadcasted_iota(jnp.int32, (ST, rows_t), 0) == seg_t).astype(jnp.bfloat16)
        owner = lax.rem(doc + n_doc - min(r, 2), n_doc)
        seg_q = qseg_ref[pl.ds(owner, 1), :]
        row = lax.broadcasted_iota(jnp.int32, (CHUNKS * ry, rows_q), 0)
        token = lax.broadcasted_iota(jnp.int32, (CHUNKS * ry, rows_q), 1)
        mine = core * half + (row // ry) * chunk + my_y * (NX * ry) + my_x * ry + row % ry
        ids = jnp.sum(jnp.where(token == mine, seg_q, 0), axis=1, keepdims=True)
        lane = lax.broadcasted_iota(jnp.int32, (CHUNKS * ry, LANES), 1)
        onehot_q = (lane == ids + r * SQ).astype(jnp.bfloat16)
        return onehot_t, jnp.concatenate([onehot_q] * 3, axis=0)

    def segment_sum(r, hots):
        onehot_t, onehot_q = hots
        grads = grads_up[r - 2] if r >= 2 else done[GRAD, r]
        parts = thirds(done[ACT, r] * grads, 0)
        left = lax.dot_general(onehot_t, parts, CONTRACT, preferred_element_type=F32)
        total = jnp.dot(thirds(left, 0), onehot_q, preferred_element_type=F32)
        return (total[:ST] + total[ST : 2 * ST]) + total[2 * ST :]

    def arrive_and_hop(m):
        for far in range(2):
            qa_arrival(m, far).wait_recv()
            qa_hop(m, far).start()

    for j in range(4):
        local(j).start()
    greet = [sibling, x_peer, x_other]
    greet += [(up, spot(my_y, my_x, other)), (down, spot(my_y, my_x, other))]
    greet += [(up, spot(my_y, 1 - my_x, core)), (down, spot(my_y, 1 - my_x, core))]
    greet += [y_peer(d) for d in range(1, NY)]
    greet += [y_peer(d, up) for d in range(NY)]
    greet += [y_peer(d, down) for d in range(NY)]
    barrier = pltpu.get_barrier_semaphore()
    for who in greet:
        pl.semaphore_signal(barrier, inc=1, device_id=who, device_id_type=MESH)
    pl.semaphore_wait(barrier, len(greet))

    for far in range(2):
        qg_up(far).start()
    tg_down(0).start()
    for j in range(4):
        swap_out(j).start()
    for far in range(2):
        qa_up(0, far).start()
    ta_down(0).start()
    for m in range(1, CHUNKS):
        for far in range(2):
            qa_up(m, far).start()
    seg_copy.start()

    for j in range(2):
        local(j).wait()
        swap_in(j).wait_recv()
    unit("g0")
    for j in range(2, 4):
        local(j).wait()
        swap_in(j).wait_recv()
    unit("a0")
    for far in range(2):
        qg_arrival(far).wait_recv()
    unit("g1")
    tg_down(0).wait_recv()
    tg_down(1).start()
    tg_across(0, core).start()
    for p in range(1, TPARTS):
        ta_down(p).start()
    tg_across(0, other).wait_recv()
    unit("g2")
    arrive_and_hop(0)
    y_finish("g0")
    y_finish("a0")
    arrive_and_hop(1)
    unit("a1_01")
    y_finish("g1")
    arrive_and_hop(2)
    ta_down(0).wait_recv()
    ta_across(0, core).start()
    y_finish("g2")
    arrive_and_hop(3)
    unit("a1_23")
    tg_down(1).wait_recv()
    tg_across(1, core).start()
    y_finish("a1_01")
    tg_across(1, other).wait_recv()
    unit("g3")
    hop_arrival(0)
    unit("a2_0")
    y_finish("a1_23")
    hop_arrival(1)
    unit("a2_1")
    y_finish("g3")
    y_finish("a2_0")
    ta_down(1).wait_recv()
    ta_across(1, core).start()
    for p in range(2):
        ta_across(p, other).wait_recv()
    unit("a3_01")
    y_finish("a2_1")
    seg_copy.wait_recv()
    hots_0, hots_1, hots_2, hots_3 = onehots(0), onehots(1), onehots(2), onehots(3)
    hop_arrival(2)
    unit("a2_2")
    unit("a3_2")
    y_finish("a3_01")
    y_finish("a2_2")
    y_finish("a3_2")
    ta_down(2).wait_recv()
    ta_across(2, core).start()
    ta_across(2, other).wait_recv()
    unit("a3_last")
    qa_hop(3, 0).wait_recv()
    for name in ("a3_3", "a2_3"):
        half_compute(name)
    qa_hop(3, 1).wait_recv()
    for name in HELD:
        x_start(name)
    unit("a3_3")
    unit("a2_3")
    for name in ("g2", "g3"):
        x_finish(name)
    gout[...], gout_step[...] = squeeze(done[GRAD, 2], done[GRAD, 3])
    for copy in g_move():
        copy.start()
    for name in ("a2_0", "a2_1", "a3_01", "a2_2", "a3_2"):
        x_finish(name)
    y_finish("a3_last")
    y_finish("a3_3")
    y_finish("a2_3")
    for name in HELD:
        x_finish(name)
    base = segment_sum(0, hots_0) + segment_sum(1, hots_1)
    for copy in g_move():
        copy.wait_recv()
    grads_up[0], grads_up[1] = unsqueeze(gin[...], gin_step[...])
    x_finish("a3_last")
    x_finish("a3_3")
    small[...] = segment_sum(3, hots_3)
    fu = [
        remote(small, fin_y.at[1, my_y], fy_send.at[1, d], fy_recv.at[1, my_y], y_peer(d, up))
        for d in range(NY)
    ]
    for copy in fu:
        copy.start()
    x_finish("a2_3")
    fin_y[0, my_y] = base + segment_sum(2, hots_2)
    fy = [
        remote(fin_y.at[0, my_y], fin_y.at[0, my_y], fy_send.at[0, d], fy_recv.at[0, my_y], y_peer(d))
        for d in range(1, NY)
    ]
    for copy in fy:
        copy.start()
    for d in range(1, NY):
        y = y_of(d)
        remote(fin_y.at[0, y], fin_y.at[0, y], fy_send.at[0, d], fy_recv.at[0, y], y_peer(d)).wait_recv()
    for d in range(NY):
        y = y_of(d)
        remote(small, fin_y.at[1, y], fy_send.at[1, d], fy_recv.at[1, y], y_peer(d, up)).wait_recv()
    total = fin_y[0, 0] + fin_y[1, 0]
    for y in range(1, NY):
        total = total + (fin_y[0, y] + fin_y[1, y])
    mine = lax.rem(place, NX * NCORE)
    fin_x[mine] = total
    fx = []
    for i, who in enumerate((sibling, x_peer, x_other)):
        fx.append(remote(fin_x.at[mine], fin_x.at[mine], fx_send.at[i], fx_recv.at[mine], who))
        fx[-1].start()
    for i, (x, c) in enumerate(((my_x, other), (1 - my_x, core), (1 - my_x, other))):
        at = x * NCORE + c
        remote(fin_x.at[at], fin_x.at[at], fx_send.at[i], fx_recv.at[at], sibling).wait_recv()
    out_ref[...] = ((fin_x[0] + fin_x[1]) + (fin_x[2] + fin_x[3])) * factor

    seg_copy.wait_send()
    for copy in fy + fu + fx:
        copy.wait_send()
    for j in range(4):
        swap_out(j).wait_send()
    for far in range(2):
        qg_up(far).wait_send()
    for m in range(CHUNKS):
        for far in range(2):
            qa_up(m, far).wait_send()
            qa_hop(m, far).wait_send()
    for step in range(2):
        tg_down(step).wait_send()
        tg_across(step, core).wait_send()
    for p in range(TPARTS):
        ta_down(p).wait_send()
        ta_across(p, core).wait_send()
    for copy in g_move():
        copy.wait_send()
    for name in ORDER:
        for d in range(1, NY):
            for copy in y_copy(name, d):
                copy.wait_send()
        for copy in x_copy(name):
            copy.wait_send()


def on_device(n_doc, train_acts, train_grads, query_acts, query_grads, train_seg, query_seg):
    rows_t, wide_a = train_acts.shape
    rows_q, wide_g = query_grads.shape
    half = rows_q // NCORE
    rows = half // (NY * NX)
    units = len(ORDER)
    dma = pltpu.SemaphoreType.DMA
    anywhere = pl.BlockSpec(memory_space=pl.ANY)
    vmem = pl.BlockSpec(memory_space=pltpu.VMEM)
    bf16 = jnp.bfloat16

    def pair(*shape):
        return [dma(shape), dma(shape)]

    sums = pl.pallas_call(
        functools.partial(kernel, n_doc),
        out_shape=jax.ShapeDtypeStruct((ST, LANES), F32),
        in_specs=[anywhere] * 4 + [vmem] * 2,
        out_specs=vmem,
        scratch_shapes=[
            pltpu.VMEM((2, rows_t, NCORE * wide_a), bf16),
            pltpu.VMEM((3, rows_t, NCORE * wide_g), bf16),
            pltpu.VMEM((3, half, NCORE * wide_a), bf16),
            pltpu.VMEM((2, half, NCORE * wide_g), bf16),
            pltpu.VMEM((2, CYCLE, NY, NX, rows, rows_t), F32),
            pltpu.VMEM((2, CYCLE, NY, rows, rows_t), I32),
            pltpu.VMEM((units, NY, 8, LANES), F32),
            pltpu.VMEM((2, CYCLE, NY - 1, rows, rows_t), I32),
            pltpu.VMEM((units, NY - 1, 8, LANES), F32),
            pltpu.VMEM((units, rows, rows_t // 2), I32),
            pltpu.VMEM((units, 8, LANES), F32),
            pltpu.VMEM((units, rows, rows_t // 2), I32),
            pltpu.VMEM((units, 8, LANES), F32),
            pltpu.VMEM((2, CYCLE, rows, rows_t), F32),
            pltpu.VMEM((rows, rows_t), I32),
            pltpu.VMEM((8, LANES), F32),
            pltpu.VMEM((rows, rows_t), I32),
            pltpu.VMEM((8, LANES), F32),
            pltpu.VMEM((2, rows, rows_t), F32),
            pltpu.VMEM((1, rows_t), I32),
            pltpu.VMEM((ST, LANES), F32),
            pltpu.VMEM((2, NY, ST, LANES), F32),
            pltpu.VMEM((NX * NCORE, ST, LANES), F32),
            pltpu.VMEM((2, rows_t, half // CHUNKS), F32),
            dma((4,)),
            *pair(4),
            *pair(2),
            *pair(CHUNKS, 2),
            *pair(CHUNKS, 2),
            *pair(2),
            *pair(TPARTS),
            *pair(2),
            *pair(TPARTS),
            *pair(units, NY - 1, 2),
            *pair(units, 2),
            *pair(2),
            dma,
            dma,
            *pair(2, NY),
            *pair(NX * NCORE),
        ],
        compiler_params=pltpu.CompilerParams(
            collective_id=0, has_side_effects=True, vmem_limit_bytes=56 * 1024 * 1024
        ),
        name="influence",
    )(train_acts, train_grads, query_acts, query_grads, train_seg, query_seg)
    return sums[:, : CYCLE * SQ]


def solution(mesh):
    in_specs = (
        P("doc", "hidden"),
        P("doc", "hidden"),
        P("doc", "hidden"),
        P("doc", "hidden"),
        P("doc", None),
        P(),
    )
    return jax.shard_map(
        functools.partial(on_device, mesh.shape["doc"]),
        mesh=mesh,
        in_specs=in_specs,
        out_specs=P("doc", None),
        check_vma=False,
    )
```

```python
import functools
import math

import jax
import jax.numpy as jnp
from jax import lax
from jax.experimental import pallas as pl
from jax.experimental.pallas import tpu as pltpu
from jax.sharding import PartitionSpec as P

ST = 8
SQ = 8
CYCLE = 4
NY = 4
NX = 2
NCORE = 2
X_HI = 2
CHUNKS = 4
TPARTS = 3
LANES = 128
ACT = 0
GRAD = 1
MESH = pl.DeviceIdType.MESH
CONTRACT = (((1,), (1,)), ((), ()))
F32 = jnp.float32
I32 = jnp.int32
TOP = 32767.0
LEAST = 1e-34

UNITS = {
    "g0": (GRAD, 0, 0, 4, 0, 3),
    "a0": (ACT, 0, 0, 4, 0, 3),
    "g1": (GRAD, 1, 0, 4, 0, 3),
    "g2": (GRAD, 2, 0, 4, 0, 3),
    "g3": (GRAD, 3, 0, 4, 0, 3),
    "a1_01": (ACT, 1, 0, 2, 0, 3),
    "a1_23": (ACT, 1, 2, 2, 0, 3),
    "a2_0": (ACT, 2, 0, 1, 0, 3),
    "a2_1": (ACT, 2, 1, 1, 0, 3),
    "a2_2": (ACT, 2, 2, 1, 0, 3),
    "a2_3": (ACT, 2, 3, 1, 0, 3),
    "a3_01": (ACT, 3, 0, 2, 0, 2),
    "a3_2": (ACT, 3, 2, 1, 0, 2),
    "a3_3": (ACT, 3, 3, 1, 0, 3),
    "a3_last": (ACT, 3, 0, 3, 2, 1),
}
ORDER = list(UNITS)
HELD = ("g0", "a0", "g1", "a1_01", "a1_23")


def spread(tile, rows, lanes):
    wide = jnp.concatenate([tile] * (lanes // LANES), axis=1) if lanes > LANES else tile
    return jnp.concatenate([wide] * (rows // 8), axis=0) if rows > 8 else wide


def highest(value):
    rows, lanes = value.shape
    top = jnp.max(jnp.abs(value).reshape(rows // 8, 8, lanes), axis=0)
    return functools.reduce(
        jnp.maximum, [top[:, b * LANES : (b + 1) * LANES] for b in range(lanes // LANES)]
    )


def squeeze(high, low):
    scale = jnp.maximum(jnp.maximum(highest(high), highest(low)), LEAST)
    times = spread(TOP / scale, *high.shape)
    packed = jnp.round(high * times).astype(I32) * 65536 + jnp.round(low * times).astype(I32)
    return packed, scale * (1.0 / TOP)


def unsqueeze(packed, step):
    high = lax.shift_right_arithmetic(packed + 32768, jnp.full_like(packed, 16))
    low = packed - high * 65536
    step = spread(step, *packed.shape)
    return high.astype(F32) * step, low.astype(F32) * step


def thirds(value, axis):
    parts = []
    for _ in range(3):
        parts.append(value.astype(jnp.bfloat16))
        value = value - parts[-1].astype(F32)
    return jnp.concatenate(parts, axis=axis)


def kernel(
    n_doc,
    ta_hbm,
    tg_hbm,
    qa_hbm,
    qg_hbm,
    tseg_ref,
    qseg_ref,
    out_ref,
    ta,
    tg,
    qa,
    qg,
    gram,
    yout,
    yout_step,
    yin,
    yin_step,
    xout,
    xout_step,
    xin,
    xin_step,
    done,
    gout,
    gout_step,
    gin,
    gin_step,
    grads_up,
    segn,
    small,
    fin_y,
    fin_x,
    early_sum,
    local_sem,
    own_send,
    own_recv,
    qg_send,
    qg_recv,
    qa_send,
    qa_recv,
    hop_send,
    hop_recv,
    tg_send,
    tg_recv,
    ta_send,
    ta_recv,
    tgf_send,
    tgf_recv,
    taf_send,
    taf_recv,
    y_send,
    y_recv,
    x_send,
    x_recv,
    g_send,
    g_recv,
    s_send,
    s_recv,
    fy_send,
    fy_recv,
    fx_send,
    fx_recv,
):
    rows_t, wide_a = ta_hbm.shape
    rows_q, wide_g = qg_hbm.shape
    half = rows_q // NCORE
    chunk = half // CHUNKS
    part = rows_t // TPARTS
    ry = chunk // (NY * NX)
    factor = math.sqrt(ST * SQ / (rows_t * rows_q))

    doc = lax.axis_index("doc")
    place = lax.axis_index("hidden")
    core = lax.rem(place, NCORE)
    other = 1 - core
    my_x = lax.rem(place // NCORE, NX)
    my_y = place // (NCORE * NX)
    up = lax.rem(doc + 1, n_doc)
    down = lax.rem(doc + n_doc - 1, n_doc)

    def y_of(d):
        return lax.rem(my_y + d, NY)

    def spot(y, x, c):
        return y * (NX * NCORE) + x * NCORE + c

    sibling = (doc, spot(my_y, my_x, other))
    deep = n_doc // X_HI
    wrap = lax.rem(doc, deep) // (deep - 1)
    keep_far = my_x + wrap * (1 - 2 * my_x)

    def keep(kind, r):
        return keep_far if kind == GRAD and r >= 2 else my_x

    x_peer = (doc, spot(my_y, 1 - my_x, core))
    x_other = (doc, spot(my_y, 1 - my_x, other))

    def y_peer(d, of=doc):
        return (of, spot(y_of(d), my_x, core))

    def remote(src, dst, send, recv, who):
        return pltpu.make_async_remote_copy(
            src_ref=src, dst_ref=dst, send_sem=send, recv_sem=recv, device_id=who, device_id_type=MESH
        )

    def cols(wide, whose):
        return pl.ds(pl.multiple_of(whose * wide, LANES), wide)

    def q_half(whose):
        return pl.ds(pl.multiple_of(whose * half, half), half)

    def swap(j, whose_q, whose):
        return (
            (qg_hbm.at[q_half(whose_q), :], qg.at[0, :, cols(wide_g, whose)]),
            (tg_hbm, tg.at[0, :, cols(wide_g, whose)]),
            (qa_hbm.at[q_half(whose_q), :], qa.at[0, :, cols(wide_a, whose)]),
            (ta_hbm, ta.at[0, :, cols(wide_a, whose)]),
        )[j]

    def swap_out(j):
        return remote(*swap(j, other, core), own_send.at[j], own_recv.at[j], sibling)

    def swap_in(j):
        return remote(*swap(j, core, other), own_send.at[j], own_recv.at[j], sibling)

    def local(j):
        return pltpu.make_async_copy(*swap(j, core, core), local_sem.at[j])

    def who_up(far):
        return core if far == 0 else other

    def qg_up(far):
        to = who_up(far)
        return remote(
            qg_hbm.at[q_half(to), :],
            qg.at[1, :, cols(wide_g, core)],
            qg_send.at[far],
            qg_recv.at[far],
            (up, spot(my_y, my_x, to)),
        )

    def qg_arrival(far):
        return remote(
            qg_hbm.at[q_half(core), :],
            qg.at[1, :, cols(wide_g, who_up(far))],
            qg_send.at[far],
            qg_recv.at[far],
            (up, spot(my_y, my_x, who_up(far))),
        )

    def q_chunk(m):
        return pl.ds(m * chunk, chunk)

    def qa_up(m, far):
        to = who_up(far)
        return remote(
            qa_hbm.at[pl.ds(pl.multiple_of(to * half + m * chunk, chunk), chunk), :],
            qa.at[1, q_chunk(m), cols(wide_a, core)],
            qa_send.at[m, far],
            qa_recv.at[m, far],
            (up, spot(my_y, my_x, to)),
        )

    def qa_arrival(m, far):
        return remote(
            qa_hbm.at[pl.ds(pl.multiple_of(core * half + m * chunk, chunk), chunk), :],
            qa.at[1, q_chunk(m), cols(wide_a, who_up(far))],
            qa_send.at[m, far],
            qa_recv.at[m, far],
            (up, spot(my_y, my_x, who_up(far))),
        )

    def qa_hop(m, far):
        at = cols(wide_a, who_up(far))
        return remote(
            qa.at[1, q_chunk(m), at],
            qa.at[2, q_chunk(m), at],
            hop_send.at[m, far],
            hop_recv.at[m, far],
            (up, place),
        )

    def hop_arrival(m):
        for far in range(2):
            qa_hop(m, far).wait_recv()

    def tg_down(step):
        src = tg_hbm if step == 0 else tg.at[step, :, cols(wide_g, core)]
        return remote(
            src, tg.at[step + 1, :, cols(wide_g, core)], tg_send.at[step], tg_recv.at[step], (down, place)
        )

    def tg_across(step, whose):
        ref = tg.at[step + 1, :, cols(wide_g, whose)]
        return remote(ref, ref, tgf_send.at[step], tgf_recv.at[step], sibling)

    def t_part(p):
        return pl.ds(p * part, part)

    def ta_down(p):
        return remote(
            ta_hbm.at[t_part(p), :],
            ta.at[1, t_part(p), cols(wide_a, core)],
            ta_send.at[p],
            ta_recv.at[p],
            (down, place),
        )

    def ta_across(p, whose):
        ref = ta.at[1, t_part(p), cols(wide_a, whose)]
        return remote(ref, ref, taf_send.at[p], taf_recv.at[p], sibling)

    seg_copy = remote(tseg_ref, segn, s_send, s_recv, (down, place))

    def area(name):
        kind, r, m, n, p, k = UNITS[name]
        return kind, r, pl.ds(m * ry, n * ry), pl.ds(p * part, k * part)

    early = []

    def half_compute(name):
        _, r, m, n, _, _ = UNITS[name]
        at = cols(wide_a, core)
        early_sum[len(early)] = lax.dot_general(
            ta[1 if r == 3 else 0, :, at],
            qa[2, m * chunk : (m + n) * chunk, at],
            CONTRACT,
            preferred_element_type=F32,
        )
        early.append(name)

    def compute(name):
        kind, r, m, n, p, k = UNITS[name]
        if kind == ACT:
            query, train = qa.at[min(r, 2)], ta.at[1 if r == 3 else 0]
        else:
            query, train = qg.at[min(r, 1)], tg.at[max(r - 1, 0)]
        left = query[m * chunk : (m + n) * chunk, :]
        right = train[p * part : (p + k) * part, :]
        if name in early:
            at = cols(wide_a, other)
            late = lax.dot_general(
                ta[1 if r == 3 else 0, :, at],
                qa[2, m * chunk : (m + n) * chunk, at],
                CONTRACT,
                preferred_element_type=F32,
            )
            total = (early_sum[early.index(name)] + late).T
        elif n == CHUNKS:
            total = lax.dot_general(left, right, CONTRACT, preferred_element_type=F32)
        else:
            total = lax.dot_general(right, left, CONTRACT, preferred_element_type=F32).T
        for i in range(n):
            gram[kind, r, :, :, (m + i) * ry : (m + i + 1) * ry, p * part : (p + k) * part] = total[
                i * chunk : (i + 1) * chunk
            ].reshape(NY, NX, ry, k * part)

    def y_copy(name, d):
        kind, r, rows, lanes = area(name)
        u = ORDER.index(name)
        return (
            remote(
                yout.at[kind, r, y_of(d), rows, lanes],
                yin.at[kind, r, d - 1, rows, lanes],
                y_send.at[u, d - 1, 0],
                y_recv.at[u, d - 1, 0],
                y_peer(d),
            ),
            remote(
                yout_step.at[u, y_of(d)],
                yin_step.at[u, d - 1],
                y_send.at[u, d - 1, 1],
                y_recv.at[u, d - 1, 1],
                y_peer(d),
            ),
        )

    def x_copy(name):
        _, _, _, n, _, k = UNITS[name]
        u = ORDER.index(name)
        piece = (u, pl.ds(0, n * ry), pl.ds(0, k * part // 2))
        return (
            remote(xout.at[piece], xin.at[piece], x_send.at[u, 0], x_recv.at[u, 0], x_peer),
            remote(xout_step.at[u], xin_step.at[u], x_send.at[u, 1], x_recv.at[u, 1], x_peer),
        )

    def g_move():
        who = (up, spot(my_y, keep_far, core))
        return (
            remote(gout, gin, g_send.at[0], g_recv.at[0], who),
            remote(gout_step, gin_step, g_send.at[1], g_recv.at[1], who),
        )

    def unit(name):
        compute(name)
        kind, r, rows, lanes = area(name)
        for d in range(1, NY):
            y = y_of(d)
            packed, step = squeeze(gram[kind, r, y, 0, rows, lanes], gram[kind, r, y, 1, rows, lanes])
            yout[kind, r, y, rows, lanes] = packed
            yout_step[ORDER.index(name), y] = step
            for copy in y_copy(name, d):
                copy.start()

    def x_start(name):
        for copy in x_copy(name):
            copy.start()

    def y_finish(name):
        kind, r, m, n, p, k = UNITS[name]
        _, _, rows, lanes = area(name)
        u = ORDER.index(name)
        high, low = gram[kind, r, my_y, 0, rows, lanes], gram[kind, r, my_y, 1, rows, lanes]
        for d in range(1, NY):
            for copy in y_copy(name, d):
                copy.wait_recv()
            more = unsqueeze(yin[kind, r, d - 1, rows, lanes], yin_step[u, d - 1])
            high, low = high + more[0], low + more[1]
        gram[kind, r, my_y, 0, rows, lanes] = high
        gram[kind, r, my_y, 1, rows, lanes] = low
        go = gram[kind, r, my_y, 1 - keep(kind, r), rows, lanes]
        wide = k * part // 2
        packed, step = squeeze(go[:, :wide], go[:, wide:])
        xout[u, : n * ry, :wide] = packed
        xout_step[u] = step
        if name not in HELD:
            x_start(name)

    def x_finish(name):
        kind, r, m, n, p, k = UNITS[name]
        _, _, rows, _ = area(name)
        u = ORDER.index(name)
        for copy in x_copy(name):
            copy.wait_recv()
        wide = k * part // 2
        for i, more in enumerate(unsqueeze(xin[u, : n * ry, :wide], xin_step[u])):
            lanes = pl.ds(p * part + i * wide, wide)
            done[kind, r, rows, lanes] = gram[kind, r, my_y, keep(kind, r), rows, lanes] + more

    def onehots(r):
        seg_t = (segn if r == 3 else tseg_ref)[...]
        onehot_t = (lax.broadcasted_iota(jnp.int32, (ST, rows_t), 0) == seg_t).astype(jnp.bfloat16)
        owner = lax.rem(doc + n_doc - min(r, 2), n_doc)
        seg_q = qseg_ref[pl.ds(owner, 1), :]
        row = lax.broadcasted_iota(jnp.int32, (CHUNKS * ry, rows_q), 0)
        token = lax.broadcasted_iota(jnp.int32, (CHUNKS * ry, rows_q), 1)
        mine = core * half + (row // ry) * chunk + my_y * (NX * ry) + my_x * ry + row % ry
        ids = jnp.sum(jnp.where(token == mine, seg_q, 0), axis=1, keepdims=True)
        lane = lax.broadcasted_iota(jnp.int32, (CHUNKS * ry, LANES), 1)
        onehot_q = (lane == ids + r * SQ).astype(jnp.bfloat16)
        return onehot_t, jnp.concatenate([onehot_q] * 3, axis=0)

    def segment_sum(r, hots):
        onehot_t, onehot_q = hots
        grads = grads_up[r - 2] if r >= 2 else done[GRAD, r]
        parts = thirds(done[ACT, r] * grads, 0)
        left = lax.dot_general(onehot_t, parts, CONTRACT, preferred_element_type=F32)
        total = jnp.dot(thirds(left, 0), onehot_q, preferred_element_type=F32)
        return (total[:ST] + total[ST : 2 * ST]) + total[2 * ST :]

    def arrive_and_hop(m):
        for far in range(2):
            qa_arrival(m, far).wait_recv()
            qa_hop(m, far).start()

    for j in range(4):
        local(j).start()
    greet = [y_peer(d, up) for d in range(NY)]
    greet += [y_peer(d, down) for d in range(NY)]
    greet += [(up, spot(my_y, my_x, other)), (down, spot(my_y, my_x, other))]
    greet += [(up, spot(my_y, 1 - my_x, core)), (down, spot(my_y, 1 - my_x, core))]
    greet += [y_peer(d) for d in range(1, NY)]
    greet += [x_peer, x_other, sibling]
    barrier = pltpu.get_barrier_semaphore()
    for who in greet:
        pl.semaphore_signal(barrier, inc=1, device_id=who, device_id_type=MESH)
    pl.semaphore_wait(barrier, len(greet))

    for far in range(2):
        qg_up(far).start()
    tg_down(0).start()
    for j in range(4):
        swap_out(j).start()
    for far in range(2):
        qa_up(0, far).start()
    ta_down(0).start()
    for m in range(1, CHUNKS):
        for far in range(2):
            qa_up(m, far).start()
    seg_copy.start()

    for j in range(2):
        local(j).wait()
        swap_in(j).wait_recv()
    unit("g0")
    for j in range(2, 4):
        local(j).wait()
        swap_in(j).wait_recv()
    unit("a0")
    for far in range(2):
        qg_arrival(far).wait_recv()
    unit("g1")
    tg_down(0).wait_recv()
    tg_down(1).start()
    tg_across(0, core).start()
    for p in range(1, TPARTS):
        ta_down(p).start()
    tg_across(0, other).wait_recv()
    unit("g2")
    arrive_and_hop(0)
    y_finish("g0")
    y_finish("a0")
    arrive_and_hop(1)
    unit("a1_01")
    y_finish("g1")
    arrive_and_hop(2)
    ta_down(0).wait_recv()
    ta_across(0, core).start()
    y_finish("g2")
    arrive_and_hop(3)
    unit("a1_23")
    tg_down(1).wait_recv()
    tg_across(1, core).start()
    y_finish("a1_01")
    tg_across(1, other).wait_recv()
    unit("g3")
    hop_arrival(0)
    unit("a2_0")
    y_finish("a1_23")
    hop_arrival(1)
    unit("a2_1")
    y_finish("g3")
    y_finish("a2_0")
    ta_down(1).wait_recv()
    ta_across(1, core).start()
    for p in range(2):
        ta_across(p, other).wait_recv()
    unit("a3_01")
    y_finish("a2_1")
    seg_copy.wait_recv()
    hots_0, hots_1, hots_2, hots_3 = onehots(0), onehots(1), onehots(2), onehots(3)
    hop_arrival(2)
    unit("a2_2")
    unit("a3_2")
    y_finish("a3_01")
    y_finish("a2_2")
    y_finish("a3_2")
    ta_down(2).wait_recv()
    ta_across(2, core).start()
    ta_across(2, other).wait_recv()
    unit("a3_last")
    qa_hop(3, 0).wait_recv()
    for name in ("a3_3", "a2_3"):
        half_compute(name)
    qa_hop(3, 1).wait_recv()
    for name in HELD:
        x_start(name)
    unit("a3_3")
    unit("a2_3")
    for name in ("g2", "g3"):
        x_finish(name)
    gout[...], gout_step[...] = squeeze(done[GRAD, 2], done[GRAD, 3])
    for copy in g_move():
        copy.start()
    for name in ("a2_0", "a2_1", "a3_01", "a2_2", "a3_2"):
        x_finish(name)
    y_finish("a3_last")
    y_finish("a3_3")
    y_finish("a2_3")
    for name in HELD:
        x_finish(name)
    base = segment_sum(0, hots_0) + segment_sum(1, hots_1)
    for copy in g_move():
        copy.wait_recv()
    grads_up[0], grads_up[1] = unsqueeze(gin[...], gin_step[...])
    x_finish("a3_last")
    x_finish("a3_3")
    small[...] = segment_sum(3, hots_3)
    fu = [
        remote(small, fin_y.at[1, my_y], fy_send.at[1, d], fy_recv.at[1, my_y], y_peer(d, up))
        for d in range(NY)
    ]
    for copy in fu:
        copy.start()
    x_finish("a2_3")
    fin_y[0, my_y] = base + segment_sum(2, hots_2)
    fy = [
        remote(fin_y.at[0, my_y], fin_y.at[0, my_y], fy_send.at[0, d], fy_recv.at[0, my_y], y_peer(d))
        for d in range(1, NY)
    ]
    for copy in fy:
        copy.start()
    for d in range(1, NY):
        y = y_of(d)
        remote(fin_y.at[0, y], fin_y.at[0, y], fy_send.at[0, d], fy_recv.at[0, y], y_peer(d)).wait_recv()
    for d in range(NY):
        y = y_of(d)
        remote(small, fin_y.at[1, y], fy_send.at[1, d], fy_recv.at[1, y], y_peer(d, up)).wait_recv()
    total = fin_y[0, 0] + fin_y[1, 0]
    for y in range(1, NY):
        total = total + (fin_y[0, y] + fin_y[1, y])
    mine = lax.rem(place, NX * NCORE)
    fin_x[mine] = total
    fx = []
    for i, who in enumerate((sibling, x_peer, x_other)):
        fx.append(remote(fin_x.at[mine], fin_x.at[mine], fx_send.at[i], fx_recv.at[mine], who))
        fx[-1].start()
    for i, (x, c) in enumerate(((my_x, other), (1 - my_x, core), (1 - my_x, other))):
        at = x * NCORE + c
        remote(fin_x.at[at], fin_x.at[at], fx_send.at[i], fx_recv.at[at], sibling).wait_recv()
    out_ref[...] = (((fin_x[0] + fin_x[1]) + (fin_x[2] + fin_x[3])) * factor)[:, : CYCLE * SQ]

    seg_copy.wait_send()
    for copy in fy + fu + fx:
        copy.wait_send()
    for j in range(4):
        swap_out(j).wait_send()
    for far in range(2):
        qg_up(far).wait_send()
    for m in range(CHUNKS):
        for far in range(2):
            qa_up(m, far).wait_send()
            qa_hop(m, far).wait_send()
    for step in range(2):
        tg_down(step).wait_send()
        tg_across(step, core).wait_send()
    for p in range(TPARTS):
        ta_down(p).wait_send()
        ta_across(p, core).wait_send()
    for copy in g_move():
        copy.wait_send()
    for name in ORDER:
        for d in range(1, NY):
            for copy in y_copy(name, d):
                copy.wait_send()
        for copy in x_copy(name):
            copy.wait_send()


def on_device(n_doc, train_acts, train_grads, query_acts, query_grads, train_seg, query_seg):
    rows_t, wide_a = train_acts.shape
    rows_q, wide_g = query_grads.shape
    half = rows_q // NCORE
    rows = half // (NY * NX)
    units = len(ORDER)
    dma = pltpu.SemaphoreType.DMA
    anywhere = pl.BlockSpec(memory_space=pl.ANY)
    vmem = pl.BlockSpec(memory_space=pltpu.VMEM)
    bf16 = jnp.bfloat16

    def pair(*shape):
        return [dma(shape), dma(shape)]

    return pl.pallas_call(
        functools.partial(kernel, n_doc),
        out_shape=jax.ShapeDtypeStruct((ST, CYCLE * SQ), F32),
        in_specs=[anywhere] * 4 + [vmem] * 2,
        out_specs=vmem,
        scratch_shapes=[
            pltpu.VMEM((2, rows_t, NCORE * wide_a), bf16),
            pltpu.VMEM((3, rows_t, NCORE * wide_g), bf16),
            pltpu.VMEM((3, half, NCORE * wide_a), bf16),
            pltpu.VMEM((2, half, NCORE * wide_g), bf16),
            pltpu.VMEM((2, CYCLE, NY, NX, rows, rows_t), F32),
            pltpu.VMEM((2, CYCLE, NY, rows, rows_t), I32),
            pltpu.VMEM((units, NY, 8, LANES), F32),
            pltpu.VMEM((2, CYCLE, NY - 1, rows, rows_t), I32),
            pltpu.VMEM((units, NY - 1, 8, LANES), F32),
            pltpu.VMEM((units, rows, rows_t // 2), I32),
            pltpu.VMEM((units, 8, LANES), F32),
            pltpu.VMEM((units, rows, rows_t // 2), I32),
            pltpu.VMEM((units, 8, LANES), F32),
            pltpu.VMEM((2, CYCLE, rows, rows_t), F32),
            pltpu.VMEM((rows, rows_t), I32),
            pltpu.VMEM((8, LANES), F32),
            pltpu.VMEM((rows, rows_t), I32),
            pltpu.VMEM((8, LANES), F32),
            pltpu.VMEM((2, rows, rows_t), F32),
            pltpu.VMEM((1, rows_t), I32),
            pltpu.VMEM((ST, LANES), F32),
            pltpu.VMEM((2, NY, ST, LANES), F32),
            pltpu.VMEM((NX * NCORE, ST, LANES), F32),
            pltpu.VMEM((2, rows_t, half // CHUNKS), F32),
            dma((4,)),
            *pair(4),
            *pair(2),
            *pair(CHUNKS, 2),
            *pair(CHUNKS, 2),
            *pair(2),
            *pair(TPARTS),
            *pair(2),
            *pair(TPARTS),
            *pair(units, NY - 1, 2),
            *pair(units, 2),
            *pair(2),
            dma,
            dma,
            *pair(2, NY),
            *pair(NX * NCORE),
        ],
        compiler_params=pltpu.CompilerParams(
            collective_id=0, has_side_effects=True, vmem_limit_bytes=56 * 1024 * 1024
        ),
        name="influence",
    )(train_acts, train_grads, query_acts, query_grads, train_seg, query_seg)


def solution(mesh):
    in_specs = (
        P("doc", "hidden"),
        P("doc", "hidden"),
        P("doc", "hidden"),
        P("doc", "hidden"),
        P("doc", None),
        P(),
    )
    return jax.shard_map(
        functools.partial(on_device, mesh.shape["doc"]),
        mesh=mesh,
        in_specs=in_specs,
        out_specs=P("doc", None),
        check_vma=False,
    )
```
